128 devices in a mesh: graph: 32 (over z, y, core), feat: 4 (over x).
Axes of the slice: x: 4, y: 4, z: 4, core: 2. Of those that a mesh axis runs over, the one named last changes fastest.
Arguments:
- grid_feat: bfloat16 [131072, 512], P('graph'), may hold values from -6 to 6
- mesh_feat: bfloat16 [65536, 512], P('graph'), may hold values from -6 to 6
- send_rows: int32 [32, 32, 256], P('graph'), may hold values from 0 to 4095
- tile_src: int32 [128, 8], P('graph'), may hold values from 0 to 95
- edge_mask: int32 [65536, 1024], P('graph'), may hold values from 0 to 1, as said below
- gain_src: float32 [512], replicated, may hold values from 0.1 to 1.9
- gain_dst: float32 [512], replicated, may hold values from 0.1 to 1.9
- w_query: bfloat16 [512, 512], P(None, 'feat')
- w_key: bfloat16 [512, 512], P(None, 'feat'), may hold values from -0.25 to 0.25
- w_value: bfloat16 [512, 512], P(None, 'feat'), may hold values from -0.25 to 0.25
- w_out: bfloat16 [512, 512], P('feat'), may hold values from -0.25 to 0.25
- d_out: bfloat16 [65536, 512], P('graph', 'feat'), may hold values from -6 to 6
Outputs:
- mesh_out: bfloat16 [65536, 512], P('graph', 'feat')
- grad_grid: bfloat16 [131072, 512], P('graph', 'feat')
- grad_mesh: bfloat16 [65536, 512], P('graph', 'feat')
- grad_wq: float32 [512, 512], P(None, 'feat')
- grad_wk: float32 [512, 512], P(None, 'feat')
- grad_wv: float32 [512, 512], P(None, 'feat')
- grad_wo: float32 [512, 512], P('feat')
The draws below stay inside these ranges and needn't reach their ends.
Inputs may be any that keep to these rules, and one draw needn't show every extreme that they name: `edge_mask`: slot 0 of every mesh row is valid.
All inputs are finite; a program needn't handle non-finite values.
Results may differ from the reference program's by a relative error of at most 0.03.
The reference program's roundings to bfloat16 on the way count: a program that leaves them out, or rounds other values in their place, can miss the bound.
Values may be sent and summed in bfloat16 or wider, within the bound.
No kernel may reach another device: no remote copies, remote signals or barrier semaphores. Data moves between devices by JAX's collectives and lax.ppermute only.
A program may use at most 192 MiB of HBM per device.

```python
import jax
import jax.numpy as jnp
from jax import lax

D = 512
HEADS = 8
G_DEV = 4096
M_DEV = 2048
B = 256
TS = 128
TM = 512
KT = 8
GRID = 131072
MESH = 65536
N_GRAPH = 32


def draw_edge_mask(key, part):
    key = jax.random.fold_in(key, 7)
    random_bits = jax.random.randint(key, (MESH, KT * TS), 0, 2)
    column = jnp.arange(KT * TS)[None, :]
    return jnp.where(column == 0, 1, random_bits).astype(jnp.int32)


def draw_w_query(key, part):
    key = jax.random.fold_in(key, 11)
    matrix = jax.random.normal(key, (D, D), jnp.float32) * D ** (-0.5)
    return matrix.astype(jnp.bfloat16)


def plant(result, key, low, largest):
    shape = result.shape
    place = [jax.random.randint(jax.random.fold_in(key, axis), (), 0, shape[axis]) for axis in range(len(shape))]
    result = result.at[tuple(place)].set(low)
    longest = shape.index(max(shape))
    place[longest] = (place[longest] + 1) % shape[longest]
    return result.at[tuple(place)].set(largest)


def steps_of(key, shape, cuts, least, top_value):
    factor_of = 1.0
    for position, blocks in cuts:
        steps = jax.random.uniform(jax.random.fold_in(jax.random.fold_in(key, 6), position), (blocks,), jnp.float32, least / len(cuts), top_value / len(cuts))
        factor_of = factor_of * jnp.repeat(jnp.exp(steps), shape[position] // blocks).reshape((-1,) + (1,) * (len(shape) - 1 - position))
    return factor_of


def centred(stream_key, dims, scale, limit, shards=(), kind=jnp.bfloat16):
    level = steps_of(stream_key, dims, shards, -0.22, 0.18) if shards else 1.0
    entries = jax.random.normal(stream_key, dims, jnp.float32) * scale * level
    return jnp.minimum(jnp.maximum(entries, -limit), limit).astype(kind)


def setup_inputs(seed: int = 0) -> dict:
    arg_keys = jax.random.split(jax.random.key(seed), 13)
    grid_feat = centred(arg_keys[0], (GRID, D), 1.0, 6.0, ((0, 32),))
    mesh_feat = centred(arg_keys[1], (MESH, D), 1.0, 6.0, ((0, 32),))
    send_rows = plant(jax.random.randint(arg_keys[2], (N_GRAPH, N_GRAPH, B), 0, G_DEV), jax.random.fold_in(arg_keys[2], 1), 0, G_DEV - 1).astype(jnp.int32)
    tile_src = plant(jax.random.randint(arg_keys[3], (MESH // TM, KT), 0, (G_DEV + N_GRAPH * B) // TS), jax.random.fold_in(arg_keys[3], 1), 0, ((G_DEV + N_GRAPH * B) // TS) - 1).astype(jnp.int32)
    edge_mask = draw_edge_mask(jax.random.fold_in(arg_keys[12], 71), 0)
    gain_src = jnp.clip(1.0 + 0.18 * jax.random.normal(arg_keys[5], (D,), jnp.float32), 0.1, 1.9)
    gain_dst = jnp.clip(1.0 + 0.18 * jax.random.normal(arg_keys[6], (D,), jnp.float32), 0.1, 1.9)
    w_query = draw_w_query(jax.random.fold_in(arg_keys[12], 71), 0)
    w_key = centred(arg_keys[8], (D, D), D ** -0.5, 0.25, ((1, 4),))
    w_value = centred(arg_keys[9], (D, D), D ** -0.5, 0.25, ((1, 4),))
    w_out = centred(arg_keys[10], (D, D), D ** -0.5, 0.25, ((0, 4),))
    d_out = centred(arg_keys[11], (MESH, D), 1.0, 6.0, ((0, 32), (1, 4)))
    return dict(grid_feat=grid_feat, mesh_feat=mesh_feat, send_rows=send_rows, tile_src=tile_src, edge_mask=edge_mask, gain_src=gain_src, gain_dst=gain_dst, w_query=w_query, w_key=w_key, w_value=w_value, w_out=w_out, d_out=d_out)


def normalize(values_in):
    centre = values_in - lax.optimization_barrier(jnp.mean(values_in, axis=-1, keepdims=True))
    variance = lax.optimization_barrier(jnp.mean(centre * centre, axis=-1, keepdims=True))
    inverse = lax.rsqrt(variance + 1e-05)
    return (centre * inverse, inverse)

def norm_back(grad_hat, normed, inverse):
    first = lax.optimization_barrier(jnp.mean(grad_hat, axis=-1, keepdims=True))
    second = lax.optimization_barrier(jnp.mean(grad_hat * normed, axis=-1, keepdims=True))
    return (grad_hat - first - normed * second) * inverse

def block_terms(queries, key_block, value_block, validity, grad_block):
    row_count = queries.shape[0]
    slot_count = key_block.shape[0]
    q_heads = queries.astype(jnp.float32).reshape(row_count, HEADS, -1)
    k_heads = key_block.astype(jnp.float32).reshape(slot_count, HEADS, -1)
    v_heads = value_block.astype(jnp.float32).reshape(slot_count, HEADS, -1)
    g_heads = grad_block.astype(jnp.float32).reshape(row_count, HEADS, -1)
    scores = jnp.einsum('thd,ehd->hte', q_heads, k_heads)
    allowed = (validity > 0)[None, :, :]
    scores = jnp.where(allowed, scores, -1e+30)
    highest = lax.optimization_barrier(jnp.max(scores, axis=-1, keepdims=True))
    raised = jnp.where(allowed, jnp.exp(scores - highest), 0.0)
    attention = raised / lax.optimization_barrier(jnp.sum(raised, axis=-1, keepdims=True))
    weights = lax.optimization_barrier(attention.astype(jnp.bfloat16)).astype(jnp.float32)
    attended = jnp.einsum('hte,ehd->thd', weights, v_heads).reshape(row_count, -1).astype(jnp.bfloat16)
    d_weights = jnp.einsum('thd,ehd->hte', g_heads, v_heads)
    d_values = jnp.einsum('hte,thd->ehd', weights, g_heads).reshape(slot_count, -1)
    d_scores = attention * (d_weights - lax.optimization_barrier(jnp.sum(attention * d_weights, axis=-1, keepdims=True)))
    scores_b = lax.optimization_barrier(d_scores.astype(jnp.bfloat16)).astype(jnp.float32)
    d_query = jnp.einsum('hte,ehd->thd', scores_b, k_heads).reshape(row_count, -1)
    d_keys = jnp.einsum('hte,thd->ehd', scores_b, q_heads).reshape(slot_count, -1)
    return (attended, d_query, d_keys, d_values)

def reference(grid_feat, mesh_feat, send_rows, tile_src, edge_mask, gain_src, gain_dst, w_query, w_key, w_value, w_out, d_out):
    src_hat, src_inverse = normalize(grid_feat.astype(jnp.float32))
    src_normed = (src_hat * gain_src.astype(jnp.float32)).astype(jnp.bfloat16)
    dst_hat, dst_inverse = normalize(mesh_feat.astype(jnp.float32))
    dst_normed = (dst_hat * gain_dst.astype(jnp.float32)).astype(jnp.bfloat16)
    query_all = (jnp.dot(dst_normed, w_query, preferred_element_type=jnp.float32) * 0.125).astype(jnp.bfloat16)
    key_all = jnp.dot(src_normed, w_key, preferred_element_type=jnp.float32).astype(jnp.bfloat16)
    value_all = jnp.dot(src_normed, w_value, preferred_element_type=jnp.float32).astype(jnp.bfloat16)
    d_attn = jnp.dot(d_out, w_out.T, preferred_element_type=jnp.float32).astype(jnp.bfloat16)
    blocks_dev = M_DEV // TM
    peer_ids = jnp.arange(N_GRAPH, dtype=jnp.int32)

    def partition(carry, partition_id):
        key_sum, value_sum = carry
        halo_index = (peer_ids[:, None] * G_DEV + send_rows[:, partition_id, :]).reshape(-1).astype(jnp.int32)
        own_keys = lax.dynamic_slice_in_dim(key_all, partition_id * G_DEV, G_DEV, 0)
        own_values = lax.dynamic_slice_in_dim(value_all, partition_id * G_DEV, G_DEV, 0)
        key_table = jnp.concatenate([own_keys, key_all[halo_index]], axis=0).reshape(-1, TS, D)
        value_table = jnp.concatenate([own_values, value_all[halo_index]], axis=0).reshape(-1, TS, D)
        query_rows = lax.dynamic_slice_in_dim(query_all, partition_id * M_DEV, M_DEV, 0).reshape(blocks_dev, TM, D)
        grad_rows = lax.dynamic_slice_in_dim(d_attn, partition_id * M_DEV, M_DEV, 0).reshape(blocks_dev, TM, D)
        mask_rows = lax.dynamic_slice_in_dim(edge_mask, partition_id * M_DEV, M_DEV, 0).reshape(blocks_dev, TM, KT * TS)
        tile_rows = lax.dynamic_slice_in_dim(tile_src, partition_id * blocks_dev, blocks_dev, 0)

        def one_block(tables, inputs):
            key_grad, value_grad = tables
            query_block, grad_block, validity, tile_ids = inputs
            key_block = key_table[tile_ids].reshape(-1, D)
            value_block = value_table[tile_ids].reshape(-1, D)
            attended, d_query, d_keys, d_values = block_terms(query_block, key_block, value_block, validity, grad_block)
            key_grad = key_grad.at[tile_ids].add(d_keys.reshape(-1, TS, D))
            value_grad = value_grad.at[tile_ids].add(d_values.reshape(-1, TS, D))
            return ((key_grad, value_grad), (attended, d_query.astype(jnp.bfloat16)))
        zero_table = jnp.zeros(key_table.shape, jnp.float32)
        (key_grad, value_grad), (attended, d_query) = lax.scan(one_block, (zero_table, zero_table), (query_rows, grad_rows, mask_rows, tile_rows))
        key_grad = lax.optimization_barrier(key_grad.reshape(-1, D).astype(jnp.bfloat16)).astype(jnp.float32)
        value_grad = lax.optimization_barrier(value_grad.reshape(-1, D).astype(jnp.bfloat16)).astype(jnp.float32)
        own_key_sum = lax.dynamic_slice_in_dim(key_sum, partition_id * G_DEV, G_DEV, 0) + key_grad[:G_DEV]
        own_value_sum = lax.dynamic_slice_in_dim(value_sum, partition_id * G_DEV, G_DEV, 0) + value_grad[:G_DEV]
        key_sum = lax.dynamic_update_slice_in_dim(key_sum, own_key_sum, partition_id * G_DEV, 0)
        value_sum = lax.dynamic_update_slice_in_dim(value_sum, own_value_sum, partition_id * G_DEV, 0)
        key_sum = key_sum.at[halo_index].add(key_grad[G_DEV:])
        value_sum = value_sum.at[halo_index].add(value_grad[G_DEV:])
        return ((key_sum, value_sum), (attended.reshape(M_DEV, D), d_query.reshape(M_DEV, D)))
    zero_grid = jnp.zeros((N_GRAPH * G_DEV, D), jnp.float32)
    (key_sum, value_sum), (attended, d_query) = lax.scan(partition, (zero_grid, zero_grid), peer_ids)
    attended = attended.reshape(-1, D)
    d_query = d_query.reshape(-1, D)
    key_sum = key_sum.astype(jnp.bfloat16)
    value_sum = value_sum.astype(jnp.bfloat16)
    mixed_sum = jnp.dot(attended, w_out, preferred_element_type=jnp.float32)
    mesh_out = (mesh_feat.astype(jnp.float32) + mixed_sum).astype(jnp.bfloat16)
    grad_wo = jnp.dot(attended.T, d_out, preferred_element_type=jnp.float32)
    grad_wq = 0.125 * jnp.dot(dst_normed.T, d_query, preferred_element_type=jnp.float32)
    grad_wk = jnp.dot(src_normed.T, key_sum, preferred_element_type=jnp.float32)
    grad_wv = jnp.dot(src_normed.T, value_sum, preferred_element_type=jnp.float32)
    d_src = jnp.dot(key_sum, w_key.T, preferred_element_type=jnp.float32) + jnp.dot(value_sum, w_value.T, preferred_element_type=jnp.float32)
    d_dst = 0.125 * jnp.dot(d_query, w_query.T, preferred_element_type=jnp.float32)
    grad_grid = norm_back(d_src * gain_src.astype(jnp.float32), src_hat, src_inverse).astype(jnp.bfloat16)
    grad_mesh = (d_out.astype(jnp.float32) + norm_back(d_dst * gain_dst.astype(jnp.float32), dst_hat, dst_inverse)).astype(jnp.bfloat16)
    return (mesh_out, grad_grid, grad_mesh, grad_wq, grad_wk, grad_wv, grad_wo)
```

```python
import jax
import jax.numpy as jnp
from jax import lax
from jax.experimental import pallas as pl
from jax.experimental.pallas import tpu as pltpu
from jax.sharding import PartitionSpec as P

HEAD = 64
PAIR = 2 * HEAD
TS = 128
TM = 512
QUAD = 4
BIG = 1e30

NT = (((1,), (1,)), ((), ()))
NN = (((1,), (0,)), ((), ()))
TN = (((0,), (0,)), ((), ()))


def mm(a, b, dims=NN):
    return lax.dot_general(a, b, dims, preferred_element_type=jnp.float32)


def params(mib, *semantics):
    return pltpu.CompilerParams(vmem_limit_bytes=mib * 2**20)


def vmem():
    return pl.BlockSpec(memory_space=pltpu.VMEM)


def smem():
    return pl.BlockSpec(memory_space=pltpu.SMEM)


def hat_of(values):
    centre = values - jnp.mean(values, axis=-1, keepdims=True)
    inverse = lax.rsqrt(jnp.mean(centre * centre, axis=-1, keepdims=True) + 1e-05)
    return centre * inverse, inverse


def norm_back(grad, hat, inverse):
    first = jnp.mean(grad, axis=-1, keepdims=True)
    second = jnp.mean(grad * hat, axis=-1, keepdims=True)
    return (grad - first - hat * second) * inverse


def source_kernel(feat_ref, gain_ref, weight_ref, normed_ref, pairs_ref):
    hat, _ = hat_of(feat_ref[...].astype(jnp.float32))
    normed = (hat * gain_ref[...]).astype(jnp.bfloat16)
    normed_ref[...] = normed
    pairs = mm(normed, weight_ref[...]).astype(jnp.bfloat16)
    for h in range(pairs_ref.shape[0]):
        pairs_ref[h] = pairs[:, h * PAIR : (h + 1) * PAIR]


def source_terms(feat, gain, weight):
    rows, width = feat.shape
    heads = weight.shape[1] // PAIR
    step = 512
    return pl.pallas_call(
        source_kernel,
        grid=(rows // step,),
        in_specs=[
            pl.BlockSpec((step, width), lambda i: (i, 0)),
            pl.BlockSpec((1, width), lambda i: (0, 0)),
            pl.BlockSpec(weight.shape, lambda i: (0, 0)),
        ],
        out_specs=[
            pl.BlockSpec((step, width), lambda i: (i, 0)),
            pl.BlockSpec((heads, step, PAIR), lambda i: (0, i, 0)),
        ],
        out_shape=[
            jax.ShapeDtypeStruct((rows, width), jnp.bfloat16),
            jax.ShapeDtypeStruct((heads, rows, PAIR), jnp.bfloat16),
        ],
        compiler_params=params(32),
        cost_estimate=pl.CostEstimate(
            flops=2 * rows * width * heads * PAIR, bytes_accessed=10 * 2**20, transcendentals=rows
        ),
        name="source_terms",
    )(feat, gain, weight)


def list_tiles(need_ref, list_ref):
    def add(t, count):
        used = need_ref[t] > 0

        @pl.when(used)
        def _():
            list_ref[count] = t

        return count + used.astype(jnp.int32)

    return lax.fori_loop(0, need_ref.shape[0], add, jnp.int32(0))


def gather_kernel(need_ref, pairs_ref, rows_ref, out_ref, table, list_ref):
    heads = pairs_ref.shape[0]
    table_rows = pairs_ref.shape[1]
    for h in range(heads):
        table[:, h * PAIR : (h + 1) * PAIR] = pairs_ref[h]
    count = list_tiles(need_ref, list_ref)
    depth = 256

    def quad(step, carry):
        tiles = [list_ref[jnp.minimum(step * QUAD + k, count - 1)] for k in range(QUAD)]
        wanted = jnp.concatenate(
            [jnp.transpose(jnp.broadcast_to(rows_ref[t], (TS, TS))) for t in tiles], axis=0
        )
        lane = lax.broadcasted_iota(jnp.int32, (QUAD * TS, TS), 1)
        away = wanted - lane
        total = jnp.zeros((QUAD * TS, heads * PAIR), jnp.float32)
        for c in range(table_rows // depth):
            hot = jnp.concatenate(
                [
                    jnp.where(away == c * depth + part * TS, 1.0, 0.0).astype(jnp.bfloat16)
                    for part in range(depth // TS)
                ],
                axis=1,
            )
            total = total + mm(hot, table[c * depth : (c + 1) * depth, :])
        total = total.astype(jnp.bfloat16)
        for k, t in enumerate(tiles):
            for h in range(heads):
                out_ref[t // 2, h, pl.ds((t % 2) * TS, TS), :] = total[
                    k * TS : (k + 1) * TS, h * PAIR : (h + 1) * PAIR
                ]
        return carry

    lax.fori_loop(0, (count + QUAD - 1) // QUAD, quad, 0)


def gather_rows(need, pairs, rows):
    heads, table_rows, _ = pairs.shape
    peers = need.shape[0] // 2
    return pl.pallas_call(
        gather_kernel,
        in_specs=[smem(), vmem(), vmem()],
        out_specs=vmem(),
        out_shape=jax.ShapeDtypeStruct((peers, heads, 2 * TS, PAIR), jnp.bfloat16),
        scratch_shapes=[
            pltpu.VMEM((table_rows, heads * PAIR), jnp.bfloat16),
            pltpu.SMEM((need.shape[0],), jnp.int32),
        ],
        compiler_params=params(40),
        cost_estimate=pl.CostEstimate(
            flops=6 * 10**9, bytes_accessed=6 * 2**20, transcendentals=0
        ),
        name="gather_rows",
    )(need, pairs, rows)


def target_kernel(feat_ref, gain_ref, wq_ref, wo_ref, cot_ref, normed_ref, pairs_ref):
    hat, _ = hat_of(feat_ref[...].astype(jnp.float32))
    normed = (hat * gain_ref[...]).astype(jnp.bfloat16)
    normed_ref[...] = normed
    cot = jnp.concatenate([cot_ref[f] for f in range(cot_ref.shape[0])], axis=1)
    pairs = mm(normed, wq_ref[...]) * 0.125 + mm(cot, wo_ref[...])
    pairs = pairs.astype(jnp.bfloat16)
    for h in range(pairs_ref.shape[0]):
        pairs_ref[h] = pairs[:, h * PAIR : (h + 1) * PAIR]


def target_terms(feat, gain, wq, wo, cot):
    rows, width = feat.shape
    heads = wq.shape[1] // PAIR
    groups, _, columns = cot.shape
    step = 512
    return pl.pallas_call(
        target_kernel,
        grid=(rows // step,),
        in_specs=[
            pl.BlockSpec((step, width), lambda i: (i, 0)),
            pl.BlockSpec((1, width), lambda i: (0, 0)),
            pl.BlockSpec(wq.shape, lambda i: (0, 0)),
            pl.BlockSpec(wo.shape, lambda i: (0, 0)),
            pl.BlockSpec((groups, step, columns), lambda i: (0, i, 0)),
        ],
        out_specs=[
            pl.BlockSpec((step, width), lambda i: (i, 0)),
            pl.BlockSpec((heads, step, PAIR), lambda i: (0, i, 0)),
        ],
        out_shape=[
            jax.ShapeDtypeStruct((rows, width), jnp.bfloat16),
            jax.ShapeDtypeStruct((heads, rows, PAIR), jnp.bfloat16),
        ],
        compiler_params=params(32),
        cost_estimate=pl.CostEstimate(
            flops=4 * rows * width * heads * PAIR, bytes_accessed=8 * 2**20, transcendentals=rows
        ),
        name="target_terms",
    )(feat, gain, wq, wo, cot)


def attention_kernel(
    tiles_ref,
    own_ref,
    halo_ref,
    pairs_ref,
    valid_ref,
    mixed_ref,
    own_grad_ref,
    halo_grad_ref,
    table,
    bias,
    scores,
    slopes,
    both,
    total,
    sems,
):
    j = pl.program_id(0)
    blocks, heads, tiles = table.shape[0], table.shape[1], table.shape[2]
    own_tiles = own_ref.shape[1] // TS

    def fetch(b, h, k, start):
        t = tiles_ref[b, k]
        if not start:
            pltpu.make_async_copy(
                own_ref.at[h, pl.ds(0, TS), :], table.at[b, h, k], sems.at[b, h, k]
            ).wait()
            return

        @pl.when(t < own_tiles)
        def _():
            pltpu.make_async_copy(
                own_ref.at[h, pl.ds(pl.multiple_of(t * TS, TS), TS), :],
                table.at[b, h, k],
                sems.at[b, h, k],
            ).start()

        @pl.when(t >= own_tiles)
        def _():
            o = t - own_tiles
            pltpu.make_async_copy(
                halo_ref.at[o // 2, h, pl.ds(pl.multiple_of((o % 2) * TS, TS), TS), :],
                table.at[b, h, k],
                sems.at[b, h, k],
            ).start()

    @pl.when(j == 0)
    def _():
        for b in range(blocks):
            for h in range(heads):
                for k in range(tiles):
                    fetch(b, h, k, True)

        def clear(t, carry):
            total[t] = jnp.zeros(total.shape[1:], jnp.float32)
            return carry

        lax.fori_loop(0, total.shape[0], clear, 0)

    for k in range(tiles):
        away = (valid_ref[:, k * TS : (k + 1) * TS] - 1).astype(jnp.float32) * BIG
        bias[k] = jnp.transpose(away)

    for h in range(heads):
        for k in range(tiles):
            fetch(j, h, k, False)

    first = lax.broadcasted_iota(jnp.int32, (1, PAIR), 1) < HEAD
    keep_first = jnp.where(first, 1.0, 0.0).astype(jnp.bfloat16)
    keep_second = jnp.where(first, 0.0, 1.0).astype(jnp.bfloat16)

    def fold(values, how):
        return how(values.reshape(TS // 8, 8, values.shape[-1]), axis=0)

    for h in range(heads):
        pairs = pairs_ref[h]
        queries = pairs * keep_first
        cots = pairs * keep_second
        highest = None
        for k in range(tiles):
            s = mm(table[j, h, k], queries, NT) + bias[k]
            scores[k] = s
            top = fold(s, jnp.max)
            highest = top if highest is None else jnp.maximum(highest, top)
        highest = jnp.max(highest, axis=0, keepdims=True)
        norm = None
        for k in range(tiles):
            e = jnp.exp(scores[k] - highest)
            scores[k] = e
            part = fold(e, jnp.sum)
            norm = part if norm is None else norm + part
        scale = 1.0 / jnp.sum(norm, axis=0, keepdims=True)
        delta = None
        for k in range(tiles):
            a = scores[k] * scale
            scores[k] = a
            both[k, :, TM:] = a.astype(jnp.bfloat16)
            d = mm(table[j, h, k], cots, NT)
            slopes[k] = d
            part = fold(a * d, jnp.sum)
            delta = part if delta is None else delta + part
        delta = jnp.sum(delta, axis=0, keepdims=True)
        for k in range(tiles):
            both[k, :, :TM] = (scores[k] * (slopes[k] - delta)).astype(jnp.bfloat16)
        stacked = jnp.concatenate([queries, cots], axis=0)
        for k in range(tiles):
            t = tiles_ref[j, k]
            total[t, h] = total[t, h] + mm(both[k], stacked)
        crossed = mm(
            table[j, h].reshape(tiles * TS, PAIR), both[...].reshape(tiles * TS, 2 * TM), TN
        )
        mixed = jnp.concatenate([crossed[:HEAD, :TM], crossed[HEAD:, TM:]], axis=0)
        mixed_ref[h] = jnp.transpose(mixed).astype(jnp.bfloat16)

    @pl.when(j == blocks - 1)
    def _():
        def own(t, carry):
            for h in range(heads):
                own_grad_ref[h, pl.ds(pl.multiple_of(t * TS, TS), TS), :] = total[t, h].astype(
                    jnp.bfloat16
                )
            return carry

        lax.fori_loop(0, own_tiles, own, 0)

        def halo(q, carry):
            for h in range(heads):
                for half in range(2):
                    halo_grad_ref[q, h, half * TS : (half + 1) * TS, :] = total[
                        own_tiles + 2 * q + half, h
                    ].astype(jnp.bfloat16)
            return carry

        lax.fori_loop(0, halo_grad_ref.shape[0], halo, 0)


def attention(tile_src, own, halo, pairs, valid):
    heads, rows, _ = pairs.shape
    blocks, tiles = tile_src.shape
    table_tiles = own.shape[1] // TS + 2 * halo.shape[0]
    slots = tiles * TS
    anywhere = pl.BlockSpec(memory_space=pl.ANY)
    return pl.pallas_call(
        attention_kernel,
        grid=(blocks,),
        in_specs=[
            smem(),
            anywhere,
            anywhere,
            pl.BlockSpec((heads, TM, PAIR), lambda j: (0, j, 0)),
            pl.BlockSpec((TM, slots), lambda j: (j, 0)),
        ],
        out_specs=[
            pl.BlockSpec((heads, TM, PAIR), lambda j: (0, j, 0)),
            pl.BlockSpec(own.shape, lambda j: (0, 0, 0)),
            pl.BlockSpec(halo.shape, lambda j: (0, 0, 0, 0)),
        ],
        out_shape=[
            jax.ShapeDtypeStruct((heads, rows, PAIR), jnp.bfloat16),
            jax.ShapeDtypeStruct(own.shape, jnp.bfloat16),
            jax.ShapeDtypeStruct(halo.shape, jnp.bfloat16),
        ],
        scratch_shapes=[
            pltpu.VMEM((blocks, heads, tiles, TS, PAIR), jnp.bfloat16),
            pltpu.VMEM((tiles, TS, TM), jnp.float32),
            pltpu.VMEM((tiles, TS, TM), jnp.float32),
            pltpu.VMEM((tiles, TS, TM), jnp.float32),
            pltpu.VMEM((tiles, TS, 2 * TM), jnp.bfloat16),
            pltpu.VMEM((table_tiles, heads, TS, PAIR), jnp.float32),
            pltpu.SemaphoreType.DMA((blocks, heads, tiles)),
        ],
        compiler_params=params(56),
        cost_estimate=pl.CostEstimate(
            flops=12 * heads * rows * slots * PAIR,
            bytes_accessed=24 * 2**20,
            transcendentals=heads * rows * slots,
        ),
        name="attention",
    )(tile_src, own, halo, pairs, valid)


def scatter_kernel(need_ref, own_ref, halo_ref, rows_ref, out_ref, total, list_ref):
    heads, table_rows, _ = own_ref.shape
    groups, _, group_rows, _ = out_ref.shape
    for h in range(heads):
        total[:, h * PAIR : (h + 1) * PAIR] = own_ref[h].astype(jnp.float32)
    count = list_tiles(need_ref, list_ref)

    def quad(step, carry):
        spots, parts = [], []
        for k in range(QUAD):
            place = step * QUAD + k
            t = list_ref[jnp.minimum(place, count - 1)]
            spots.append(jnp.where(place < count, rows_ref[t], -1))
            parts.append(
                jnp.concatenate(
                    [halo_ref[t // 2, h, pl.ds((t % 2) * TS, TS), :] for h in range(heads)], axis=1
                )
            )
        spots = jnp.concatenate(spots, axis=1)
        parts = jnp.concatenate(parts, axis=0)
        away = spots - lax.broadcasted_iota(jnp.int32, (512, QUAD * TS), 0)
        for c in range(table_rows // 512):
            hot = jnp.where(away == c * 512, 1.0, 0.0).astype(jnp.bfloat16)
            here = slice(c * 512, (c + 1) * 512)
            total[here, :] = total[here, :] + mm(hot, parts)
        return carry

    lax.fori_loop(0, (count + QUAD - 1) // QUAD, quad, 0)
    for f in range(groups):
        for h in range(heads):
            out_ref[f, h] = total[
                f * group_rows : (f + 1) * group_rows, h * PAIR : (h + 1) * PAIR
            ].astype(jnp.bfloat16)


def scatter_rows(need, own, halo, rows, groups):
    heads, table_rows, _ = own.shape
    return pl.pallas_call(
        scatter_kernel,
        in_specs=[smem(), vmem(), vmem(), vmem()],
        out_specs=vmem(),
        out_shape=jax.ShapeDtypeStruct(
            (groups, heads, table_rows // groups, PAIR), jnp.bfloat16
        ),
        scratch_shapes=[
            pltpu.VMEM((table_rows, heads * PAIR), jnp.float32),
            pltpu.SMEM((need.shape[0],), jnp.int32),
        ],
        compiler_params=params(40),
        cost_estimate=pl.CostEstimate(
            flops=6 * 10**9, bytes_accessed=8 * 2**20, transcendentals=0
        ),
        name="scatter_rows",
    )(need, own, halo, rows)


def wide_of(ref, keep=None):
    parts = []
    for f in range(ref.shape[0]):
        for h in range(ref.shape[1]):
            part = ref[f, h]
            parts.append(part if keep is None else part * keep)
    return jnp.concatenate(parts, axis=1)


def grid_kernel(where_ref, sums_ref, weight_ref, feat_ref, gain_ref, out_ref):
    groups, heads = sums_ref.shape[0], sums_ref.shape[1]
    weight = weight_ref[...].reshape(groups * heads * PAIR, -1)
    d_src = mm(wide_of(sums_ref), weight)
    hat, inverse = hat_of(feat_ref[...].astype(jnp.float32))
    result = norm_back(d_src * gain_ref[...], hat, inverse).astype(jnp.bfloat16)
    columns = out_ref.shape[2]
    for f in range(groups):
        out_ref[f] = result[:, f * columns : (f + 1) * columns]


def grid_rows(where, sums, weight, feat, gain):
    groups, heads, rows, _ = sums.shape
    width = feat.shape[1]
    step = 512
    steps = rows // step
    return pl.pallas_call(
        grid_kernel,
        grid_spec=pltpu.PrefetchScalarGridSpec(
            num_scalar_prefetch=1,
            grid=(steps,),
            in_specs=[
                pl.BlockSpec((groups, heads, step, PAIR), lambda i, w: (0, 0, i, 0)),
                pl.BlockSpec(weight.shape, lambda i, w: (0, 0, 0, 0)),
                pl.BlockSpec((step, width), lambda i, w: (w[0] * steps + i, 0)),
                pl.BlockSpec((1, width), lambda i, w: (0, 0)),
            ],
            out_specs=pl.BlockSpec((groups, step, width // groups), lambda i, w: (0, i, 0)),
        ),
        out_shape=jax.ShapeDtypeStruct((groups, rows, width // groups), jnp.bfloat16),
        compiler_params=params(32),
        cost_estimate=pl.CostEstimate(
            flops=2 * rows * width * groups * heads * PAIR,
            bytes_accessed=6 * 2**20,
            transcendentals=rows,
        ),
        name="grid_rows",
    )(where, sums, weight, feat, gain)


def mesh_kernel(where_ref, mixed_ref, weight_ref, feat_ref, cot_ref, gain_ref, out_ref):
    groups, heads = mixed_ref.shape[0], mixed_ref.shape[1]
    first = lax.broadcasted_iota(jnp.int32, (1, PAIR), 1) < HEAD
    keep_first = jnp.where(first, 1.0, 0.0).astype(jnp.bfloat16)
    keep_second = jnp.where(first, 0.0, 1.0).astype(jnp.bfloat16)
    weight = weight_ref[...].reshape(groups * heads * PAIR, -1)
    d_dst = mm(wide_of(mixed_ref, keep_first), weight) * 0.125
    added = mm(wide_of(mixed_ref, keep_second), weight)
    feat = feat_ref[...].astype(jnp.float32)
    hat, inverse = hat_of(feat)
    back = norm_back(d_dst * gain_ref[...], hat, inverse)
    cot = jnp.concatenate([cot_ref[f] for f in range(groups)], axis=1).astype(jnp.float32)
    mesh_out = (feat + added).astype(jnp.bfloat16)
    grad_mesh = (cot + back).astype(jnp.bfloat16)
    columns = out_ref.shape[3]
    for f in range(groups):
        out_ref[f, 0] = mesh_out[:, f * columns : (f + 1) * columns]
        out_ref[f, 1] = grad_mesh[:, f * columns : (f + 1) * columns]


def mesh_rows(where, mixed, weight, feat, cot, gain):
    groups, heads, rows, _ = mixed.shape
    width = feat.shape[1]
    columns = width // groups
    return pl.pallas_call(
        mesh_kernel,
        grid_spec=pltpu.PrefetchScalarGridSpec(
            num_scalar_prefetch=1,
            grid=(1,),
            in_specs=[
                pl.BlockSpec(mixed.shape, lambda i, w: (0, 0, 0, 0)),
                pl.BlockSpec(weight.shape, lambda i, w: (0, 0, 0, 0)),
                pl.BlockSpec((rows, width), lambda i, w: (w[0], 0)),
                pl.BlockSpec((groups, rows, columns), lambda i, w: (0, w[0], 0)),
                pl.BlockSpec((1, width), lambda i, w: (0, 0)),
            ],
            out_specs=pl.BlockSpec((groups, 2, rows, columns), lambda i, w: (0, 0, 0, 0)),
        ),
        out_shape=jax.ShapeDtypeStruct((groups, 2, rows, columns), jnp.bfloat16),
        compiler_params=params(32),
        cost_estimate=pl.CostEstimate(
            flops=4 * rows * width * groups * heads * PAIR,
            bytes_accessed=6 * 2**20,
            transcendentals=rows,
        ),
        name="mesh_rows",
    )(where, mixed, weight, feat, cot, gain)


def exchange(values, axis):
    return lax.all_to_all(values, axis, split_axis=0, concat_axis=0, tiled=True)


def sum_over_graph(values, peers):
    rows, columns = values.shape
    shares = exchange(values.reshape(peers, rows // peers, columns), "graph")
    share = jnp.sum(shares, axis=0)
    return exchange(jnp.broadcast_to(share[None], shares.shape), "graph").reshape(rows, columns)


def by_head(first, second, axis):
    parts = []
    for h in range(first.shape[axis] // HEAD):
        parts.append(lax.slice_in_dim(first, h * HEAD, (h + 1) * HEAD, axis=axis))
        parts.append(lax.slice_in_dim(second, h * HEAD, (h + 1) * HEAD, axis=axis))
    return jnp.concatenate(parts, axis=axis)


def body(
    grid_feat,
    mesh_feat,
    send_rows,
    tile_src,
    edge_mask,
    gain_src,
    gain_dst,
    w_query,
    w_key,
    w_value,
    w_out,
    d_out,
):
    grid_count, width = grid_feat.shape
    mesh_count = mesh_feat.shape[0]
    columns = w_query.shape[1]
    heads = columns // HEAD
    groups = width // columns
    peers = send_rows.shape[1]
    own_tiles = grid_count // TS
    where = lax.axis_index("feat").astype(jnp.int32).reshape(1)
    gain_src = gain_src.reshape(1, width)
    gain_dst = gain_dst.reshape(1, width)
    rows = send_rows.reshape(2 * peers, 1, TS)

    wanted = own_tiles + jnp.arange(2 * peers, dtype=jnp.int32)
    need = jnp.any(tile_src.reshape(-1, 1) == wanted[None, :], axis=0).astype(jnp.int32)
    need = exchange(
        jnp.broadcast_to(need.reshape(peers, 2, 1), (peers, 2, TS)), "graph"
    )[:, :, 0].reshape(-1)

    normed_src, pairs = source_terms(grid_feat, gain_src, by_head(w_key, w_value, 1))
    halo = exchange(gather_rows(need, pairs, rows), "graph")

    cot = lax.all_gather(d_out, "feat", axis=0)
    back_weights = jnp.stack(
        [
            by_head(w_key.T, w_value.T, 0).reshape(heads, PAIR, width),
            by_head(w_query.T, w_out, 0).reshape(heads, PAIR, width),
        ]
    )
    back_weights = lax.all_gather(back_weights, "feat", axis=0)

    zeros = jnp.zeros_like(w_query)
    normed_dst, targets = target_terms(
        mesh_feat, gain_dst, by_head(w_query, zeros, 1), by_head(zeros, w_out.T, 1), cot
    )
    mixed, own_grad, halo_grad = attention(tile_src, pairs, halo, targets, edge_mask)

    returned = exchange(halo_grad, "graph")

    mixed_rows = exchange(
        jnp.swapaxes(mixed.reshape(heads, groups, mesh_count // groups, PAIR), 0, 1), "feat"
    )
    mesh_result = exchange(
        mesh_rows(where, mixed_rows, back_weights[:, 1], mesh_feat, cot, gain_dst), "feat"
    )
    mesh_out = mesh_result[:, 0].reshape(mesh_count, columns)
    grad_mesh = mesh_result[:, 1].reshape(mesh_count, columns)
    d_query = jnp.concatenate([mixed[h, :, :HEAD] for h in range(heads)], axis=1)
    attended = jnp.concatenate([mixed[h, :, HEAD:] for h in range(heads)], axis=1)
    full_cot = jnp.swapaxes(cot, 0, 1).reshape(mesh_count, width)
    grad_wq = 0.125 * mm(normed_dst, d_query, TN)
    grad_wo = mm(attended, full_cot, TN)

    sums = scatter_rows(need, own_grad, returned, rows, groups)
    columns_of = jnp.swapaxes(sums, 0, 1).reshape(heads, grid_count, PAIR)
    grad_pairs = [mm(normed_src, columns_of[h], TN) for h in range(heads)]
    grad_wk = jnp.concatenate([g[:, :HEAD] for g in grad_pairs], axis=1)
    grad_wv = jnp.concatenate([g[:, HEAD:] for g in grad_pairs], axis=1)
    sum_rows = exchange(sums, "feat")
    grad_grid = exchange(
        grid_rows(where, sum_rows, back_weights[:, 0], grid_feat, gain_src), "feat"
    ).reshape(grid_count, columns)

    early = sum_over_graph(
        jnp.concatenate([grad_wq, grad_wo.reshape(width, columns)], axis=0), peers
    )
    late = sum_over_graph(jnp.concatenate([grad_wk, grad_wv], axis=0), peers)
    return (
        mesh_out,
        grad_grid,
        grad_mesh,
        early[:width],
        late[:width],
        late[width:],
        early[width:].reshape(columns, width),
    )


def solution(mesh):
    in_specs = (
        P("graph", None),
        P("graph", None),
        P("graph", None, None),
        P("graph", None),
        P("graph", None),
        P(),
        P(),
        P(None, "feat"),
        P(None, "feat"),
        P(None, "feat"),
        P("feat", None),
        P("graph", "feat"),
    )
    out_specs = (
        P("graph", "feat"),
        P("graph", "feat"),
        P("graph", "feat"),
        P(None, "feat"),
        P(None, "feat"),
        P(None, "feat"),
        P("feat", None),
    )
    return jax.shard_map(body, mesh=mesh, in_specs=in_specs, out_specs=out_specs, check_vma=False)
```

```python
import jax
import jax.numpy as jnp
from jax import lax
from jax.experimental import pallas as pl
from jax.experimental.pallas import tpu as pltpu
from jax.sharding import PartitionSpec as P

HEAD = 64
PAIR = 2 * HEAD
TS = 128
TM = 512
QUAD = 4
BIG = 1e30

NT = (((1,), (1,)), ((), ()))
NN = (((1,), (0,)), ((), ()))
TN = (((0,), (0,)), ((), ()))


def mm(a, b, dims=NN):
    return lax.dot_general(a, b, dims, preferred_element_type=jnp.float32)


def room(mib):
    return pltpu.CompilerParams(vmem_limit_bytes=mib * 2**20)


VMEM = pl.BlockSpec(memory_space=pltpu.VMEM)
SMEM = pl.BlockSpec(memory_space=pltpu.SMEM)
ANY = pl.BlockSpec(memory_space=pl.ANY)


def cost(microseconds):
    return pl.CostEstimate(
        flops=int(microseconds * 1.15e9), bytes_accessed=2**20, transcendentals=0
    )


def hat_of(values):
    centre = values - jnp.mean(values, axis=-1, keepdims=True)
    inverse = lax.rsqrt(jnp.mean(centre * centre, axis=-1, keepdims=True) + 1e-05)
    return centre * inverse, inverse


def norm_back(grad, hat, inverse):
    first = jnp.mean(grad, axis=-1, keepdims=True)
    second = jnp.mean(grad * hat, axis=-1, keepdims=True)
    return (grad - first - hat * second) * inverse


def halves():
    first = lax.broadcasted_iota(jnp.int32, (1, PAIR), 1) < HEAD
    return (
        jnp.where(first, 1.0, 0.0).astype(jnp.bfloat16),
        jnp.where(first, 0.0, 1.0).astype(jnp.bfloat16),
    )


def source_kernel(feat_hbm, gain_ref, key_ref, value_ref, pairs_ref, weight, feat, sems):
    i = pl.program_id(0)
    ahead = 3

    def fetch(n):
        step = feat.shape[1]
        here = pl.ds(pl.multiple_of(n * step, step), step)
        return pltpu.make_async_copy(feat_hbm.at[here, :], feat.at[n], sems.at[n])

    @pl.when(i == 0)
    def _():
        for n in range(ahead):
            fetch(n).start()
        for h in range(key_ref.shape[1] // HEAD):
            here = slice(h * HEAD, (h + 1) * HEAD)
            weight[:, h * PAIR : (h + 1) * PAIR] = jnp.concatenate(
                [key_ref[:, here], value_ref[:, here]], axis=1
            )

    @pl.when(i + ahead < feat.shape[0])
    def _():
        fetch(i + ahead).start()

    fetch(i).wait()
    hat, _ = hat_of(feat[i].astype(jnp.float32))
    normed = (hat * gain_ref[...]).astype(jnp.bfloat16)
    pairs_ref[...] = mm(normed, weight[...]).astype(jnp.bfloat16)


def source_terms(feat, gain, w_key, w_value):
    rows, width = feat.shape
    wide = 2 * w_key.shape[1]
    step = 512
    steps = rows // step
    whole = pl.BlockSpec(w_key.shape, lambda i: (0, 0))
    return pl.pallas_call(
        source_kernel,
        grid=(steps,),
        in_specs=[ANY, pl.BlockSpec((1, width), lambda i: (0, 0)), whole, whole],
        out_specs=pl.BlockSpec((step, wide), lambda i: (i, 0)),
        out_shape=jax.ShapeDtypeStruct((rows, wide), jnp.bfloat16),
        scratch_shapes=[
            pltpu.VMEM((width, wide), jnp.bfloat16),
            pltpu.VMEM((steps, step, width), jnp.bfloat16),
            pltpu.SemaphoreType.DMA((steps,)),
        ],
        compiler_params=room(60),
        cost_estimate=cost(8),
        name="source_terms",
    )(feat, gain, w_key, w_value)


def list_tiles(need_ref, list_ref):
    def add(t, count):
        used = need_ref[t] > 0

        @pl.when(used)
        def _():
            list_ref[count] = t

        return count + used.astype(jnp.int32)

    return lax.fori_loop(0, need_ref.shape[0], add, jnp.int32(0))


def gather_kernel(need_ref, rows_ref, table_ref, *rest):
    out_refs = rest[:-4]
    hot, sent, list_ref, sems = rest[-4:]
    half = table_ref.shape[1]
    count = list_tiles(need_ref, list_ref)

    def copy(slot, k, h, t):
        return pltpu.make_async_copy(
            sent.at[slot, h, pl.ds(k * TS, TS), :],
            out_refs[h].at[t // 2, pl.ds(pl.multiple_of((t % 2) * TS, TS), TS), :],
            sems.at[slot, k, h],
        )

    def each(step, act):
        for k in range(QUAD):
            place = step * QUAD + k

            @pl.when(jnp.logical_and(place >= 0, place < count))
            def _():
                t = list_ref[jnp.maximum(place, 0)]
                for h in range(len(out_refs)):
                    act(copy(lax.rem(step + 2, 2), k, h, t))

    def quad(step, carry):
        tiles = [list_ref[jnp.minimum(step * QUAD + k, count - 1)] for k in range(QUAD)]
        wanted = jnp.concatenate(
            [jnp.transpose(jnp.broadcast_to(rows_ref[t], (TS, TS))) for t in tiles], axis=0
        )
        upper = wanted >= half
        away = jnp.where(upper, wanted - half, wanted)
        away = away - lax.broadcasted_iota(jnp.int32, (QUAD * TS, TS), 1)
        for c in range(half // TS):
            hot[:, c * TS : (c + 1) * TS] = jnp.where(away == c * TS, 1.0, 0.0).astype(
                jnp.bfloat16
            )
        low = mm(hot[...], table_ref[0])
        high = mm(hot[...], table_ref[1])
        each(step - 2, lambda c: c.wait())
        slot = lax.rem(step, 2)
        for h in range(len(out_refs)):
            here = slice(h * PAIR, (h + 1) * PAIR)
            sent[slot, h] = jnp.where(upper, high[:, here], low[:, here]).astype(jnp.bfloat16)
        each(step, lambda c: c.start())
        return carry

    steps = (count + QUAD - 1) // QUAD
    lax.fori_loop(0, steps, quad, 0)
    each(steps - 2, lambda c: c.wait())
    each(steps - 1, lambda c: c.wait())


def gather_rows(need, rows, pairs):
    count, wide = pairs.shape
    heads = wide // PAIR
    peers = need.shape[0] // 2
    return pl.pallas_call(
        gather_kernel,
        in_specs=[SMEM, VMEM, VMEM],
        out_specs=[ANY] * heads,
        out_shape=[jax.ShapeDtypeStruct((peers, 2 * TS, PAIR), jnp.bfloat16)] * heads,
        scratch_shapes=[
            pltpu.VMEM((QUAD * TS, count // 2), jnp.bfloat16),
            pltpu.VMEM((2, heads, QUAD * TS, PAIR), jnp.bfloat16),
            pltpu.SMEM((need.shape[0],), jnp.int32),
            pltpu.SemaphoreType.DMA((2, QUAD, heads)),
        ],
        compiler_params=room(60),
        cost_estimate=cost(10),
        name="gather_rows",
    )(need, rows, pairs.reshape(2, count // 2, wide))


def normed_kernel(feat_ref, gain_ref, normed_ref):
    hat, _ = hat_of(feat_ref[...].astype(jnp.float32))
    normed_ref[...] = (hat * gain_ref[...]).astype(jnp.bfloat16)


def normed_rows(feat, gain):
    rows, width = feat.shape
    step = 512
    return pl.pallas_call(
        normed_kernel,
        grid=(rows // step,),
        in_specs=[
            pl.BlockSpec((step, width), lambda i: (i, 0)),
            pl.BlockSpec((1, width), lambda i: (0, 0)),
        ],
        out_specs=pl.BlockSpec((step, width), lambda i: (i, 0)),
        out_shape=jax.ShapeDtypeStruct((rows, width), jnp.bfloat16),
        compiler_params=room(60),
        cost_estimate=cost(8),
        name="normed_rows",
    )(feat, gain)


def target_kernel(feat_ref, gain_ref, wq_ref, wo_ref, cot_ref, normed_ref, *pairs_refs):
    hat, _ = hat_of(feat_ref[...].astype(jnp.float32))
    normed = (hat * gain_ref[...]).astype(jnp.bfloat16)
    normed_ref[...] = normed
    cot = jnp.concatenate([cot_ref[f] for f in range(cot_ref.shape[0])], axis=1)
    queries = (mm(normed, wq_ref[...]) * 0.125).astype(jnp.bfloat16)
    cots = mm(cot, wo_ref[...], NT).astype(jnp.bfloat16)
    for h, ref in enumerate(pairs_refs):
        here = slice(h * HEAD, (h + 1) * HEAD)
        ref[...] = jnp.concatenate([queries[:, here], cots[:, here]], axis=1)


def target_terms(feat, gain, w_query, w_out, cot):
    rows, width = feat.shape
    groups, _, columns = cot.shape
    heads = columns // HEAD
    step = 512
    return pl.pallas_call(
        target_kernel,
        grid=(rows // step,),
        in_specs=[
            pl.BlockSpec((step, width), lambda i: (i, 0)),
            pl.BlockSpec((1, width), lambda i: (0, 0)),
            pl.BlockSpec(w_query.shape, lambda i: (0, 0)),
            pl.BlockSpec(w_out.shape, lambda i: (0, 0)),
            pl.BlockSpec((groups, step, columns), lambda i: (0, i, 0)),
        ],
        out_specs=[pl.BlockSpec((step, width), lambda i: (i, 0))]
        + [pl.BlockSpec((step, PAIR), lambda i: (i, 0))] * heads,
        out_shape=[jax.ShapeDtypeStruct((rows, width), jnp.bfloat16)]
        + [jax.ShapeDtypeStruct((rows, PAIR), jnp.bfloat16)] * heads,
        compiler_params=room(60),
        cost_estimate=cost(6),
        name="target_terms",
    )(feat, gain, w_query, w_out, cot)


def attention_kernel(
    head,
    tiles_ref,
    own_ref,
    halo_ref,
    pairs_ref,
    valid_ref,
    normed_ref,
    cot_ref,
    own_grad_ref,
    halo_grad_ref,
    weight_grad_ref,
    mixed_ref,
    table,
    bias,
    scores,
    slopes,
    both,
    total,
    sems,
):
    j = pl.program_id(0)
    blocks, tiles = table.shape[0], table.shape[1]
    own_tiles = own_ref.shape[0] // TS

    def fetch(b, k):
        t = tiles_ref[b, k]

        @pl.when(t < own_tiles)
        def _():
            here = pl.ds(pl.multiple_of(t * TS, TS), TS)
            pltpu.make_async_copy(
                own_ref.at[here, pl.ds(head * PAIR, PAIR)], table.at[b, k], sems.at[b, k]
            ).start()

        @pl.when(t >= own_tiles)
        def _():
            o = t - own_tiles
            here = pl.ds(pl.multiple_of((o % 2) * TS, TS), TS)
            pltpu.make_async_copy(
                halo_ref.at[o // 2, here, :], table.at[b, k], sems.at[b, k]
            ).start()

    @pl.when(j == 0)
    def _():
        for b in range(blocks):
            for k in range(tiles):
                fetch(b, k)

        def clear(t, carry):
            total[t] = jnp.zeros(total.shape[1:], jnp.float32)
            return carry

        lax.fori_loop(0, total.shape[0], clear, 0)
        weight_grad_ref[...] = jnp.zeros(weight_grad_ref.shape, jnp.float32)

    for k in range(tiles):
        away = (valid_ref[:, k * TS : (k + 1) * TS] - 1).astype(jnp.float32) * BIG
        bias[k] = jnp.transpose(away)

    for k in range(tiles):
        pltpu.make_async_copy(
            own_ref.at[pl.ds(0, TS), pl.ds(head * PAIR, PAIR)], table.at[j, k], sems.at[j, k]
        ).wait()

    def fold(values, how):
        return how(values.reshape(TS // 8, 8, values.shape[-1]), axis=0)

    keep_first, keep_second = halves()
    pairs = pairs_ref[...]
    queries = pairs * keep_first
    cots = pairs * keep_second
    highest = None
    for k in range(tiles):
        s = mm(table[j, k], queries, NT) + bias[k]
        scores[k] = s
        top = fold(s, jnp.max)
        highest = top if highest is None else jnp.maximum(highest, top)
    highest = jnp.max(highest, axis=0, keepdims=True)
    norm = None
    for k in range(tiles):
        e = jnp.exp(scores[k] - highest)
        scores[k] = e
        part = fold(e, jnp.sum)
        norm = part if norm is None else norm + part
    scale = 1.0 / jnp.sum(norm, axis=0, keepdims=True)
    delta = None
    for k in range(tiles):
        a = scores[k] * scale
        scores[k] = a
        both[k, :, TM:] = a.astype(jnp.bfloat16)
        d = mm(table[j, k], cots, NT)
        slopes[k] = d
        part = fold(a * d, jnp.sum)
        delta = part if delta is None else delta + part
    delta = jnp.sum(delta, axis=0, keepdims=True)
    for k in range(tiles):
        both[k, :, :TM] = (scores[k] * (slopes[k] - delta)).astype(jnp.bfloat16)
    stacked = jnp.concatenate([queries, cots], axis=0)
    for k in range(tiles):
        t = tiles_ref[j, k]
        total[t] = total[t] + mm(both[k], stacked)
    crossed = mm(table[j].reshape(tiles * TS, PAIR), both[...].reshape(tiles * TS, 2 * TM), TN)
    d_query = crossed[:HEAD, :TM]
    attended = crossed[HEAD:, TM:]
    mixed = jnp.concatenate([d_query, attended], axis=0)
    mixed_ref[...] = jnp.transpose(mixed).astype(jnp.bfloat16)
    cot = jnp.concatenate([cot_ref[f] for f in range(cot_ref.shape[0])], axis=1)
    wq_part = mm(d_query.astype(jnp.bfloat16), normed_ref[...])
    wo_part = mm(attended.astype(jnp.bfloat16), cot)
    columns = weight_grad_ref.shape[2]
    for f in range(weight_grad_ref.shape[0]):
        here = slice(f * columns, (f + 1) * columns)
        weight_grad_ref[f, :HEAD] += wq_part[:, here]
        weight_grad_ref[f, HEAD:] += wo_part[:, here]

    @pl.when(j == blocks - 1)
    def _():
        def own(t, carry):
            here = pl.ds(pl.multiple_of(t * TS, TS), TS)
            own_grad_ref[here, :] = total[t].astype(jnp.bfloat16)
            return carry

        lax.fori_loop(0, own_tiles, own, 0)

        def halo(q, carry):
            for half in range(2):
                halo_grad_ref[q, half * TS : (half + 1) * TS, :] = total[
                    own_tiles + 2 * q + half
                ].astype(jnp.bfloat16)
            return carry

        lax.fori_loop(0, halo_grad_ref.shape[0], halo, 0)


def attention(head, tile_src, own, halo, pairs, valid, normed, cot):
    rows, _ = pairs.shape
    blocks, tiles = tile_src.shape
    groups, _, columns = cot.shape
    width = normed.shape[1]
    own_grad = (own.shape[0], PAIR)
    table_tiles = own.shape[0] // TS + 2 * halo.shape[0]
    slots = tiles * TS
    return pl.pallas_call(
        lambda *refs: attention_kernel(head, *refs),
        grid=(blocks,),
        in_specs=[
            SMEM,
            ANY,
            ANY,
            pl.BlockSpec((TM, PAIR), lambda j: (j, 0)),
            pl.BlockSpec((TM, slots), lambda j: (j, 0)),
            pl.BlockSpec((TM, width), lambda j: (j, 0)),
            pl.BlockSpec((groups, TM, columns), lambda j: (0, j, 0)),
        ],
        out_specs=[
            pl.BlockSpec(own_grad, lambda j: (0, 0)),
            pl.BlockSpec(halo.shape, lambda j: (0, 0, 0)),
            pl.BlockSpec((groups, PAIR, columns), lambda j: (0, 0, 0)),
            pl.BlockSpec((TM, PAIR), lambda j: (j, 0)),
        ],
        out_shape=[
            jax.ShapeDtypeStruct(own_grad, jnp.bfloat16),
            jax.ShapeDtypeStruct(halo.shape, jnp.bfloat16),
            jax.ShapeDtypeStruct((groups, PAIR, columns), jnp.float32),
            jax.ShapeDtypeStruct((rows, PAIR), jnp.bfloat16),
        ],
        scratch_shapes=[
            pltpu.VMEM((blocks, tiles, TS, PAIR), jnp.bfloat16),
            pltpu.VMEM((tiles, TS, TM), jnp.float32),
            pltpu.VMEM((tiles, TS, TM), jnp.float32),
            pltpu.VMEM((tiles, TS, TM), jnp.float32),
            pltpu.VMEM((tiles, TS, 2 * TM), jnp.bfloat16),
            pltpu.VMEM((table_tiles, TS, PAIR), jnp.float32),
            pltpu.SemaphoreType.DMA((blocks, tiles)),
        ],
        compiler_params=room(60),
        cost_estimate=cost(18),
        name="attention",
    )(tile_src, own, halo, pairs, valid, normed, cot)


def scatter_kernel(earlier, where_ref, need_ref, own_ref, halo_ref, rows_ref, normed_hbm, *rest):
    *rest, total, normed, grad, list_ref, sem = rest
    done, grad_ref, out_refs = rest[:earlier], rest[earlier], rest[earlier + 1 :]
    table_rows = own_ref.shape[0]
    half = table_rows // 2
    groups = len(out_refs)
    group_rows = table_rows // groups
    chunk = 512
    fetch = pltpu.make_async_copy(normed_hbm, normed, sem)
    fetch.start()
    total[...] = own_ref[...].astype(jnp.float32)
    count = list_tiles(need_ref, list_ref)

    def quad(step, carry):
        spots, parts = [], []
        for k in range(QUAD):
            place = step * QUAD + k
            t = list_ref[jnp.minimum(place, count - 1)]
            spot = jnp.where(place < count, rows_ref[t], -1)
            upper = jnp.transpose(jnp.broadcast_to(spot, (TS, TS))) >= half
            part = halo_ref[t // 2, pl.ds((t % 2) * TS, TS), :]
            keep = jnp.where(upper, 1.0, 0.0).astype(jnp.bfloat16)
            drop = jnp.where(upper, 0.0, 1.0).astype(jnp.bfloat16)
            parts.append(jnp.concatenate([part * drop, part * keep], axis=1))
            spots.append(jnp.where(spot >= half, spot - half, spot))
        spots = jnp.concatenate(spots, axis=1)
        parts = jnp.concatenate(parts, axis=0)
        away = spots - lax.broadcasted_iota(jnp.int32, (chunk, QUAD * TS), 0)
        for c in range(half // chunk):
            hot = jnp.where(away == c * chunk, 1.0, 0.0).astype(jnp.bfloat16)
            added = mm(hot, parts)
            for n in range(2):
                here = slice(n * half + c * chunk, n * half + (c + 1) * chunk)
                total[here, :] = total[here, :] + added[:, n * PAIR : (n + 1) * PAIR]
        return carry

    lax.fori_loop(0, (count + QUAD - 1) // QUAD, quad, 0)
    for s, ref in enumerate(out_refs):
        f = lax.rem(where_ref[0] + s, groups)
        here = pl.ds(pl.multiple_of(f * group_rows, group_rows), group_rows)
        ref[...] = total[here, :].astype(jnp.bfloat16)
    fetch.wait()
    columns = grad.shape[2]
    for n in range(groups):
        here = slice(n * group_rows, (n + 1) * group_rows)
        added = mm(total[here, :].astype(jnp.bfloat16), normed[here, :], TN)
        for f in range(groups):
            part = added[:, f * columns : (f + 1) * columns]
            grad[f] = part if n == 0 else grad[f] + part
    if not earlier:
        grad_ref[...] = grad[...]
        return
    rows = grad_ref.shape[1] // (earlier + 1)
    per_block = grad.shape[1] // rows
    for p in range(grad_ref.shape[0]):
        here = slice(p % per_block * rows, (p % per_block + 1) * rows)
        for m, ref in enumerate(list(done) + [grad]):
            grad_ref[p, m * rows : (m + 1) * rows, :] = ref[p // per_block, here, :]


def scatter_rows(where, need, own, halo, rows, normed, groups, earlier=(), peers=None):
    table_rows = own.shape[0]
    columns = normed.shape[1] // groups
    grad = (groups, PAIR, columns)
    out = grad
    if earlier:
        out = (peers, groups * PAIR // peers * (len(earlier) + 1), columns)
    return pl.pallas_call(
        lambda *refs: scatter_kernel(len(earlier), *refs),
        in_specs=[SMEM, SMEM, VMEM, VMEM, VMEM, ANY] + [VMEM] * len(earlier),
        out_specs=[VMEM] * (1 + groups),
        out_shape=[jax.ShapeDtypeStruct(out, jnp.float32)]
        + [jax.ShapeDtypeStruct((table_rows // groups, PAIR), jnp.bfloat16)] * groups,
        scratch_shapes=[
            pltpu.VMEM((table_rows, PAIR), jnp.float32),
            pltpu.VMEM(normed.shape, jnp.bfloat16),
            pltpu.VMEM(grad, jnp.float32),
            pltpu.SMEM((need.shape[0],), jnp.int32),
            pltpu.SemaphoreType.DMA,
        ],
        compiler_params=room(60),
        cost_estimate=cost(11),
        name="scatter_rows",
    )(where, need, own, halo, rows, normed, *earlier)


def finish_kernel(shares_ref, wq_ref, wk_ref, wv_ref, wo_ref, grads):
    count, total_rows, _ = grads.shape
    heads = count // 2
    rows = shares_ref.shape[1] // count
    for p in range(shares_ref.shape[0]):
        for m in range(count):
            grads[m, p * rows : (p + 1) * rows, :] = shares_ref[p, m * rows : (m + 1) * rows, :]
    for f in range(total_rows // PAIR):
        block = slice(f * PAIR, (f + 1) * PAIR)
        turned = [jnp.transpose(grads[m, block, :]) for m in range(count)]
        for h in range(heads):
            here = slice(h * HEAD, (h + 1) * HEAD)
            wo_ref[here, block] = grads[h, f * PAIR + HEAD : (f + 1) * PAIR, :]
        wq_ref[block, :] = 0.125 * jnp.concatenate([t[:, :HEAD] for t in turned[:heads]], axis=1)
        wk_ref[block, :] = jnp.concatenate([t[:, :HEAD] for t in turned[heads:]], axis=1)
        wv_ref[block, :] = jnp.concatenate([t[:, HEAD:] for t in turned[heads:]], axis=1)


def finish(shares, width, columns):
    tall = jax.ShapeDtypeStruct((width, columns), jnp.float32)
    return pl.pallas_call(
        finish_kernel,
        in_specs=[VMEM],
        out_specs=[VMEM] * 4,
        out_shape=[tall] * 3 + [jax.ShapeDtypeStruct((columns, width), jnp.float32)],
        scratch_shapes=[pltpu.VMEM((2 * columns // HEAD, width, columns), jnp.float32)],
        compiler_params=room(24),
        cost_estimate=cost(2),
        name="finish",
    )(shares)


def grid_kernel(groups, heads, where_ref, weight_ref, feat_ref, gain_ref, *rest):
    parts = rest[: groups * heads]
    out_refs = rest[groups * heads : -1]
    placed = rest[-1]
    me = where_ref[0]
    d_src = None
    for s in range(groups):
        f = lax.rem(me - s + groups, groups)
        for h in range(heads):
            part = mm(parts[s * heads + h][...], weight_ref[f, 0, h])
            d_src = part if d_src is None else d_src + part
    hat, inverse = hat_of(feat_ref[...].astype(jnp.float32))
    result = norm_back(d_src * gain_ref[...], hat, inverse).astype(jnp.bfloat16)
    columns = placed.shape[2]
    for f in range(groups):
        placed[f] = result[:, f * columns : (f + 1) * columns]
    for s, ref in enumerate(out_refs):
        ref[...] = placed[lax.rem(me + s, groups)]


def grid_rows(where, weight, feat, gain, parts):
    groups, heads = len(parts), len(parts[0])
    rows = parts[0][0].shape[0]
    width = feat.shape[1]
    columns = width // groups
    step = 256
    steps = rows // step
    return pl.pallas_call(
        lambda *refs: grid_kernel(groups, heads, *refs),
        grid_spec=pltpu.PrefetchScalarGridSpec(
            num_scalar_prefetch=1,
            grid=(steps,),
            in_specs=[
                pl.BlockSpec((groups, 1, heads, PAIR, width), lambda i, w: (0, 0, 0, 0, 0)),
                pl.BlockSpec((step, width), lambda i, w: (w[0] * steps + i, 0)),
                pl.BlockSpec((1, width), lambda i, w: (0, 0)),
            ]
            + [pl.BlockSpec((step, PAIR), lambda i, w: (i, 0))] * (groups * heads),
            out_specs=[pl.BlockSpec((step, columns), lambda i, w: (i, 0))] * groups,
            scratch_shapes=[pltpu.VMEM((groups, step, columns), jnp.bfloat16)],
        ),
        out_shape=[jax.ShapeDtypeStruct((rows, columns), jnp.bfloat16)] * groups,
        compiler_params=room(60),
        cost_estimate=cost(6),
        name="grid_rows",
    )(where, weight, feat, gain, *[part for row in parts for part in row])


def mesh_kernel(heads, where_ref, weight_ref, feat_ref, cot_ref, gain_ref, *rest):
    parts, (mesh_out_ref, grad_ref, wide) = rest[:heads], rest[heads:]
    groups, columns = weight_ref.shape[0], cot_ref.shape[1]
    mine = pl.ds(pl.multiple_of(where_ref[0] * columns, columns), columns)
    keep_first, keep_second = halves()
    d_dst, added = None, None
    for f in range(groups):
        for h in range(heads):
            part = parts[h][f]
            one = mm(part * keep_first, weight_ref[f, 0, h])
            two = mm(part * keep_second, weight_ref[f, 0, h, :, mine])
            d_dst = one if d_dst is None else d_dst + one
            added = two if added is None else added + two
    feat = feat_ref[...].astype(jnp.float32)
    hat, inverse = hat_of(feat)
    wide[0] = feat
    wide[1] = norm_back(d_dst * 0.125 * gain_ref[...], hat, inverse)
    mesh_out_ref[...] = (wide[0, :, mine] + added).astype(jnp.bfloat16)
    grad_ref[...] = (cot_ref[...].astype(jnp.float32) + wide[1, :, mine]).astype(jnp.bfloat16)


def mesh_rows(where, weight, feat, cot, gain, parts):
    groups, heads = weight.shape[0], len(parts)
    rows, width = feat.shape
    columns = cot.shape[1]
    step = 256
    narrow = pl.BlockSpec((step, columns), lambda i, w: (i, 0))
    return pl.pallas_call(
        lambda *refs: mesh_kernel(heads, *refs),
        grid_spec=pltpu.PrefetchScalarGridSpec(
            num_scalar_prefetch=1,
            grid=(rows // step,),
            in_specs=[
                pl.BlockSpec((groups, 1, heads, PAIR, width), lambda i, w: (0, 1, 0, 0, 0)),
                pl.BlockSpec((step, width), lambda i, w: (i, 0)),
                narrow,
                pl.BlockSpec((1, width), lambda i, w: (0, 0)),
            ]
            + [pl.BlockSpec((groups, step, PAIR), lambda i, w: (0, i, 0))] * heads,
            out_specs=[narrow] * 2,
            scratch_shapes=[pltpu.VMEM((2, step, width), jnp.float32)],
        ),
        out_shape=[jax.ShapeDtypeStruct((rows, columns), jnp.bfloat16)] * 2,
        compiler_params=room(60),
        cost_estimate=cost(11),
        name="mesh_rows",
    )(where, weight, feat, cot, gain, *parts)


def place_kernel(groups, where_ref, *rest):
    parts, out_ref = rest[:groups], rest[groups]
    rows = parts[0].shape[0]
    for s in range(groups):
        f = lax.rem(where_ref[0] - s + groups, groups)
        here = pl.ds(pl.multiple_of(f * rows, rows), rows)
        out_ref[here, :] = parts[s][...]


def place_rows(where, parts):
    groups = len(parts)
    rows, columns = parts[0].shape
    return pl.pallas_call(
        lambda *refs: place_kernel(groups, *refs),
        in_specs=[SMEM] + [VMEM] * groups,
        out_specs=VMEM,
        out_shape=jax.ShapeDtypeStruct((groups * rows, columns), jnp.bfloat16),
        compiler_params=room(24),
        cost_estimate=cost(2),
        name="place_rows",
    )(where, *parts)


def over_graph(values):
    return lax.all_to_all(values, "graph", split_axis=0, concat_axis=0, tiled=True)


def over_feat(parts):
    groups = len(parts)
    return [parts[0]] + [
        lax.ppermute(parts[s], "feat", [(i, (i + s) % groups) for i in range(groups)])
        for s in range(1, groups)
    ]


def after(values, earlier):
    return lax.optimization_barrier((values, earlier))


def by_head(first, second):
    heads = first.shape[0] // HEAD
    parts = [x.reshape(heads, HEAD, -1) for x in (first, second)]
    return jnp.concatenate(parts, axis=1)


def body(
    grid_feat,
    mesh_feat,
    send_rows,
    tile_src,
    edge_mask,
    gain_src,
    gain_dst,
    w_query,
    w_key,
    w_value,
    w_out,
    d_out,
):
    grid_count, width = grid_feat.shape
    columns = w_query.shape[1]
    heads = columns // HEAD
    groups = width // columns
    peers = send_rows.shape[1]
    own_tiles = grid_count // TS
    where = lax.axis_index("feat").astype(jnp.int32).reshape(1)
    gain_src = gain_src.reshape(1, width)
    gain_dst = gain_dst.reshape(1, width)
    rows = send_rows.reshape(2 * peers, 1, TS)

    wanted = own_tiles + jnp.arange(2 * peers, dtype=jnp.int32)
    need = jnp.any(tile_src.reshape(-1, 1) == wanted[None, :], axis=0).astype(jnp.int32)
    need = over_graph(jnp.broadcast_to(need.reshape(peers, 2, 1), (peers, 2, TS)))
    need = need[:, :, 0].reshape(-1)

    cot = lax.all_gather(d_out, "feat", axis=0)
    back_weights = jnp.stack([by_head(w_key.T, w_value.T), by_head(w_query.T, w_out)])
    back_weights = lax.all_gather(back_weights, "feat", axis=0)

    pairs = source_terms(grid_feat, gain_src, w_key, w_value)
    outgoing = gather_rows(need, rows, pairs)
    normed_src = normed_rows(grid_feat, gain_src)
    normed_dst, *targets = target_terms(mesh_feat, gain_dst, w_query, w_out, cot)

    halo = []
    for h in range(heads):
        sent = outgoing[h]
        if h > 0:
            sent, (halo[h - 1], normed_src) = after(sent, (halo[h - 1], normed_src))
        halo.append(over_graph(sent))

    own_grads, returned, mixed, weight_grads = [], [], [], []
    for h in range(heads):
        own_grad, halo_grad, weight_grad, mixed_columns = attention(
            h, tile_src, pairs, halo[h], targets[h], edge_mask, normed_dst, cot
        )
        own_grads.append(own_grad)
        weight_grads.append(weight_grad)
        mixed.append(lax.all_gather(mixed_columns, "feat", axis=0))
        if h == 0:
            halo_grad, (halo[heads - 1], back_weights) = after(
                halo_grad, (halo[heads - 1], back_weights)
            )
        else:
            halo_grad, (returned[h - 1], mixed[h - 1]) = after(
                halo_grad, (returned[h - 1], mixed[h - 1])
            )
        returned.append(over_graph(halo_grad))

    sums = []
    for h in range(heads):
        last = h == heads - 1
        if last:
            returned[h], (sums, weight_grads, mixed) = after(
                returned[h], (sums, weight_grads, mixed)
            )
        weight_grad, *blocks = scatter_rows(
            where,
            need,
            own_grads[h],
            returned[h],
            rows,
            normed_src,
            groups,
            weight_grads if last else (),
            peers,
        )
        weight_grads.append(weight_grad)
        sums.append(over_feat(blocks))

    share = jnp.sum(over_graph(weight_grads[-1]), axis=0)
    sum_rows = [[sums[h][s] for h in range(heads)] for s in range(groups)]
    grid_parts = grid_rows(where, back_weights, grid_feat, gain_src, sum_rows)

    share, (grid_parts, mixed) = after(share, (grid_parts, mixed))
    grad_grid = place_rows(where, over_feat(grid_parts))
    shares = over_graph(jnp.broadcast_to(share[None], weight_grads[-1].shape))
    mesh_out, grad_mesh = mesh_rows(where, back_weights, mesh_feat, d_out, gain_dst, mixed)
    shares, (mesh_out, grad_mesh) = after(shares, (mesh_out, grad_mesh))
    grad_wq, grad_wk, grad_wv, grad_wo = finish(shares, width, columns)
    return (mesh_out, grad_grid, grad_mesh, grad_wq, grad_wk, grad_wv, grad_wo)


def solution(mesh):
    in_specs = (
        P("graph", None),
        P("graph", None),
        P("graph", None, None),
        P("graph", None),
        P("graph", None),
        P(),
        P(),
        P(None, "feat"),
        P(None, "feat"),
        P(None, "feat"),
        P("feat", None),
        P("graph", "feat"),
    )
    out_specs = (
        P("graph", "feat"),
        P("graph", "feat"),
        P("graph", "feat"),
        P(None, "feat"),
        P(None, "feat"),
        P(None, "feat"),
        P("feat", None),
    )
    return jax.shard_map(body, mesh=mesh, in_specs=in_specs, out_specs=out_specs, check_vma=False)
```

```python
import jax
import jax.numpy as jnp
from jax import lax
from jax.experimental import pallas as pl
from jax.experimental.pallas import tpu as pltpu
from jax.sharding import PartitionSpec as P

HEAD = 64
PAIR = 2 * HEAD
TS = 128
TM = 512
QUAD = 4
BIG = 1e30

NT = (((1,), (1,)), ((), ()))
NN = (((1,), (0,)), ((), ()))
TN = (((0,), (0,)), ((), ()))


def mm(a, b, dims=NN):
    return lax.dot_general(a, b, dims, preferred_element_type=jnp.float32)


def room(mib):
    return pltpu.CompilerParams(vmem_limit_bytes=mib * 2**20)


VMEM = pl.BlockSpec(memory_space=pltpu.VMEM)
SMEM = pl.BlockSpec(memory_space=pltpu.SMEM)
ANY = pl.BlockSpec(memory_space=pl.ANY)


def cost(microseconds):
    return pl.CostEstimate(
        flops=int(microseconds * 1.15e9), bytes_accessed=2**20, transcendentals=0
    )


def hat_of(values):
    centre = values - jnp.mean(values, axis=-1, keepdims=True)
    inverse = lax.rsqrt(jnp.mean(centre * centre, axis=-1, keepdims=True) + 1e-05)
    return centre * inverse, inverse


def norm_back(grad, hat, inverse):
    first = jnp.mean(grad, axis=-1, keepdims=True)
    second = jnp.mean(grad * hat, axis=-1, keepdims=True)
    return (grad - first - hat * second) * inverse


def halves():
    first = lax.broadcasted_iota(jnp.int32, (1, PAIR), 1) < HEAD
    return (
        jnp.where(first, 1.0, 0.0).astype(jnp.bfloat16),
        jnp.where(first, 0.0, 1.0).astype(jnp.bfloat16),
    )


def source_kernel(feat_hbm, gain_ref, key_ref, value_ref, pairs_ref, weight, feat, sems):
    i = pl.program_id(0)
    ahead = 2

    def fetch(n):
        step = feat.shape[1]
        here = pl.ds(pl.multiple_of(n * step, step), step)
        return pltpu.make_async_copy(feat_hbm.at[here, :], feat.at[n], sems.at[n])

    @pl.when(i == 0)
    def _():
        for n in range(ahead):
            fetch(n).start()
        for h in range(key_ref.shape[1] // HEAD):
            here = slice(h * HEAD, (h + 1) * HEAD)
            weight[:, h * PAIR : (h + 1) * PAIR] = jnp.concatenate(
                [key_ref[:, here], value_ref[:, here]], axis=1
            )

    @pl.when(i + ahead < feat.shape[0])
    def _():
        fetch(i + ahead).start()

    fetch(i).wait()
    hat, _ = hat_of(feat[i].astype(jnp.float32))
    normed = (hat * gain_ref[...]).astype(jnp.bfloat16)
    pairs_ref[...] = mm(normed, weight[...]).astype(jnp.bfloat16)


def source_terms(feat, gain, w_key, w_value):
    rows, width = feat.shape
    wide = 2 * w_key.shape[1]
    step = 1024
    steps = rows // step
    whole = pl.BlockSpec(w_key.shape, lambda i: (0, 0))
    return pl.pallas_call(
        source_kernel,
        grid=(steps,),
        in_specs=[ANY, pl.BlockSpec((1, width), lambda i: (0, 0)), whole, whole],
        out_specs=pl.BlockSpec((step, wide), lambda i: (i, 0)),
        out_shape=jax.ShapeDtypeStruct((rows, wide), jnp.bfloat16),
        scratch_shapes=[
            pltpu.VMEM((width, wide), jnp.bfloat16),
            pltpu.VMEM((steps, step, width), jnp.bfloat16),
            pltpu.SemaphoreType.DMA((steps,)),
        ],
        compiler_params=room(60),
        cost_estimate=cost(8),
        name="source_terms",
    )(feat, gain, w_key, w_value)


def list_tiles(need_ref, list_ref):
    def add(t, count):
        used = need_ref[t // 2, t % 2, 0] > 0

        @pl.when(used)
        def _():
            list_ref[count] = t

        return count + used.astype(jnp.int32)

    return lax.fori_loop(0, list_ref.shape[0], add, jnp.int32(0))


def gather_kernel(need_ref, rows_ref, table_hbm, *rest):
    out_refs = rest[:-6]
    table_ref, hot, sent, list_ref, sems, table_sem = rest[-6:]
    half = table_ref.shape[1]
    fetch = pltpu.make_async_copy(table_hbm, table_ref, table_sem)
    fetch.start()
    count = list_tiles(need_ref, list_ref)

    def copy(slot, k, h, t):
        return pltpu.make_async_copy(
            sent.at[slot, h, pl.ds(k * TS, TS), :],
            out_refs[h].at[t // 2, pl.ds(pl.multiple_of((t % 2) * TS, TS), TS), :],
            sems.at[slot, k, h],
        )

    def each(step, act):
        for k in range(QUAD):
            place = step * QUAD + k

            @pl.when(jnp.logical_and(place >= 0, place < count))
            def _():
                t = list_ref[jnp.maximum(place, 0)]
                for h in range(len(out_refs)):
                    act(copy(lax.rem(step + 2, 2), k, h, t))

    def quad(step, carry):
        tiles = [list_ref[jnp.minimum(step * QUAD + k, count - 1)] for k in range(QUAD)]
        wanted = jnp.concatenate(
            [jnp.transpose(jnp.broadcast_to(rows_ref[t], (TS, TS))) for t in tiles], axis=0
        )
        upper = wanted >= half
        away = jnp.where(upper, wanted - half, wanted)
        away = away - lax.broadcasted_iota(jnp.int32, (QUAD * TS, TS), 1)
        for c in range(half // TS):
            hot[:, c * TS : (c + 1) * TS] = jnp.where(away == c * TS, 1.0, 0.0).astype(
                jnp.bfloat16
            )
        low = mm(hot[...], table_ref[0])
        high = mm(hot[...], table_ref[1])
        each(step - 2, lambda c: c.wait())
        slot = lax.rem(step, 2)
        for h in range(len(out_refs)):
            here = slice(h * PAIR, (h + 1) * PAIR)
            sent[slot, h] = jnp.where(upper, high[:, here], low[:, here]).astype(jnp.bfloat16)
        each(step, lambda c: c.start())
        return carry

    steps = (count + QUAD - 1) // QUAD
    fetch.wait()
    lax.fori_loop(0, steps, quad, 0)
    each(steps - 2, lambda c: c.wait())
    each(steps - 1, lambda c: c.wait())


def gather_rows(need, rows, pairs):
    count, wide = pairs.shape
    heads = wide // PAIR
    peers = need.shape[0]
    return pl.pallas_call(
        gather_kernel,
        in_specs=[SMEM, VMEM, ANY],
        out_specs=[ANY] * heads,
        out_shape=[jax.ShapeDtypeStruct((peers, 2 * TS, PAIR), jnp.bfloat16)] * heads,
        scratch_shapes=[
            pltpu.VMEM((2, count // 2, wide), jnp.bfloat16),
            pltpu.VMEM((QUAD * TS, count // 2), jnp.bfloat16),
            pltpu.VMEM((2, heads, QUAD * TS, PAIR), jnp.bfloat16),
            pltpu.SMEM((2 * need.shape[0],), jnp.int32),
            pltpu.SemaphoreType.DMA((2, QUAD, heads)),
            pltpu.SemaphoreType.DMA,
        ],
        compiler_params=room(60),
        cost_estimate=cost(10),
        name="gather_rows",
    )(need, rows, pairs.reshape(2, count // 2, wide))


def normed_kernel(feat_ref, gain_ref, normed_ref):
    hat, _ = hat_of(feat_ref[...].astype(jnp.float32))
    normed_ref[...] = (hat * gain_ref[...]).astype(jnp.bfloat16)


def normed_rows(feat, gain):
    rows, width = feat.shape
    step = 512
    return pl.pallas_call(
        normed_kernel,
        grid=(rows // step,),
        in_specs=[
            pl.BlockSpec((step, width), lambda i: (i, 0)),
            pl.BlockSpec((1, width), lambda i: (0, 0)),
        ],
        out_specs=pl.BlockSpec((step, width), lambda i: (i, 0)),
        out_shape=jax.ShapeDtypeStruct((rows, width), jnp.bfloat16),
        compiler_params=room(60),
        cost_estimate=cost(8),
        name="normed_rows",
    )(feat, gain)


def target_kernel(feat_ref, gain_ref, wq_ref, wo_ref, cot_ref, normed_ref, *pairs_refs):
    hat, _ = hat_of(feat_ref[...].astype(jnp.float32))
    normed = (hat * gain_ref[...]).astype(jnp.bfloat16)
    normed_ref[...] = normed
    cot = jnp.concatenate([cot_ref[f] for f in range(cot_ref.shape[0])], axis=1)
    queries = (mm(normed, wq_ref[...]) * 0.125).astype(jnp.bfloat16)
    cots = mm(cot, wo_ref[...], NT).astype(jnp.bfloat16)
    for h, ref in enumerate(pairs_refs):
        here = slice(h * HEAD, (h + 1) * HEAD)
        ref[...] = jnp.concatenate([queries[:, here], cots[:, here]], axis=1)


def target_terms(feat, gain, w_query, w_out, cot):
    rows, width = feat.shape
    groups, _, columns = cot.shape
    heads = columns // HEAD
    step = 512
    return pl.pallas_call(
        target_kernel,
        grid=(rows // step,),
        in_specs=[
            pl.BlockSpec((step, width), lambda i: (i, 0)),
            pl.BlockSpec((1, width), lambda i: (0, 0)),
            pl.BlockSpec(w_query.shape, lambda i: (0, 0)),
            pl.BlockSpec(w_out.shape, lambda i: (0, 0)),
            pl.BlockSpec((groups, step, columns), lambda i: (0, i, 0)),
        ],
        out_specs=[pl.BlockSpec((step, width), lambda i: (i, 0))]
        + [pl.BlockSpec((step, PAIR), lambda i: (i, 0))] * heads,
        out_shape=[jax.ShapeDtypeStruct((rows, width), jnp.bfloat16)]
        + [jax.ShapeDtypeStruct((rows, PAIR), jnp.bfloat16)] * heads,
        compiler_params=room(60),
        cost_estimate=cost(6),
        name="target_terms",
    )(feat, gain, w_query, w_out, cot)


def attention_kernel(
    head,
    tiles_ref,
    own_ref,
    halo_ref,
    pairs_ref,
    valid_ref,
    normed_ref,
    cot_ref,
    own_grad_ref,
    halo_grad_ref,
    weight_grad_ref,
    mixed_ref,
    table,
    bias,
    scores,
    slopes,
    both,
    total,
    sems,
):
    j = pl.program_id(0)
    blocks, tiles = table.shape[0], table.shape[1]
    own_tiles = own_ref.shape[0] // TS

    def fetch(b, k):
        t = tiles_ref[b, k]

        @pl.when(t < own_tiles)
        def _():
            here = pl.ds(pl.multiple_of(t * TS, TS), TS)
            pltpu.make_async_copy(
                own_ref.at[here, pl.ds(head * PAIR, PAIR)], table.at[b, k], sems.at[b, k]
            ).start()

        @pl.when(t >= own_tiles)
        def _():
            o = t - own_tiles
            here = pl.ds(pl.multiple_of((o % 2) * TS, TS), TS)
            pltpu.make_async_copy(
                halo_ref.at[o // 2, here, :], table.at[b, k], sems.at[b, k]
            ).start()

    @pl.when(j == 0)
    def _():
        for b in range(blocks):
            for k in range(tiles):
                fetch(b, k)

        def clear(t, carry):
            total[t] = jnp.zeros(total.shape[1:], jnp.float32)
            return carry

        lax.fori_loop(0, total.shape[0], clear, 0)
        weight_grad_ref[...] = jnp.zeros(weight_grad_ref.shape, jnp.float32)

    for k in range(tiles):
        away = (valid_ref[:, k * TS : (k + 1) * TS] - 1).astype(jnp.float32) * BIG
        bias[k] = jnp.transpose(away)

    for k in range(tiles):
        pltpu.make_async_copy(
            own_ref.at[pl.ds(0, TS), pl.ds(head * PAIR, PAIR)], table.at[j, k], sems.at[j, k]
        ).wait()

    def fold(values, how):
        return how(values.reshape(TS // 8, 8, values.shape[-1]), axis=0)

    keep_first, keep_second = halves()
    pairs = pairs_ref[...]
    queries = pairs * keep_first
    cots = pairs * keep_second
    highest = None
    for k in range(tiles):
        s = mm(table[j, k], queries, NT) + bias[k]
        scores[k] = s
        top = fold(s, jnp.max)
        highest = top if highest is None else jnp.maximum(highest, top)
    highest = jnp.max(highest, axis=0, keepdims=True)
    norm = None
    for k in range(tiles):
        e = jnp.exp(scores[k] - highest)
        scores[k] = e
        part = fold(e, jnp.sum)
        norm = part if norm is None else norm + part
    scale = 1.0 / jnp.sum(norm, axis=0, keepdims=True)
    delta = None
    for k in range(tiles):
        a = scores[k] * scale
        scores[k] = a
        both[k, :, TM:] = a.astype(jnp.bfloat16)
        d = mm(table[j, k], cots, NT)
        slopes[k] = d
        part = fold(a * d, jnp.sum)
        delta = part if delta is None else delta + part
    delta = jnp.sum(delta, axis=0, keepdims=True)
    for k in range(tiles):
        both[k, :, :TM] = (scores[k] * (slopes[k] - delta)).astype(jnp.bfloat16)
    stacked = jnp.concatenate([queries, cots], axis=0)
    for k in range(tiles):
        t = tiles_ref[j, k]
        total[t] = total[t] + mm(both[k], stacked)
    crossed = mm(table[j].reshape(tiles * TS, PAIR), both[...].reshape(tiles * TS, 2 * TM), TN)
    d_query = crossed[:HEAD, :TM]
    attended = crossed[HEAD:, TM:]
    mixed = jnp.concatenate([d_query, attended], axis=0)
    mixed_ref[...] = jnp.transpose(mixed).astype(jnp.bfloat16)
    cot = jnp.concatenate([cot_ref[f] for f in range(cot_ref.shape[0])], axis=1)
    wq_part = mm(d_query.astype(jnp.bfloat16), normed_ref[...])
    wo_part = mm(attended.astype(jnp.bfloat16), cot)
    columns = weight_grad_ref.shape[2]
    for f in range(weight_grad_ref.shape[0]):
        here = slice(f * columns, (f + 1) * columns)
        weight_grad_ref[f, :HEAD] += wq_part[:, here]
        weight_grad_ref[f, HEAD:] += wo_part[:, here]

    @pl.when(j == blocks - 1)
    def _():
        def own(t, carry):
            here = pl.ds(pl.multiple_of(t * TS, TS), TS)
            own_grad_ref[here, :] = total[t].astype(jnp.bfloat16)
            return carry

        lax.fori_loop(0, own_tiles, own, 0)

        def halo(q, carry):
            for half in range(2):
                halo_grad_ref[q, half * TS : (half + 1) * TS, :] = total[
                    own_tiles + 2 * q + half
                ].astype(jnp.bfloat16)
            return carry

        lax.fori_loop(0, halo_grad_ref.shape[0], halo, 0)


def attention(head, tile_src, own, halo, pairs, valid, normed, cot):
    rows, _ = pairs.shape
    blocks, tiles = tile_src.shape
    groups, _, columns = cot.shape
    width = normed.shape[1]
    own_grad = (own.shape[0], PAIR)
    table_tiles = own.shape[0] // TS + 2 * halo.shape[0]
    slots = tiles * TS
    return pl.pallas_call(
        lambda *refs: attention_kernel(head, *refs),
        grid=(blocks,),
        in_specs=[
            SMEM,
            ANY,
            ANY,
            pl.BlockSpec((TM, PAIR), lambda j: (j, 0)),
            pl.BlockSpec((TM, slots), lambda j: (j, 0)),
            pl.BlockSpec((TM, width), lambda j: (j, 0)),
            pl.BlockSpec((groups, TM, columns), lambda j: (0, j, 0)),
        ],
        out_specs=[
            pl.BlockSpec(own_grad, lambda j: (0, 0)),
            pl.BlockSpec(halo.shape, lambda j: (0, 0, 0)),
            pl.BlockSpec((groups, PAIR, columns), lambda j: (0, 0, 0)),
            pl.BlockSpec((TM, PAIR), lambda j: (j, 0)),
        ],
        out_shape=[
            jax.ShapeDtypeStruct(own_grad, jnp.bfloat16),
            jax.ShapeDtypeStruct(halo.shape, jnp.bfloat16),
            jax.ShapeDtypeStruct((groups, PAIR, columns), jnp.float32),
            jax.ShapeDtypeStruct((rows, PAIR), jnp.bfloat16),
        ],
        scratch_shapes=[
            pltpu.VMEM((blocks, tiles, TS, PAIR), jnp.bfloat16),
            pltpu.VMEM((tiles, TS, TM), jnp.float32),
            pltpu.VMEM((tiles, TS, TM), jnp.float32),
            pltpu.VMEM((tiles, TS, TM), jnp.float32),
            pltpu.VMEM((tiles, TS, 2 * TM), jnp.bfloat16),
            pltpu.VMEM((table_tiles, TS, PAIR), jnp.float32),
            pltpu.SemaphoreType.DMA((blocks, tiles)),
        ],
        compiler_params=room(60),
        cost_estimate=cost(18),
        name="attention",
    )(tile_src, own, halo, pairs, valid, normed, cot)


def scatter_kernel(earlier, where_ref, need_ref, own_ref, halo_ref, rows_ref, normed_hbm, *rest):
    *rest, total, normed, grad, list_ref, sem = rest
    done, grad_ref, out_refs = rest[:earlier], rest[earlier], rest[earlier + 1 :]
    table_rows = own_ref.shape[0]
    half = table_rows // 2
    groups = len(out_refs)
    group_rows = table_rows // groups
    chunk = 512
    fetch = pltpu.make_async_copy(normed_hbm, normed, sem)
    fetch.start()
    total[...] = own_ref[...].astype(jnp.float32)
    count = list_tiles(need_ref, list_ref)

    def quad(step, carry):
        spots, parts = [], []
        for k in range(QUAD):
            place = step * QUAD + k
            t = list_ref[jnp.minimum(place, count - 1)]
            spot = jnp.where(place < count, rows_ref[t], -1)
            upper = jnp.transpose(jnp.broadcast_to(spot, (TS, TS))) >= half
            part = halo_ref[t // 2, pl.ds((t % 2) * TS, TS), :]
            keep = jnp.where(upper, 1.0, 0.0).astype(jnp.bfloat16)
            drop = jnp.where(upper, 0.0, 1.0).astype(jnp.bfloat16)
            parts.append(jnp.concatenate([part * drop, part * keep], axis=1))
            spots.append(jnp.where(spot >= half, spot - half, spot))
        spots = jnp.concatenate(spots, axis=1)
        parts = jnp.concatenate(parts, axis=0)
        away = spots - lax.broadcasted_iota(jnp.int32, (chunk, QUAD * TS), 0)
        for c in range(half // chunk):
            hot = jnp.where(away == c * chunk, 1.0, 0.0).astype(jnp.bfloat16)
            added = mm(hot, parts)
            for n in range(2):
                here = slice(n * half + c * chunk, n * half + (c + 1) * chunk)
                total[here, :] = total[here, :] + added[:, n * PAIR : (n + 1) * PAIR]
        return carry

    lax.fori_loop(0, (count + QUAD - 1) // QUAD, quad, 0)
    for s, ref in enumerate(out_refs):
        f = lax.rem(where_ref[0] + s, groups)
        here = pl.ds(pl.multiple_of(f * group_rows, group_rows), group_rows)
        ref[...] = total[here, :].astype(jnp.bfloat16)
    fetch.wait()
    columns = grad.shape[2]
    for n in range(groups):
        here = slice(n * group_rows, (n + 1) * group_rows)
        added = mm(total[here, :].astype(jnp.bfloat16), normed[here, :], TN)
        for f in range(groups):
            part = added[:, f * columns : (f + 1) * columns]
            grad[f] = part if n == 0 else grad[f] + part
    if not earlier:
        grad_ref[...] = grad[...]
        return
    rows = grad_ref.shape[1] // (earlier + 1)
    per_block = grad.shape[1] // rows
    for p in range(grad_ref.shape[0]):
        here = slice(p % per_block * rows, (p % per_block + 1) * rows)
        for m, ref in enumerate(list(done) + [grad]):
            grad_ref[p, m * rows : (m + 1) * rows, :] = ref[p // per_block, here, :]


def scatter_rows(where, need, own, halo, rows, normed, groups, earlier=(), peers=None):
    table_rows = own.shape[0]
    columns = normed.shape[1] // groups
    grad = (groups, PAIR, columns)
    out = grad
    if earlier:
        out = (peers, groups * PAIR // peers * (len(earlier) + 1), columns)
    return pl.pallas_call(
        lambda *refs: scatter_kernel(len(earlier), *refs),
        in_specs=[SMEM, SMEM, VMEM, VMEM, VMEM, ANY] + [VMEM] * len(earlier),
        out_specs=[VMEM] * (1 + groups),
        out_shape=[jax.ShapeDtypeStruct(out, jnp.float32)]
        + [jax.ShapeDtypeStruct((table_rows // groups, PAIR), jnp.bfloat16)] * groups,
        scratch_shapes=[
            pltpu.VMEM((table_rows, PAIR), jnp.float32),
            pltpu.VMEM(normed.shape, jnp.bfloat16),
            pltpu.VMEM(grad, jnp.float32),
            pltpu.SMEM((2 * need.shape[0],), jnp.int32),
            pltpu.SemaphoreType.DMA,
        ],
        compiler_params=room(60),
        cost_estimate=cost(11),
        name="scatter_rows",
    )(where, need, own, halo, rows, normed, *earlier)


def finish_kernel(shares_ref, wq_ref, wk_ref, wv_ref, wo_ref, grads):
    count, total_rows, _ = grads.shape
    heads = count // 2
    rows = shares_ref.shape[1] // count
    for p in range(shares_ref.shape[0]):
        for m in range(count):
            grads[m, p * rows : (p + 1) * rows, :] = shares_ref[p, m * rows : (m + 1) * rows, :]
    for f in range(total_rows // PAIR):
        block = slice(f * PAIR, (f + 1) * PAIR)
        turned = [jnp.transpose(grads[m, block, :]) for m in range(count)]
        for h in range(heads):
            here = slice(h * HEAD, (h + 1) * HEAD)
            wo_ref[here, block] = grads[h, f * PAIR + HEAD : (f + 1) * PAIR, :]
        wq_ref[block, :] = 0.125 * jnp.concatenate([t[:, :HEAD] for t in turned[:heads]], axis=1)
        wk_ref[block, :] = jnp.concatenate([t[:, :HEAD] for t in turned[heads:]], axis=1)
        wv_ref[block, :] = jnp.concatenate([t[:, HEAD:] for t in turned[heads:]], axis=1)


def finish(shares, width, columns):
    tall = jax.ShapeDtypeStruct((width, columns), jnp.float32)
    return pl.pallas_call(
        finish_kernel,
        in_specs=[VMEM],
        out_specs=[VMEM] * 4,
        out_shape=[tall] * 3 + [jax.ShapeDtypeStruct((columns, width), jnp.float32)],
        scratch_shapes=[pltpu.VMEM((2 * columns // HEAD, width, columns), jnp.float32)],
        compiler_params=room(24),
        cost_estimate=cost(2),
        name="finish",
    )(shares)


def grid_kernel(groups, heads, where_ref, weight_ref, feat_ref, gain_ref, *rest):
    parts = rest[: groups * heads]
    out_refs = rest[groups * heads : -1]
    placed = rest[-1]
    me = where_ref[0]
    d_src = None
    for s in range(groups):
        f = lax.rem(me - s + groups, groups)
        for h in range(heads):
            part = mm(parts[s * heads + h][...], weight_ref[f, 0, h])
            d_src = part if d_src is None else d_src + part
    hat, inverse = hat_of(feat_ref[...].astype(jnp.float32))
    result = norm_back(d_src * gain_ref[...], hat, inverse).astype(jnp.bfloat16)
    columns = placed.shape[2]
    for f in range(groups):
        placed[f] = result[:, f * columns : (f + 1) * columns]
    for s, ref in enumerate(out_refs):
        ref[...] = placed[lax.rem(me + s, groups)]


def grid_rows(where, weight, feat, gain, parts):
    groups, heads = len(parts), len(parts[0])
    rows = parts[0][0].shape[0]
    width = feat.shape[1]
    columns = width // groups
    step = 512
    steps = rows // step
    return pl.pallas_call(
        lambda *refs: grid_kernel(groups, heads, *refs),
        grid_spec=pltpu.PrefetchScalarGridSpec(
            num_scalar_prefetch=1,
            grid=(steps,),
            in_specs=[
                pl.BlockSpec((groups, 1, heads, PAIR, width), lambda i, w: (0, 0, 0, 0, 0)),
                pl.BlockSpec((step, width), lambda i, w: (w[0] * steps + i, 0)),
                pl.BlockSpec((1, width), lambda i, w: (0, 0)),
            ]
            + [pl.BlockSpec((step, PAIR), lambda i, w: (i, 0))] * (groups * heads),
            out_specs=[pl.BlockSpec((step, columns), lambda i, w: (i, 0))] * groups,
            scratch_shapes=[pltpu.VMEM((groups, step, columns), jnp.bfloat16)],
        ),
        out_shape=[jax.ShapeDtypeStruct((rows, columns), jnp.bfloat16)] * groups,
        compiler_params=room(60),
        cost_estimate=cost(6),
        name="grid_rows",
    )(where, weight, feat, gain, *[part for row in parts for part in row])


def mesh_kernel(heads, where_ref, weight_ref, feat_ref, cot_ref, gain_ref, *rest):
    parts, (mesh_out_ref, grad_ref, wide) = rest[:heads], rest[heads:]
    groups, columns = weight_ref.shape[0], cot_ref.shape[1]
    mine = pl.ds(pl.multiple_of(where_ref[0] * columns, columns), columns)
    keep_first, keep_second = halves()
    d_dst, added = None, None
    for f in range(groups):
        for h in range(heads):
            part = parts[h][f]
            one = mm(part * keep_first, weight_ref[f, 0, h])
            two = mm(part * keep_second, weight_ref[f, 0, h, :, mine])
            d_dst = one if d_dst is None else d_dst + one
            added = two if added is None else added + two
    feat = feat_ref[...].astype(jnp.float32)
    hat, inverse = hat_of(feat)
    wide[0] = feat
    wide[1] = norm_back(d_dst * 0.125 * gain_ref[...], hat, inverse)
    mesh_out_ref[...] = (wide[0, :, mine] + added).astype(jnp.bfloat16)
    grad_ref[...] = (cot_ref[...].astype(jnp.float32) + wide[1, :, mine]).astype(jnp.bfloat16)


def mesh_rows(where, weight, feat, cot, gain, parts):
    groups, heads = weight.shape[0], len(parts)
    rows, width = feat.shape
    columns = cot.shape[1]
    step = 256
    narrow = pl.BlockSpec((step, columns), lambda i, w: (i, 0))
    return pl.pallas_call(
        lambda *refs: mesh_kernel(heads, *refs),
        grid_spec=pltpu.PrefetchScalarGridSpec(
            num_scalar_prefetch=1,
            grid=(rows // step,),
            in_specs=[
                pl.BlockSpec((groups, 1, heads, PAIR, width), lambda i, w: (0, 1, 0, 0, 0)),
                pl.BlockSpec((step, width), lambda i, w: (i, 0)),
                narrow,
                pl.BlockSpec((1, width), lambda i, w: (0, 0)),
            ]
            + [pl.BlockSpec((groups, step, PAIR), lambda i, w: (0, i, 0))] * heads,
            out_specs=[narrow] * 2,
            scratch_shapes=[pltpu.VMEM((2, step, width), jnp.float32)],
        ),
        out_shape=[jax.ShapeDtypeStruct((rows, columns), jnp.bfloat16)] * 2,
        compiler_params=room(60),
        cost_estimate=cost(11),
        name="mesh_rows",
    )(where, weight, feat, cot, gain, *parts)


def place_kernel(groups, where_ref, *rest):
    parts, out_ref = rest[:groups], rest[groups]
    rows = parts[0].shape[0]
    for s in range(groups):
        f = lax.rem(where_ref[0] - s + groups, groups)
        here = pl.ds(pl.multiple_of(f * rows, rows), rows)
        out_ref[here, :] = parts[s][...]


def place_rows(where, parts):
    groups = len(parts)
    rows, columns = parts[0].shape
    return pl.pallas_call(
        lambda *refs: place_kernel(groups, *refs),
        in_specs=[SMEM] + [VMEM] * groups,
        out_specs=VMEM,
        out_shape=jax.ShapeDtypeStruct((groups * rows, columns), jnp.bfloat16),
        compiler_params=room(24),
        cost_estimate=cost(2),
        name="place_rows",
    )(where, *parts)


def over_graph(values):
    return lax.all_to_all(values, "graph", split_axis=0, concat_axis=0, tiled=True)


def over_feat(parts):
    groups = len(parts)
    return [parts[0]] + [
        lax.ppermute(parts[s], "feat", [(i, (i + s) % groups) for i in range(groups)])
        for s in range(1, groups)
    ]


def after(values, earlier):
    return lax.optimization_barrier((values, earlier))


def by_head(first, second):
    heads = first.shape[0] // HEAD
    parts = [x.reshape(heads, HEAD, -1) for x in (first, second)]
    return jnp.concatenate(parts, axis=1)


def body(
    grid_feat,
    mesh_feat,
    send_rows,
    tile_src,
    edge_mask,
    gain_src,
    gain_dst,
    w_query,
    w_key,
    w_value,
    w_out,
    d_out,
):
    grid_count, width = grid_feat.shape
    columns = w_query.shape[1]
    heads = columns // HEAD
    groups = width // columns
    peers = send_rows.shape[1]
    own_tiles = grid_count // TS
    where = lax.axis_index("feat").astype(jnp.int32).reshape(1)
    gain_src = gain_src.reshape(1, width)
    gain_dst = gain_dst.reshape(1, width)
    rows = send_rows.reshape(2 * peers, 1, TS)

    wanted = own_tiles + jnp.arange(2 * peers, dtype=jnp.int32)
    need = jnp.any(tile_src.reshape(-1, 1) == wanted[None, :], axis=0).astype(jnp.int32)
    need = over_graph(jnp.broadcast_to(need.reshape(peers, 2, 1), (peers, 2, TS)))

    cot = lax.all_gather(d_out, "feat", axis=0)
    back_weights = jnp.stack([by_head(w_key.T, w_value.T), by_head(w_query.T, w_out)])
    back_weights = lax.all_gather(back_weights, "feat", axis=0)

    pairs = source_terms(grid_feat, gain_src, w_key, w_value)
    outgoing = gather_rows(need, rows, pairs)
    normed_src = normed_rows(grid_feat, gain_src)
    normed_dst, *targets = target_terms(mesh_feat, gain_dst, w_query, w_out, cot)

    halo = []
    for h in range(heads):
        sent = outgoing[h]
        if h > 0:
            sent, (halo[h - 1], normed_src) = after(sent, (halo[h - 1], normed_src))
        halo.append(over_graph(sent))

    own_grads, returned, mixed, weight_grads = [], [], [], []
    for h in range(heads):
        own_grad, halo_grad, weight_grad, mixed_columns = attention(
            h, tile_src, pairs, halo[h], targets[h], edge_mask, normed_dst, cot
        )
        own_grads.append(own_grad)
        weight_grads.append(weight_grad)
        mixed.append(lax.all_gather(mixed_columns, "feat", axis=0))
        if h == 0:
            halo_grad, (halo[heads - 1], back_weights) = after(
                halo_grad, (halo[heads - 1], back_weights)
            )
        else:
            halo_grad, (returned[h - 1], mixed[h - 1]) = after(
                halo_grad, (returned[h - 1], mixed[h - 1])
            )
        returned.append(over_graph(halo_grad))

    sums = []
    for h in range(heads):
        last = h == heads - 1
        if last:
            returned[h], (sums, weight_grads, mixed) = after(
                returned[h], (sums, weight_grads, mixed)
            )
        weight_grad, *blocks = scatter_rows(
            where,
            need,
            own_grads[h],
            returned[h],
            rows,
            normed_src,
            groups,
            weight_grads if last else (),
            peers,
        )
        weight_grads.append(weight_grad)
        sums.append(over_feat(blocks))

    mixed, payload = after(mixed, weight_grads[-1])
    mesh_out, grad_mesh = mesh_rows(where, back_weights, mesh_feat, d_out, gain_dst, mixed)
    share = jnp.sum(over_graph(payload), axis=0)
    share, (sums, mesh_out, grad_mesh) = after(share, (sums, mesh_out, grad_mesh))
    shares = over_graph(jnp.broadcast_to(share[None], payload.shape))
    sum_rows = [[sums[h][s] for h in range(heads)] for s in range(groups)]
    grid_parts = grid_rows(where, back_weights, grid_feat, gain_src, sum_rows)
    grad_grid = place_rows(where, over_feat(grid_parts))
    shares, _ = after(shares, grid_parts)
    grad_wq, grad_wk, grad_wv, grad_wo = finish(shares, width, columns)
    return (mesh_out, grad_grid, grad_mesh, grad_wq, grad_wk, grad_wv, grad_wo)


def solution(mesh):
    in_specs = (
        P("graph", None),
        P("graph", None),
        P("graph", None, None),
        P("graph", None),
        P("graph", None),
        P(),
        P(),
        P(None, "feat"),
        P(None, "feat"),
        P(None, "feat"),
        P("feat", None),
        P("graph", "feat"),
    )
    out_specs = (
        P("graph", "feat"),
        P("graph", "feat"),
        P("graph", "feat"),
        P(None, "feat"),
        P(None, "feat"),
        P(None, "feat"),
        P("feat", None),
    )
    return jax.shard_map(body, mesh=mesh, in_specs=in_specs, out_specs=out_specs, check_vma=False)
```

```python
import jax
import jax.numpy as jnp
from jax import lax
from jax.experimental import pallas as pl
from jax.experimental.pallas import tpu as pltpu
from jax.sharding import PartitionSpec as P

HEAD = 64
PAIR = 2 * HEAD
TS = 128
TM = 512
QUAD = 4
BIG = 1e30

NT = (((1,), (1,)), ((), ()))
NN = (((1,), (0,)), ((), ()))
TN = (((0,), (0,)), ((), ()))


def mm(a, b, dims=NN):
    return lax.dot_general(a, b, dims, preferred_element_type=jnp.float32)


def room(mib):
    return pltpu.CompilerParams(vmem_limit_bytes=mib * 2**20)


VMEM = pl.BlockSpec(memory_space=pltpu.VMEM)
SMEM = pl.BlockSpec(memory_space=pltpu.SMEM)
ANY = pl.BlockSpec(memory_space=pl.ANY)


def cost(microseconds):
    return pl.CostEstimate(
        flops=int(microseconds * 1.15e9), bytes_accessed=2**20, transcendentals=0
    )


def hat_of(values):
    centre = values - jnp.mean(values, axis=-1, keepdims=True)
    inverse = lax.rsqrt(jnp.mean(centre * centre, axis=-1, keepdims=True) + 1e-05)
    return centre * inverse, inverse


def norm_back(grad, hat, inverse):
    first = jnp.mean(grad, axis=-1, keepdims=True)
    second = jnp.mean(grad * hat, axis=-1, keepdims=True)
    return (grad - first - hat * second) * inverse


def halves():
    first = lax.broadcasted_iota(jnp.int32, (1, PAIR), 1) < HEAD
    return (
        jnp.where(first, 1.0, 0.0).astype(jnp.bfloat16),
        jnp.where(first, 0.0, 1.0).astype(jnp.bfloat16),
    )


def source_kernel(feat_hbm, gain_ref, key_ref, value_ref, pairs_ref, weight, feat, sems):
    i = pl.program_id(0)
    ahead = 2

    def fetch(n):
        step = feat.shape[1]
        here = pl.ds(pl.multiple_of(n * step, step), step)
        return pltpu.make_async_copy(feat_hbm.at[here, :], feat.at[n], sems.at[n])

    @pl.when(i == 0)
    def _():
        for n in range(ahead):
            fetch(n).start()
        for h in range(key_ref.shape[1] // HEAD):
            here = slice(h * HEAD, (h + 1) * HEAD)
            weight[:, h * PAIR : (h + 1) * PAIR] = jnp.concatenate(
                [key_ref[:, here], value_ref[:, here]], axis=1
            )

    @pl.when(i + ahead < feat.shape[0])
    def _():
        fetch(i + ahead).start()

    fetch(i).wait()
    hat, _ = hat_of(feat[i].astype(jnp.float32))
    normed = (hat * gain_ref[...]).astype(jnp.bfloat16)
    pairs_ref[...] = mm(normed, weight[...]).astype(jnp.bfloat16)


def source_terms(feat, gain, w_key, w_value):
    rows, width = feat.shape
    wide = 2 * w_key.shape[1]
    step = 1024
    steps = rows // step
    whole = pl.BlockSpec(w_key.shape, lambda i: (0, 0))
    return pl.pallas_call(
        source_kernel,
        grid=(steps,),
        in_specs=[ANY, pl.BlockSpec((1, width), lambda i: (0, 0)), whole, whole],
        out_specs=pl.BlockSpec((step, wide), lambda i: (i, 0)),
        out_shape=jax.ShapeDtypeStruct((rows, wide), jnp.bfloat16),
        scratch_shapes=[
            pltpu.VMEM((width, wide), jnp.bfloat16),
            pltpu.VMEM((steps, step, width), jnp.bfloat16),
            pltpu.SemaphoreType.DMA((steps,)),
        ],
        compiler_params=room(60),
        cost_estimate=cost(8),
        name="source_terms",
    )(feat, gain, w_key, w_value)


def list_tiles(need_ref, list_ref):
    def add(t, count):
        used = need_ref[t] > 0

        @pl.when(used)
        def _():
            list_ref[count] = t

        return count + used.astype(jnp.int32)

    return lax.fori_loop(0, list_ref.shape[0], add, jnp.int32(0))


def gather_kernel(need_ref, rows_ref, table_hbm, *rest):
    out_refs = rest[:-6]
    table_ref, hot, sent, list_ref, sems, table_sem = rest[-6:]
    half = table_ref.shape[1]
    fetch = pltpu.make_async_copy(table_hbm, table_ref, table_sem)
    fetch.start()
    count = list_tiles(need_ref, list_ref)

    def copy(slot, k, h, t):
        return pltpu.make_async_copy(
            sent.at[slot, h, pl.ds(k * TS, TS), :],
            out_refs[h].at[t // 2, pl.ds(pl.multiple_of((t % 2) * TS, TS), TS), :],
            sems.at[slot, k, h],
        )

    def each(step, act):
        for k in range(QUAD):
            place = step * QUAD + k

            @pl.when(jnp.logical_and(place >= 0, place < count))
            def _():
                t = list_ref[jnp.maximum(place, 0)]
                for h in range(len(out_refs)):
                    act(copy(lax.rem(step + 2, 2), k, h, t))

    def quad(step, carry):
        tiles = [list_ref[jnp.minimum(step * QUAD + k, count - 1)] for k in range(QUAD)]
        wanted = jnp.concatenate(
            [jnp.transpose(jnp.broadcast_to(rows_ref[t], (TS, TS))) for t in tiles], axis=0
        )
        upper = wanted >= half
        away = jnp.where(upper, wanted - half, wanted)
        away = away - lax.broadcasted_iota(jnp.int32, (QUAD * TS, TS), 1)
        for c in range(half // TS):
            hot[:, c * TS : (c + 1) * TS] = jnp.where(away == c * TS, 1.0, 0.0).astype(
                jnp.bfloat16
            )
        low = mm(hot[...], table_ref[0])
        high = mm(hot[...], table_ref[1])
        each(step - 2, lambda c: c.wait())
        slot = lax.rem(step, 2)
        for h in range(len(out_refs)):
            here = slice(h * PAIR, (h + 1) * PAIR)
            sent[slot, h] = jnp.where(upper, high[:, here], low[:, here]).astype(jnp.bfloat16)
        each(step, lambda c: c.start())
        return carry

    steps = (count + QUAD - 1) // QUAD
    fetch.wait()
    lax.fori_loop(0, steps, quad, 0)
    each(steps - 2, lambda c: c.wait())
    each(steps - 1, lambda c: c.wait())


def gather_rows(need, rows, pairs):
    count, wide = pairs.shape
    heads = wide // PAIR
    peers = need.shape[0] // 2
    return pl.pallas_call(
        gather_kernel,
        in_specs=[SMEM, VMEM, ANY],
        out_specs=[ANY] * heads,
        out_shape=[jax.ShapeDtypeStruct((peers, 2 * TS, PAIR), jnp.bfloat16)] * heads,
        scratch_shapes=[
            pltpu.VMEM((2, count // 2, wide), jnp.bfloat16),
            pltpu.VMEM((QUAD * TS, count // 2), jnp.bfloat16),
            pltpu.VMEM((2, heads, QUAD * TS, PAIR), jnp.bfloat16),
            pltpu.SMEM((need.shape[0],), jnp.int32),
            pltpu.SemaphoreType.DMA((2, QUAD, heads)),
            pltpu.SemaphoreType.DMA,
        ],
        compiler_params=room(60),
        cost_estimate=cost(10),
        name="gather_rows",
    )(need, rows, pairs.reshape(2, count // 2, wide))


def normed_kernel(feat_ref, gain_ref, normed_ref):
    hat, _ = hat_of(feat_ref[...].astype(jnp.float32))
    normed_ref[...] = (hat * gain_ref[...]).astype(jnp.bfloat16)


def normed_rows(feat, gain):
    rows, width = feat.shape
    step = 512
    return pl.pallas_call(
        normed_kernel,
        grid=(rows // step,),
        in_specs=[
            pl.BlockSpec((step, width), lambda i: (i, 0)),
            pl.BlockSpec((1, width), lambda i: (0, 0)),
        ],
        out_specs=pl.BlockSpec((step, width), lambda i: (i, 0)),
        out_shape=jax.ShapeDtypeStruct((rows, width), jnp.bfloat16),
        compiler_params=room(60),
        cost_estimate=cost(8),
        name="normed_rows",
    )(feat, gain)


def target_kernel(feat_ref, gain_ref, wq_ref, wo_ref, cot_ref, normed_ref, *pairs_refs):
    hat, _ = hat_of(feat_ref[...].astype(jnp.float32))
    normed = (hat * gain_ref[...]).astype(jnp.bfloat16)
    normed_ref[...] = normed
    cot = jnp.concatenate([cot_ref[f] for f in range(cot_ref.shape[0])], axis=1)
    queries = (mm(normed, wq_ref[...]) * 0.125).astype(jnp.bfloat16)
    cots = mm(cot, wo_ref[...], NT).astype(jnp.bfloat16)
    for h, ref in enumerate(pairs_refs):
        here = slice(h * HEAD, (h + 1) * HEAD)
        ref[...] = jnp.concatenate([queries[:, here], cots[:, here]], axis=1)


def target_terms(feat, gain, w_query, w_out, cot):
    rows, width = feat.shape
    groups, _, columns = cot.shape
    heads = columns // HEAD
    step = 512
    return pl.pallas_call(
        target_kernel,
        grid=(rows // step,),
        in_specs=[
            pl.BlockSpec((step, width), lambda i: (i, 0)),
            pl.BlockSpec((1, width), lambda i: (0, 0)),
            pl.BlockSpec(w_query.shape, lambda i: (0, 0)),
            pl.BlockSpec(w_out.shape, lambda i: (0, 0)),
            pl.BlockSpec((groups, step, columns), lambda i: (0, i, 0)),
        ],
        out_specs=[pl.BlockSpec((step, width), lambda i: (i, 0))]
        + [pl.BlockSpec((step, PAIR), lambda i: (i, 0))] * heads,
        out_shape=[jax.ShapeDtypeStruct((rows, width), jnp.bfloat16)]
        + [jax.ShapeDtypeStruct((rows, PAIR), jnp.bfloat16)] * heads,
        compiler_params=room(60),
        cost_estimate=cost(6),
        name="target_terms",
    )(feat, gain, w_query, w_out, cot)


def attention_kernel(
    head,
    tiles_ref,
    own_ref,
    halo_ref,
    pairs_ref,
    valid_ref,
    normed_ref,
    cot_ref,
    own_grad_ref,
    halo_grad_ref,
    weight_grad_ref,
    mixed_ref,
    table,
    bias,
    scores,
    slopes,
    both,
    total,
    sems,
):
    j = pl.program_id(0)
    blocks, tiles = table.shape[0], table.shape[1]
    own_tiles = own_ref.shape[0] // TS

    def fetch(b, k):
        t = tiles_ref[b, k]

        @pl.when(t < own_tiles)
        def _():
            here = pl.ds(pl.multiple_of(t * TS, TS), TS)
            pltpu.make_async_copy(
                own_ref.at[here, pl.ds(head * PAIR, PAIR)], table.at[b, k], sems.at[b, k]
            ).start()

        @pl.when(t >= own_tiles)
        def _():
            o = t - own_tiles
            here = pl.ds(pl.multiple_of((o % 2) * TS, TS), TS)
            pltpu.make_async_copy(
                halo_ref.at[o // 2, here, :], table.at[b, k], sems.at[b, k]
            ).start()

    @pl.when(j == 0)
    def _():
        for b in range(blocks):
            for k in range(tiles):
                fetch(b, k)

        def clear(t, carry):
            total[t] = jnp.zeros(total.shape[1:], jnp.float32)
            return carry

        lax.fori_loop(0, total.shape[0], clear, 0)
        weight_grad_ref[...] = jnp.zeros(weight_grad_ref.shape, jnp.float32)

    for k in range(tiles):
        away = (valid_ref[:, k * TS : (k + 1) * TS] - 1).astype(jnp.float32) * BIG
        bias[k] = jnp.transpose(away)

    for k in range(tiles):
        pltpu.make_async_copy(
            own_ref.at[pl.ds(0, TS), pl.ds(head * PAIR, PAIR)], table.at[j, k], sems.at[j, k]
        ).wait()

    def fold(values, how):
        return how(values.reshape(TS // 8, 8, values.shape[-1]), axis=0)

    keep_first, keep_second = halves()
    pairs = pairs_ref[...]
    queries = pairs * keep_first
    cots = pairs * keep_second
    highest = None
    for k in range(tiles):
        s = mm(table[j, k], queries, NT) + bias[k]
        scores[k] = s
        top = fold(s, jnp.max)
        highest = top if highest is None else jnp.maximum(highest, top)
    highest = jnp.max(highest, axis=0, keepdims=True)
    norm = None
    for k in range(tiles):
        e = jnp.exp(scores[k] - highest)
        scores[k] = e
        part = fold(e, jnp.sum)
        norm = part if norm is None else norm + part
    scale = 1.0 / jnp.sum(norm, axis=0, keepdims=True)
    delta = None
    for k in range(tiles):
        a = scores[k] * scale
        scores[k] = a
        both[k, :, TM:] = a.astype(jnp.bfloat16)
        d = mm(table[j, k], cots, NT)
        slopes[k] = d
        part = fold(a * d, jnp.sum)
        delta = part if delta is None else delta + part
    delta = jnp.sum(delta, axis=0, keepdims=True)
    for k in range(tiles):
        both[k, :, :TM] = (scores[k] * (slopes[k] - delta)).astype(jnp.bfloat16)
    stacked = jnp.concatenate([queries, cots], axis=0)
    for k in range(tiles):
        t = tiles_ref[j, k]
        total[t] = total[t] + mm(both[k], stacked)
    crossed = mm(table[j].reshape(tiles * TS, PAIR), both[...].reshape(tiles * TS, 2 * TM), TN)
    d_query = crossed[:HEAD, :TM]
    attended = crossed[HEAD:, TM:]
    mixed = jnp.concatenate([d_query, attended], axis=0)
    mixed_ref[...] = jnp.transpose(mixed).astype(jnp.bfloat16)
    cot = jnp.concatenate([cot_ref[f] for f in range(cot_ref.shape[0])], axis=1)
    wq_part = mm(d_query.astype(jnp.bfloat16), normed_ref[...])
    wo_part = mm(attended.astype(jnp.bfloat16), cot)
    columns = weight_grad_ref.shape[2]
    for f in range(weight_grad_ref.shape[0]):
        here = slice(f * columns, (f + 1) * columns)
        weight_grad_ref[f, :HEAD] += wq_part[:, here]
        weight_grad_ref[f, HEAD:] += wo_part[:, here]

    @pl.when(j == blocks - 1)
    def _():
        def own(t, carry):
            here = pl.ds(pl.multiple_of(t * TS, TS), TS)
            own_grad_ref[here, :] = total[t].astype(jnp.bfloat16)
            return carry

        lax.fori_loop(0, own_tiles, own, 0)

        def halo(q, carry):
            for half in range(2):
                halo_grad_ref[q, half * TS : (half + 1) * TS, :] = total[
                    own_tiles + 2 * q + half
                ].astype(jnp.bfloat16)
            return carry

        lax.fori_loop(0, halo_grad_ref.shape[0], halo, 0)


def attention(head, tile_src, own, halo, pairs, valid, normed, cot):
    rows, _ = pairs.shape
    blocks, tiles = tile_src.shape
    groups, _, columns = cot.shape
    width = normed.shape[1]
    own_grad = (own.shape[0], PAIR)
    table_tiles = own.shape[0] // TS + 2 * halo.shape[0]
    slots = tiles * TS
    return pl.pallas_call(
        lambda *refs: attention_kernel(head, *refs),
        grid=(blocks,),
        in_specs=[
            SMEM,
            ANY,
            ANY,
            pl.BlockSpec((TM, PAIR), lambda j: (j, 0)),
            pl.BlockSpec((TM, slots), lambda j: (j, 0)),
            pl.BlockSpec((TM, width), lambda j: (j, 0)),
            pl.BlockSpec((groups, TM, columns), lambda j: (0, j, 0)),
        ],
        out_specs=[
            pl.BlockSpec(own_grad, lambda j: (0, 0)),
            pl.BlockSpec(halo.shape, lambda j: (0, 0, 0)),
            pl.BlockSpec((groups, PAIR, columns), lambda j: (0, 0, 0)),
            pl.BlockSpec((TM, PAIR), lambda j: (j, 0)),
        ],
        out_shape=[
            jax.ShapeDtypeStruct(own_grad, jnp.bfloat16),
            jax.ShapeDtypeStruct(halo.shape, jnp.bfloat16),
            jax.ShapeDtypeStruct((groups, PAIR, columns), jnp.float32),
            jax.ShapeDtypeStruct((rows, PAIR), jnp.bfloat16),
        ],
        scratch_shapes=[
            pltpu.VMEM((blocks, tiles, TS, PAIR), jnp.bfloat16),
            pltpu.VMEM((tiles, TS, TM), jnp.float32),
            pltpu.VMEM((tiles, TS, TM), jnp.float32),
            pltpu.VMEM((tiles, TS, TM), jnp.float32),
            pltpu.VMEM((tiles, TS, 2 * TM), jnp.bfloat16),
            pltpu.VMEM((table_tiles, TS, PAIR), jnp.float32),
            pltpu.SemaphoreType.DMA((blocks, tiles)),
        ],
        compiler_params=room(60),
        cost_estimate=cost(18),
        name="attention",
    )(tile_src, own, halo, pairs, valid, normed, cot)


def scatter_kernel(earlier, where_ref, need_ref, own_ref, halo_ref, rows_ref, normed_hbm, *rest):
    *rest, total, normed, grad, list_ref, sem = rest
    done, grad_ref, out_refs = rest[:earlier], rest[earlier], rest[earlier + 1 :]
    table_rows = own_ref.shape[0]
    half = table_rows // 2
    groups = len(out_refs)
    group_rows = table_rows // groups
    chunk = 512
    fetch = pltpu.make_async_copy(normed_hbm, normed, sem)
    fetch.start()
    total[...] = own_ref[...].astype(jnp.float32)
    count = list_tiles(need_ref, list_ref)

    def quad(step, carry):
        spots, parts = [], []
        for k in range(QUAD):
            place = step * QUAD + k
            t = list_ref[jnp.minimum(place, count - 1)]
            spot = jnp.where(place < count, rows_ref[t], -1)
            upper = jnp.transpose(jnp.broadcast_to(spot, (TS, TS))) >= half
            part = halo_ref[t // 2, pl.ds((t % 2) * TS, TS), :]
            keep = jnp.where(upper, 1.0, 0.0).astype(jnp.bfloat16)
            drop = jnp.where(upper, 0.0, 1.0).astype(jnp.bfloat16)
            parts.append(jnp.concatenate([part * drop, part * keep], axis=1))
            spots.append(jnp.where(spot >= half, spot - half, spot))
        spots = jnp.concatenate(spots, axis=1)
        parts = jnp.concatenate(parts, axis=0)
        away = spots - lax.broadcasted_iota(jnp.int32, (chunk, QUAD * TS), 0)
        for c in range(half // chunk):
            hot = jnp.where(away == c * chunk, 1.0, 0.0).astype(jnp.bfloat16)
            added = mm(hot, parts)
            for n in range(2):
                here = slice(n * half + c * chunk, n * half + (c + 1) * chunk)
                total[here, :] = total[here, :] + added[:, n * PAIR : (n + 1) * PAIR]
        return carry

    lax.fori_loop(0, (count + QUAD - 1) // QUAD, quad, 0)
    for s, ref in enumerate(out_refs):
        f = lax.rem(where_ref[0] + s, groups)
        here = pl.ds(pl.multiple_of(f * group_rows, group_rows), group_rows)
        ref[...] = total[here, :].astype(jnp.bfloat16)
    fetch.wait()
    columns = grad.shape[2]
    for n in range(groups):
        here = slice(n * group_rows, (n + 1) * group_rows)
        added = mm(total[here, :].astype(jnp.bfloat16), normed[here, :], TN)
        for f in range(groups):
            part = added[:, f * columns : (f + 1) * columns]
            grad[f] = part if n == 0 else grad[f] + part
    if not earlier:
        grad_ref[...] = grad[...]
        return
    rows = grad_ref.shape[1] // (earlier + 1)
    per_block = grad.shape[1] // rows
    for p in range(grad_ref.shape[0]):
        here = slice(p % per_block * rows, (p % per_block + 1) * rows)
        for m, ref in enumerate(list(done) + [grad]):
            grad_ref[p, m * rows : (m + 1) * rows, :] = ref[p // per_block, here, :]


def scatter_rows(where, need, own, halo, rows, normed, groups, earlier=(), peers=None):
    table_rows = own.shape[0]
    columns = normed.shape[1] // groups
    grad = (groups, PAIR, columns)
    out = grad
    if earlier:
        out = (peers, groups * PAIR // peers * (len(earlier) + 1), columns)
    return pl.pallas_call(
        lambda *refs: scatter_kernel(len(earlier), *refs),
        in_specs=[SMEM, SMEM, VMEM, VMEM, VMEM, ANY] + [VMEM] * len(earlier),
        out_specs=[VMEM] * (1 + groups),
        out_shape=[jax.ShapeDtypeStruct(out, jnp.float32)]
        + [jax.ShapeDtypeStruct((table_rows // groups, PAIR), jnp.bfloat16)] * groups,
        scratch_shapes=[
            pltpu.VMEM((table_rows, PAIR), jnp.float32),
            pltpu.VMEM(normed.shape, jnp.bfloat16),
            pltpu.VMEM(grad, jnp.float32),
            pltpu.SMEM((need.shape[0],), jnp.int32),
            pltpu.SemaphoreType.DMA,
        ],
        compiler_params=room(60),
        cost_estimate=cost(11),
        name="scatter_rows",
    )(where, need, own, halo, rows, normed, *earlier)


def finish_kernel(shares_ref, wq_ref, wk_ref, wv_ref, wo_ref, grads):
    count, total_rows, _ = grads.shape
    heads = count // 2
    rows = shares_ref.shape[1] // count
    for p in range(shares_ref.shape[0]):
        for m in range(count):
            grads[m, p * rows : (p + 1) * rows, :] = shares_ref[p, m * rows : (m + 1) * rows, :]
    for f in range(total_rows // PAIR):
        block = slice(f * PAIR, (f + 1) * PAIR)
        turned = [jnp.transpose(grads[m, block, :]) for m in range(count)]
        for h in range(heads):
            here = slice(h * HEAD, (h + 1) * HEAD)
            wo_ref[here, block] = grads[h, f * PAIR + HEAD : (f + 1) * PAIR, :]
        wq_ref[block, :] = 0.125 * jnp.concatenate([t[:, :HEAD] for t in turned[:heads]], axis=1)
        wk_ref[block, :] = jnp.concatenate([t[:, :HEAD] for t in turned[heads:]], axis=1)
        wv_ref[block, :] = jnp.concatenate([t[:, HEAD:] for t in turned[heads:]], axis=1)


def finish(shares, width, columns):
    tall = jax.ShapeDtypeStruct((width, columns), jnp.float32)
    return pl.pallas_call(
        finish_kernel,
        in_specs=[VMEM],
        out_specs=[VMEM] * 4,
        out_shape=[tall] * 3 + [jax.ShapeDtypeStruct((columns, width), jnp.float32)],
        scratch_shapes=[pltpu.VMEM((2 * columns // HEAD, width, columns), jnp.float32)],
        compiler_params=room(24),
        cost_estimate=cost(2),
        name="finish",
    )(shares)


def grid_kernel(groups, heads, where_ref, weight_ref, feat_ref, gain_ref, *rest):
    parts = rest[: groups * heads]
    out_refs = rest[groups * heads : -1]
    placed = rest[-1]
    me = where_ref[0]
    d_src = None
    for s in range(groups):
        f = lax.rem(me - s + groups, groups)
        for h in range(heads):
            part = mm(parts[s * heads + h][...], weight_ref[f, 0, h])
            d_src = part if d_src is None else d_src + part
    hat, inverse = hat_of(feat_ref[...].astype(jnp.float32))
    result = norm_back(d_src * gain_ref[...], hat, inverse).astype(jnp.bfloat16)
    columns = placed.shape[2]
    for f in range(groups):
        placed[f] = result[:, f * columns : (f + 1) * columns]
    for s, ref in enumerate(out_refs):
        ref[...] = placed[lax.rem(me + s, groups)]


def grid_rows(where, weight, feat, gain, parts):
    groups, heads = len(parts), len(parts[0])
    rows = parts[0][0].shape[0]
    width = feat.shape[1]
    columns = width // groups
    step = 512
    steps = rows // step
    return pl.pallas_call(
        lambda *refs: grid_kernel(groups, heads, *refs),
        grid_spec=pltpu.PrefetchScalarGridSpec(
            num_scalar_prefetch=1,
            grid=(steps,),
            in_specs=[
                pl.BlockSpec((groups, 1, heads, PAIR, width), lambda i, w: (0, 0, 0, 0, 0)),
                pl.BlockSpec((step, width), lambda i, w: (w[0] * steps + i, 0)),
                pl.BlockSpec((1, width), lambda i, w: (0, 0)),
            ]
            + [pl.BlockSpec((step, PAIR), lambda i, w: (i, 0))] * (groups * heads),
            out_specs=[pl.BlockSpec((step, columns), lambda i, w: (i, 0))] * groups,
            scratch_shapes=[pltpu.VMEM((groups, step, columns), jnp.bfloat16)],
        ),
        out_shape=[jax.ShapeDtypeStruct((rows, columns), jnp.bfloat16)] * groups,
        compiler_params=room(60),
        cost_estimate=cost(6),
        name="grid_rows",
    )(where, weight, feat, gain, *[part for row in parts for part in row])


def mesh_kernel(heads, where_ref, weight_ref, feat_ref, cot_ref, gain_ref, *rest):
    parts, (mesh_out_ref, grad_ref, wide) = rest[:heads], rest[heads:]
    groups, columns = weight_ref.shape[0], cot_ref.shape[1]
    mine = pl.ds(pl.multiple_of(where_ref[0] * columns, columns), columns)
    keep_first, keep_second = halves()
    d_dst, added = None, None
    for f in range(groups):
        for h in range(heads):
            part = parts[h][f]
            one = mm(part * keep_first, weight_ref[f, 0, h])
            two = mm(part * keep_second, weight_ref[f, 0, h, :, mine])
            d_dst = one if d_dst is None else d_dst + one
            added = two if added is None else added + two
    feat = feat_ref[...].astype(jnp.float32)
    hat, inverse = hat_of(feat)
    wide[0] = feat
    wide[1] = norm_back(d_dst * 0.125 * gain_ref[...], hat, inverse)
    mesh_out_ref[...] = (wide[0, :, mine] + added).astype(jnp.bfloat16)
    grad_ref[...] = (cot_ref[...].astype(jnp.float32) + wide[1, :, mine]).astype(jnp.bfloat16)


def mesh_rows(where, weight, feat, cot, gain, parts):
    groups, heads = weight.shape[0], len(parts)
    rows, width = feat.shape
    columns = cot.shape[1]
    step = 256
    narrow = pl.BlockSpec((step, columns), lambda i, w: (i, 0))
    return pl.pallas_call(
        lambda *refs: mesh_kernel(heads, *refs),
        grid_spec=pltpu.PrefetchScalarGridSpec(
            num_scalar_prefetch=1,
            grid=(rows // step,),
            in_specs=[
                pl.BlockSpec((groups, 1, heads, PAIR, width), lambda i, w: (0, 1, 0, 0, 0)),
                pl.BlockSpec((step, width), lambda i, w: (i, 0)),
                narrow,
                pl.BlockSpec((1, width), lambda i, w: (0, 0)),
            ]
            + [pl.BlockSpec((groups, step, PAIR), lambda i, w: (0, i, 0))] * heads,
            out_specs=[narrow] * 2,
            scratch_shapes=[pltpu.VMEM((2, step, width), jnp.float32)],
        ),
        out_shape=[jax.ShapeDtypeStruct((rows, columns), jnp.bfloat16)] * 2,
        compiler_params=room(60),
        cost_estimate=cost(11),
        name="mesh_rows",
    )(where, weight, feat, cot, gain, *parts)


def place_kernel(groups, where_ref, *rest):
    parts, out_ref = rest[:groups], rest[groups]
    rows = parts[0].shape[0]
    for s in range(groups):
        f = lax.rem(where_ref[0] - s + groups, groups)
        here = pl.ds(pl.multiple_of(f * rows, rows), rows)
        out_ref[here, :] = parts[s][...]


def place_rows(where, parts):
    groups = len(parts)
    rows, columns = parts[0].shape
    return pl.pallas_call(
        lambda *refs: place_kernel(groups, *refs),
        in_specs=[SMEM] + [VMEM] * groups,
        out_specs=VMEM,
        out_shape=jax.ShapeDtypeStruct((groups * rows, columns), jnp.bfloat16),
        compiler_params=room(24),
        cost_estimate=cost(2),
        name="place_rows",
    )(where, *parts)


def over_graph(values):
    return lax.all_to_all(values, "graph", split_axis=0, concat_axis=0, tiled=True)


def over_feat(parts):
    groups = len(parts)
    return [parts[0]] + [
        lax.ppermute(parts[s], "feat", [(i, (i + s) % groups) for i in range(groups)])
        for s in range(1, groups)
    ]


def after(values, earlier):
    return lax.optimization_barrier((values, earlier))


def by_head(first, second):
    heads = first.shape[0] // HEAD
    parts = [x.reshape(heads, HEAD, -1) for x in (first, second)]
    return jnp.concatenate(parts, axis=1)


def body(
    grid_feat,
    mesh_feat,
    send_rows,
    tile_src,
    edge_mask,
    gain_src,
    gain_dst,
    w_query,
    w_key,
    w_value,
    w_out,
    d_out,
):
    grid_count, width = grid_feat.shape
    columns = w_query.shape[1]
    heads = columns // HEAD
    groups = width // columns
    peers = send_rows.shape[1]
    own_tiles = grid_count // TS
    where = lax.axis_index("feat").astype(jnp.int32).reshape(1)
    gain_src = gain_src.reshape(1, width)
    gain_dst = gain_dst.reshape(1, width)
    rows = send_rows.reshape(2 * peers, 1, TS)

    wanted = own_tiles + jnp.arange(2 * peers, dtype=jnp.int32)
    need = jnp.any(tile_src.reshape(-1, 1) == wanted[None, :], axis=0).astype(jnp.int32)
    need = over_graph(jnp.broadcast_to(need.reshape(peers, 2, 1), (peers, 2, TS)))
    need = need[:, :, 0].reshape(-1)

    cot = lax.all_gather(d_out, "feat", axis=0)
    back_weights = jnp.stack([by_head(w_key.T, w_value.T), by_head(w_query.T, w_out)])
    back_weights = lax.all_gather(back_weights, "feat", axis=0)

    pairs = source_terms(grid_feat, gain_src, w_key, w_value)
    outgoing = gather_rows(need, rows, pairs)
    normed_src = normed_rows(grid_feat, gain_src)
    normed_dst, *targets = target_terms(mesh_feat, gain_dst, w_query, w_out, cot)

    halo = []
    for h in range(heads):
        sent = outgoing[h]
        if h > 0:
            sent, (halo[h - 1], normed_src) = after(sent, (halo[h - 1], normed_src))
        halo.append(over_graph(sent))

    own_grads, returned, mixed, weight_grads = [], [], [], []
    for h in range(heads):
        own_grad, halo_grad, weight_grad, mixed_columns = attention(
            h, tile_src, pairs, halo[h], targets[h], edge_mask, normed_dst, cot
        )
        own_grads.append(own_grad)
        weight_grads.append(weight_grad)
        mixed.append(lax.all_gather(mixed_columns, "feat", axis=0))
        if h == 0:
            halo_grad, (halo[heads - 1], back_weights) = after(
                halo_grad, (halo[heads - 1], back_weights)
            )
        else:
            halo_grad, (returned[h - 1], mixed[h - 1]) = after(
                halo_grad, (returned[h - 1], mixed[h - 1])
            )
        returned.append(over_graph(halo_grad))

    sums = []
    for h in range(heads):
        last = h == heads - 1
        if last:
            returned[h], (sums, weight_grads, mixed) = after(
                returned[h], (sums, weight_grads, mixed)
            )
        weight_grad, *blocks = scatter_rows(
            where,
            need,
            own_grads[h],
            returned[h],
            rows,
            normed_src,
            groups,
            weight_grads if last else (),
            peers,
        )
        weight_grads.append(weight_grad)
        sums.append(over_feat(blocks))

    mixed, payload = after(mixed, weight_grads[-1])
    mesh_out, grad_mesh = mesh_rows(where, back_weights, mesh_feat, d_out, gain_dst, mixed)
    sum_rows = [[sums[h][s] for h in range(heads)] for s in range(groups)]
    grid_parts = grid_rows(where, back_weights, grid_feat, gain_src, sum_rows)
    share = jnp.sum(over_graph(payload), axis=0)
    share, (grid_parts, mesh_out, grad_mesh) = after(share, (grid_parts, mesh_out, grad_mesh))
    shares = over_graph(jnp.broadcast_to(share[None], payload.shape))
    grad_grid = place_rows(where, over_feat(grid_parts))
    grad_wq, grad_wk, grad_wv, grad_wo = finish(shares, width, columns)
    return (mesh_out, grad_grid, grad_mesh, grad_wq, grad_wk, grad_wv, grad_wo)


def solution(mesh):
    in_specs = (
        P("graph", None),
        P("graph", None),
        P("graph", None, None),
        P("graph", None),
        P("graph", None),
        P(),
        P(),
        P(None, "feat"),
        P(None, "feat"),
        P(None, "feat"),
        P("feat", None),
        P("graph", "feat"),
    )
    out_specs = (
        P("graph", "feat"),
        P("graph", "feat"),
        P("graph", "feat"),
        P(None, "feat"),
        P(None, "feat"),
        P(None, "feat"),
        P("feat", None),
    )
    return jax.shard_map(body, mesh=mesh, in_specs=in_specs, out_specs=out_specs, check_vma=False)
```

```python
import jax
import jax.numpy as jnp
from jax import lax
from jax.experimental import pallas as pl
from jax.experimental.pallas import tpu as pltpu
from jax.sharding import PartitionSpec as P

HEAD = 64
PAIR = 2 * HEAD
TS = 128
TM = 512
QUAD = 4
BIG = 1e30

NT = (((1,), (1,)), ((), ()))
NN = (((1,), (0,)), ((), ()))
TN = (((0,), (0,)), ((), ()))


def mm(a, b, dims=NN):
    return lax.dot_general(a, b, dims, preferred_element_type=jnp.float32)


def room(mib):
    return pltpu.CompilerParams(vmem_limit_bytes=mib * 2**20)


VMEM = pl.BlockSpec(memory_space=pltpu.VMEM)
SMEM = pl.BlockSpec(memory_space=pltpu.SMEM)
ANY = pl.BlockSpec(memory_space=pl.ANY)


def cost(microseconds):
    return pl.CostEstimate(
        flops=int(microseconds * 1.15e9), bytes_accessed=2**20, transcendentals=0
    )


def hat_of(values):
    centre = values - jnp.mean(values, axis=-1, keepdims=True)
    inverse = lax.rsqrt(jnp.mean(centre * centre, axis=-1, keepdims=True) + 1e-05)
    return centre * inverse, inverse


def norm_back(grad, hat, inverse):
    first = jnp.mean(grad, axis=-1, keepdims=True)
    second = jnp.mean(grad * hat, axis=-1, keepdims=True)
    return (grad - first - hat * second) * inverse


def halves():
    first = lax.broadcasted_iota(jnp.int32, (1, PAIR), 1) < HEAD
    return (
        jnp.where(first, 1.0, 0.0).astype(jnp.bfloat16),
        jnp.where(first, 0.0, 1.0).astype(jnp.bfloat16),
    )


def source_kernel(feat_hbm, gain_ref, key_ref, value_ref, pairs_ref, weight, feat, sems):
    i = pl.program_id(0)
    ahead = 2

    def fetch(n):
        step = feat.shape[1]
        here = pl.ds(pl.multiple_of(n * step, step), step)
        return pltpu.make_async_copy(feat_hbm.at[here, :], feat.at[n], sems.at[n])

    @pl.when(i == 0)
    def _():
        for n in range(ahead):
            fetch(n).start()
        for h in range(key_ref.shape[1] // HEAD):
            here = slice(h * HEAD, (h + 1) * HEAD)
            weight[:, h * PAIR : (h + 1) * PAIR] = jnp.concatenate(
                [key_ref[:, here], value_ref[:, here]], axis=1
            )

    @pl.when(i + ahead < feat.shape[0])
    def _():
        fetch(i + ahead).start()

    fetch(i).wait()
    hat, _ = hat_of(feat[i].astype(jnp.float32))
    normed = (hat * gain_ref[...]).astype(jnp.bfloat16)
    pairs_ref[...] = mm(normed, weight[...]).astype(jnp.bfloat16)


def source_terms(feat, gain, w_key, w_value):
    rows, width = feat.shape
    wide = 2 * w_key.shape[1]
    step = 1024
    steps = rows // step
    whole = pl.BlockSpec(w_key.shape, lambda i: (0, 0))
    return pl.pallas_call(
        source_kernel,
        grid=(steps,),
        in_specs=[ANY, pl.BlockSpec((1, width), lambda i: (0, 0)), whole, whole],
        out_specs=pl.BlockSpec((step, wide), lambda i: (i, 0)),
        out_shape=jax.ShapeDtypeStruct((rows, wide), jnp.bfloat16),
        scratch_shapes=[
            pltpu.VMEM((width, wide), jnp.bfloat16),
            pltpu.VMEM((steps, step, width), jnp.bfloat16),
            pltpu.SemaphoreType.DMA((steps,)),
        ],
        compiler_params=room(60),
        cost_estimate=cost(8),
        name="source_terms",
    )(feat, gain, w_key, w_value)


def list_tiles(need_ref, list_ref):
    def add(t, count):
        used = need_ref[t] > 0

        @pl.when(used)
        def _():
            list_ref[count] = t

        return count + used.astype(jnp.int32)

    return lax.fori_loop(0, list_ref.shape[0], add, jnp.int32(0))


def tile_rows(rows_ref, t):
    both = rows_ref[pl.ds(t // 2, 1), :]
    return jnp.where(t % 2 == 1, both[:, TS:], both[:, :TS])


def gather_kernel(need_ref, rows_ref, table_hbm, *rest):
    out_refs = rest[:-6]
    table_ref, hot, sent, list_ref, sems, table_sem = rest[-6:]
    half = table_ref.shape[1]
    fetch = pltpu.make_async_copy(table_hbm, table_ref, table_sem)
    fetch.start()
    count = list_tiles(need_ref, list_ref)

    def copy(slot, k, h, t):
        return pltpu.make_async_copy(
            sent.at[slot, h, pl.ds(k * TS, TS), :],
            out_refs[h].at[t // 2, pl.ds(pl.multiple_of((t % 2) * TS, TS), TS), :],
            sems.at[slot, k, h],
        )

    def each(step, act):
        for k in range(QUAD):
            place = step * QUAD + k

            @pl.when(jnp.logical_and(place >= 0, place < count))
            def _():
                t = list_ref[jnp.maximum(place, 0)]
                for h in range(len(out_refs)):
                    act(copy(lax.rem(step + 2, 2), k, h, t))

    def quad(step, carry):
        tiles = [list_ref[jnp.minimum(step * QUAD + k, count - 1)] for k in range(QUAD)]
        wanted = jnp.concatenate(
            [jnp.transpose(jnp.broadcast_to(tile_rows(rows_ref, t), (TS, TS))) for t in tiles], axis=0
        )
        upper = wanted >= half
        away = jnp.where(upper, wanted - half, wanted)
        away = away - lax.broadcasted_iota(jnp.int32, (QUAD * TS, TS), 1)
        for c in range(half // TS):
            hot[:, c * TS : (c + 1) * TS] = jnp.where(away == c * TS, 1.0, 0.0).astype(
                jnp.bfloat16
            )
        low = mm(hot[...], table_ref[0])
        high = mm(hot[...], table_ref[1])
        each(step - 2, lambda c: c.wait())
        slot = lax.rem(step, 2)
        for h in range(len(out_refs)):
            here = slice(h * PAIR, (h + 1) * PAIR)
            sent[slot, h] = jnp.where(upper, high[:, here], low[:, here]).astype(jnp.bfloat16)
        each(step, lambda c: c.start())
        return carry

    steps = (count + QUAD - 1) // QUAD
    fetch.wait()
    lax.fori_loop(0, steps, quad, 0)
    each(steps - 2, lambda c: c.wait())
    each(steps - 1, lambda c: c.wait())


def gather_rows(need, rows, pairs):
    count, wide = pairs.shape
    heads = wide // PAIR
    peers = need.shape[0] // 2
    return pl.pallas_call(
        gather_kernel,
        in_specs=[SMEM, VMEM, ANY],
        out_specs=[ANY] * heads,
        out_shape=[jax.ShapeDtypeStruct((peers, 2 * TS, PAIR), jnp.bfloat16)] * heads,
        scratch_shapes=[
            pltpu.VMEM((2, count // 2, wide), jnp.bfloat16),
            pltpu.VMEM((QUAD * TS, count // 2), jnp.bfloat16),
            pltpu.VMEM((2, heads, QUAD * TS, PAIR), jnp.bfloat16),
            pltpu.SMEM((need.shape[0],), jnp.int32),
            pltpu.SemaphoreType.DMA((2, QUAD, heads)),
            pltpu.SemaphoreType.DMA,
        ],
        compiler_params=room(60),
        cost_estimate=cost(10),
        name="gather_rows",
    )(need, rows, pairs.reshape(2, count // 2, wide))


def normed_kernel(feat_ref, gain_ref, normed_ref):
    hat, _ = hat_of(feat_ref[...].astype(jnp.float32))
    normed_ref[...] = (hat * gain_ref[...]).astype(jnp.bfloat16)


def normed_rows(feat, gain):
    rows, width = feat.shape
    step = 512
    return pl.pallas_call(
        normed_kernel,
        grid=(rows // step,),
        in_specs=[
            pl.BlockSpec((step, width), lambda i: (i, 0)),
            pl.BlockSpec((1, width), lambda i: (0, 0)),
        ],
        out_specs=pl.BlockSpec((step, width), lambda i: (i, 0)),
        out_shape=jax.ShapeDtypeStruct((rows, width), jnp.bfloat16),
        compiler_params=room(60),
        cost_estimate=cost(8),
        name="normed_rows",
    )(feat, gain)


def target_kernel(feat_ref, gain_ref, wq_ref, wo_ref, cot_ref, normed_ref, *pairs_refs):
    hat, _ = hat_of(feat_ref[...].astype(jnp.float32))
    normed = (hat * gain_ref[...]).astype(jnp.bfloat16)
    normed_ref[...] = normed
    cot = jnp.concatenate([cot_ref[f] for f in range(cot_ref.shape[0])], axis=1)
    queries = (mm(normed, wq_ref[...]) * 0.125).astype(jnp.bfloat16)
    cots = mm(cot, wo_ref[...], NT).astype(jnp.bfloat16)
    for h, ref in enumerate(pairs_refs):
        here = slice(h * HEAD, (h + 1) * HEAD)
        ref[...] = jnp.concatenate([queries[:, here], cots[:, here]], axis=1)


def target_terms(feat, gain, w_query, w_out, cot):
    rows, width = feat.shape
    groups, _, columns = cot.shape
    heads = columns // HEAD
    step = 512
    return pl.pallas_call(
        target_kernel,
        grid=(rows // step,),
        in_specs=[
            pl.BlockSpec((step, width), lambda i: (i, 0)),
            pl.BlockSpec((1, width), lambda i: (0, 0)),
            pl.BlockSpec(w_query.shape, lambda i: (0, 0)),
            pl.BlockSpec(w_out.shape, lambda i: (0, 0)),
            pl.BlockSpec((groups, step, columns), lambda i: (0, i, 0)),
        ],
        out_specs=[pl.BlockSpec((step, width), lambda i: (i, 0))]
        + [pl.BlockSpec((step, PAIR), lambda i: (i, 0))] * heads,
        out_shape=[jax.ShapeDtypeStruct((rows, width), jnp.bfloat16)]
        + [jax.ShapeDtypeStruct((rows, PAIR), jnp.bfloat16)] * heads,
        compiler_params=room(60),
        cost_estimate=cost(6),
        name="target_terms",
    )(feat, gain, w_query, w_out, cot)


def attention_kernel(
    head,
    tiles_ref,
    own_ref,
    halo_ref,
    pairs_ref,
    valid_ref,
    normed_ref,
    cot_ref,
    own_grad_ref,
    halo_grad_ref,
    weight_grad_ref,
    mixed_ref,
    table,
    bias,
    scores,
    slopes,
    both,
    total,
    sems,
):
    j = pl.program_id(0)
    blocks, tiles = table.shape[0], table.shape[1]
    own_tiles = own_ref.shape[0] // TS

    def fetch(b, k):
        t = tiles_ref[b, k]

        @pl.when(t < own_tiles)
        def _():
            here = pl.ds(pl.multiple_of(t * TS, TS), TS)
            pltpu.make_async_copy(
                own_ref.at[here, pl.ds(head * PAIR, PAIR)], table.at[b, k], sems.at[b, k]
            ).start()

        @pl.when(t >= own_tiles)
        def _():
            o = t - own_tiles
            here = pl.ds(pl.multiple_of((o % 2) * TS, TS), TS)
            pltpu.make_async_copy(
                halo_ref.at[o // 2, here, :], table.at[b, k], sems.at[b, k]
            ).start()

    @pl.when(j == 0)
    def _():
        for b in range(blocks):
            for k in range(tiles):
                fetch(b, k)

        def clear(t, carry):
            total[t] = jnp.zeros(total.shape[1:], jnp.float32)
            return carry

        lax.fori_loop(0, total.shape[0], clear, 0)
        weight_grad_ref[...] = jnp.zeros(weight_grad_ref.shape, jnp.float32)

    for k in range(tiles):
        away = (valid_ref[:, k * TS : (k + 1) * TS] - 1).astype(jnp.float32) * BIG
        bias[k] = jnp.transpose(away)

    for k in range(tiles):
        pltpu.make_async_copy(
            own_ref.at[pl.ds(0, TS), pl.ds(head * PAIR, PAIR)], table.at[j, k], sems.at[j, k]
        ).wait()

    def fold(values, how):
        return how(values.reshape(TS // 8, 8, values.shape[-1]), axis=0)

    keep_first, keep_second = halves()
    pairs = pairs_ref[...]
    queries = pairs * keep_first
    cots = pairs * keep_second
    highest = None
    for k in range(tiles):
        s = mm(table[j, k], queries, NT) + bias[k]
        scores[k] = s
        top = fold(s, jnp.max)
        highest = top if highest is None else jnp.maximum(highest, top)
    highest = jnp.max(highest, axis=0, keepdims=True)
    norm = None
    for k in range(tiles):
        e = jnp.exp(scores[k] - highest)
        scores[k] = e
        part = fold(e, jnp.sum)
        norm = part if norm is None else norm + part
    scale = 1.0 / jnp.sum(norm, axis=0, keepdims=True)
    delta = None
    for k in range(tiles):
        a = scores[k] * scale
        scores[k] = a
        both[k, :, TM:] = a.astype(jnp.bfloat16)
        d = mm(table[j, k], cots, NT)
        slopes[k] = d
        part = fold(a * d, jnp.sum)
        delta = part if delta is None else delta + part
    delta = jnp.sum(delta, axis=0, keepdims=True)
    for k in range(tiles):
        both[k, :, :TM] = (scores[k] * (slopes[k] - delta)).astype(jnp.bfloat16)
    stacked = jnp.concatenate([queries, cots], axis=0)
    for k in range(tiles):
        t = tiles_ref[j, k]
        total[t] = total[t] + mm(both[k], stacked)
    crossed = mm(table[j].reshape(tiles * TS, PAIR), both[...].reshape(tiles * TS, 2 * TM), TN)
    d_query = crossed[:HEAD, :TM]
    attended = crossed[HEAD:, TM:]
    mixed = jnp.concatenate([d_query, attended], axis=0)
    mixed_ref[...] = jnp.transpose(mixed).astype(jnp.bfloat16)
    cot = jnp.concatenate([cot_ref[f] for f in range(cot_ref.shape[0])], axis=1)
    wq_part = mm(d_query.astype(jnp.bfloat16), normed_ref[...])
    wo_part = mm(attended.astype(jnp.bfloat16), cot)
    columns = weight_grad_ref.shape[2]
    for f in range(weight_grad_ref.shape[0]):
        here = slice(f * columns, (f + 1) * columns)
        weight_grad_ref[f, :HEAD] += wq_part[:, here]
        weight_grad_ref[f, HEAD:] += wo_part[:, here]

    @pl.when(j == blocks - 1)
    def _():
        def own(t, carry):
            here = pl.ds(pl.multiple_of(t * TS, TS), TS)
            own_grad_ref[here, :] = total[t].astype(jnp.bfloat16)
            return carry

        lax.fori_loop(0, own_tiles, own, 0)

        def halo(q, carry):
            for half in range(2):
                halo_grad_ref[q, half * TS : (half + 1) * TS, :] = total[
                    own_tiles + 2 * q + half
                ].astype(jnp.bfloat16)
            return carry

        lax.fori_loop(0, halo_grad_ref.shape[0], halo, 0)


def attention(head, tile_src, own, halo, pairs, valid, normed, cot):
    rows, _ = pairs.shape
    blocks, tiles = tile_src.shape
    groups, _, columns = cot.shape
    width = normed.shape[1]
    own_grad = (own.shape[0], PAIR)
    table_tiles = own.shape[0] // TS + 2 * halo.shape[0]
    slots = tiles * TS
    return pl.pallas_call(
        lambda *refs: attention_kernel(head, *refs),
        grid=(blocks,),
        in_specs=[
            SMEM,
            ANY,
            ANY,
            pl.BlockSpec((TM, PAIR), lambda j: (j, 0)),
            pl.BlockSpec((TM, slots), lambda j: (j, 0)),
            pl.BlockSpec((TM, width), lambda j: (j, 0)),
            pl.BlockSpec((groups, TM, columns), lambda j: (0, j, 0)),
        ],
        out_specs=[
            pl.BlockSpec(own_grad, lambda j: (0, 0)),
            pl.BlockSpec(halo.shape, lambda j: (0, 0, 0)),
            pl.BlockSpec((groups, PAIR, columns), lambda j: (0, 0, 0)),
            pl.BlockSpec((TM, PAIR), lambda j: (j, 0)),
        ],
        out_shape=[
            jax.ShapeDtypeStruct(own_grad, jnp.bfloat16),
            jax.ShapeDtypeStruct(halo.shape, jnp.bfloat16),
            jax.ShapeDtypeStruct((groups, PAIR, columns), jnp.float32),
            jax.ShapeDtypeStruct((rows, PAIR), jnp.bfloat16),
        ],
        scratch_shapes=[
            pltpu.VMEM((blocks, tiles, TS, PAIR), jnp.bfloat16),
            pltpu.VMEM((tiles, TS, TM), jnp.float32),
            pltpu.VMEM((tiles, TS, TM), jnp.float32),
            pltpu.VMEM((tiles, TS, TM), jnp.float32),
            pltpu.VMEM((tiles, TS, 2 * TM), jnp.bfloat16),
            pltpu.VMEM((table_tiles, TS, PAIR), jnp.float32),
            pltpu.SemaphoreType.DMA((blocks, tiles)),
        ],
        compiler_params=room(60),
        cost_estimate=cost(18),
        name="attention",
    )(tile_src, own, halo, pairs, valid, normed, cot)


def scatter_kernel(earlier, where_ref, need_ref, own_ref, halo_ref, rows_ref, normed_hbm, *rest):
    *rest, total, normed, grad, list_ref, sem = rest
    done, grad_ref, out_refs = rest[:earlier], rest[earlier], rest[earlier + 1 :]
    table_rows = own_ref.shape[0]
    half = table_rows // 2
    groups = len(out_refs)
    group_rows = table_rows // groups
    chunk = 512
    fetch = pltpu.make_async_copy(normed_hbm, normed, sem)
    fetch.start()
    total[...] = own_ref[...].astype(jnp.float32)
    count = list_tiles(need_ref, list_ref)

    def quad(step, carry):
        spots, parts = [], []
        for k in range(QUAD):
            place = step * QUAD + k
            t = list_ref[jnp.minimum(place, count - 1)]
            spot = jnp.where(place < count, tile_rows(rows_ref, t), -1)
            upper = jnp.transpose(jnp.broadcast_to(spot, (TS, TS))) >= half
            part = halo_ref[t // 2, pl.ds((t % 2) * TS, TS), :]
            keep = jnp.where(upper, 1.0, 0.0).astype(jnp.bfloat16)
            drop = jnp.where(upper, 0.0, 1.0).astype(jnp.bfloat16)
            parts.append(jnp.concatenate([part * drop, part * keep], axis=1))
            spots.append(jnp.where(spot >= half, spot - half, spot))
        spots = jnp.concatenate(spots, axis=1)
        parts = jnp.concatenate(parts, axis=0)
        away = spots - lax.broadcasted_iota(jnp.int32, (chunk, QUAD * TS), 0)
        for c in range(half // chunk):
            hot = jnp.where(away == c * chunk, 1.0, 0.0).astype(jnp.bfloat16)
            added = mm(hot, parts)
            for n in range(2):
                here = slice(n * half + c * chunk, n * half + (c + 1) * chunk)
                total[here, :] = total[here, :] + added[:, n * PAIR : (n + 1) * PAIR]
        return carry

    lax.fori_loop(0, (count + QUAD - 1) // QUAD, quad, 0)
    for s, ref in enumerate(out_refs):
        f = lax.rem(where_ref[0] + s, groups)
        here = pl.ds(pl.multiple_of(f * group_rows, group_rows), group_rows)
        ref[...] = total[here, :].astype(jnp.bfloat16)
    fetch.wait()
    columns = grad.shape[2]
    for n in range(groups):
        here = slice(n * group_rows, (n + 1) * group_rows)
        added = mm(total[here, :].astype(jnp.bfloat16), normed[here, :], TN)
        for f in range(groups):
            part = added[:, f * columns : (f + 1) * columns]
            grad[f] = part if n == 0 else grad[f] + part
    if not earlier:
        grad_ref[...] = grad[...]
        return
    rows = grad_ref.shape[1] // (earlier + 1)
    per_block = grad.shape[1] // rows
    for p in range(grad_ref.shape[0]):
        here = slice(p % per_block * rows, (p % per_block + 1) * rows)
        for m, ref in enumerate(list(done) + [grad]):
            grad_ref[p, m * rows : (m + 1) * rows, :] = ref[p // per_block, here, :]


def scatter_rows(where, need, own, halo, rows, normed, groups, earlier=(), peers=None):
    table_rows = own.shape[0]
    columns = normed.shape[1] // groups
    grad = (groups, PAIR, columns)
    out = grad
    if earlier:
        out = (peers, groups * PAIR // peers * (len(earlier) + 1), columns)
    return pl.pallas_call(
        lambda *refs: scatter_kernel(len(earlier), *refs),
        in_specs=[SMEM, SMEM, VMEM, VMEM, VMEM, ANY] + [VMEM] * len(earlier),
        out_specs=[VMEM] * (1 + groups),
        out_shape=[jax.ShapeDtypeStruct(out, jnp.float32)]
        + [jax.ShapeDtypeStruct((table_rows // groups, PAIR), jnp.bfloat16)] * groups,
        scratch_shapes=[
            pltpu.VMEM((table_rows, PAIR), jnp.float32),
            pltpu.VMEM(normed.shape, jnp.bfloat16),
            pltpu.VMEM(grad, jnp.float32),
            pltpu.SMEM((need.shape[0],), jnp.int32),
            pltpu.SemaphoreType.DMA,
        ],
        compiler_params=room(60),
        cost_estimate=cost(11),
        name="scatter_rows",
    )(where, need, own, halo, rows, normed, *earlier)


def finish_kernel(shares_ref, wq_ref, wk_ref, wv_ref, wo_ref, grads):
    count, total_rows, _ = grads.shape
    heads = count // 2
    rows = shares_ref.shape[1] // count
    for p in range(shares_ref.shape[0]):
        for m in range(count):
            grads[m, p * rows : (p + 1) * rows, :] = shares_ref[p, m * rows : (m + 1) * rows, :]
    for f in range(total_rows // PAIR):
        block = slice(f * PAIR, (f + 1) * PAIR)
        turned = [jnp.transpose(grads[m, block, :]) for m in range(count)]
        for h in range(heads):
            here = slice(h * HEAD, (h + 1) * HEAD)
            wo_ref[here, block] = grads[h, f * PAIR + HEAD : (f + 1) * PAIR, :]
        wq_ref[block, :] = 0.125 * jnp.concatenate([t[:, :HEAD] for t in turned[:heads]], axis=1)
        wk_ref[block, :] = jnp.concatenate([t[:, :HEAD] for t in turned[heads:]], axis=1)
        wv_ref[block, :] = jnp.concatenate([t[:, HEAD:] for t in turned[heads:]], axis=1)


def finish(shares, width, columns):
    tall = jax.ShapeDtypeStruct((width, columns), jnp.float32)
    return pl.pallas_call(
        finish_kernel,
        in_specs=[VMEM],
        out_specs=[VMEM] * 4,
        out_shape=[tall] * 3 + [jax.ShapeDtypeStruct((columns, width), jnp.float32)],
        scratch_shapes=[pltpu.VMEM((2 * columns // HEAD, width, columns), jnp.float32)],
        compiler_params=room(24),
        cost_estimate=cost(2),
        name="finish",
    )(shares)


def grid_kernel(groups, heads, where_ref, weight_ref, feat_ref, gain_ref, *rest):
    parts = rest[: groups * heads]
    out_refs = rest[groups * heads : -1]
    placed = rest[-1]
    me = where_ref[0]
    d_src = None
    for s in range(groups):
        f = lax.rem(me - s + groups, groups)
        for h in range(heads):
            part = mm(parts[s * heads + h][...], weight_ref[f, 0, h])
            d_src = part if d_src is None else d_src + part
    hat, inverse = hat_of(feat_ref[...].astype(jnp.float32))
    result = norm_back(d_src * gain_ref[...], hat, inverse).astype(jnp.bfloat16)
    columns = placed.shape[2]
    for f in range(groups):
        placed[f] = result[:, f * columns : (f + 1) * columns]
    for s, ref in enumerate(out_refs):
        ref[...] = placed[lax.rem(me + s, groups)]


def grid_rows(where, weight, feat, gain, parts):
    groups, heads = len(parts), len(parts[0])
    rows = parts[0][0].shape[0]
    width = feat.shape[1]
    columns = width // groups
    step = 512
    steps = rows // step
    return pl.pallas_call(
        lambda *refs: grid_kernel(groups, heads, *refs),
        grid_spec=pltpu.PrefetchScalarGridSpec(
            num_scalar_prefetch=1,
            grid=(steps,),
            in_specs=[
                pl.BlockSpec((groups, 1, heads, PAIR, width), lambda i, w: (0, 0, 0, 0, 0)),
                pl.BlockSpec((step, width), lambda i, w: (w[0] * steps + i, 0)),
                pl.BlockSpec((1, width), lambda i, w: (0, 0)),
            ]
            + [pl.BlockSpec((step, PAIR), lambda i, w: (i, 0))] * (groups * heads),
            out_specs=[pl.BlockSpec((step, columns), lambda i, w: (i, 0))] * groups,
            scratch_shapes=[pltpu.VMEM((groups, step, columns), jnp.bfloat16)],
        ),
        out_shape=[jax.ShapeDtypeStruct((rows, columns), jnp.bfloat16)] * groups,
        compiler_params=room(60),
        cost_estimate=cost(6),
        name="grid_rows",
    )(where, weight, feat, gain, *[part for row in parts for part in row])


def mesh_kernel(heads, where_ref, weight_ref, feat_ref, cot_ref, gain_ref, *rest):
    parts, (mesh_out_ref, grad_ref, wide) = rest[:heads], rest[heads:]
    groups, columns = weight_ref.shape[0], cot_ref.shape[1]
    mine = pl.ds(pl.multiple_of(where_ref[0] * columns, columns), columns)
    keep_first, keep_second = halves()
    d_dst, added = None, None
    for f in range(groups):
        for h in range(heads):
            part = parts[h][f]
            one = mm(part * keep_first, weight_ref[f, 0, h])
            two = mm(part * keep_second, weight_ref[f, 0, h, :, mine])
            d_dst = one if d_dst is None else d_dst + one
            added = two if added is None else added + two
    feat = feat_ref[...].astype(jnp.float32)
    hat, inverse = hat_of(feat)
    wide[0] = feat
    wide[1] = norm_back(d_dst * 0.125 * gain_ref[...], hat, inverse)
    mesh_out_ref[...] = (wide[0, :, mine] + added).astype(jnp.bfloat16)
    grad_ref[...] = (cot_ref[...].astype(jnp.float32) + wide[1, :, mine]).astype(jnp.bfloat16)


def mesh_rows(where, weight, feat, cot, gain, parts):
    groups, heads = weight.shape[0], len(parts)
    rows, width = feat.shape
    columns = cot.shape[1]
    step = 256
    narrow = pl.BlockSpec((step, columns), lambda i, w: (i, 0))
    return pl.pallas_call(
        lambda *refs: mesh_kernel(heads, *refs),
        grid_spec=pltpu.PrefetchScalarGridSpec(
            num_scalar_prefetch=1,
            grid=(rows // step,),
            in_specs=[
                pl.BlockSpec((groups, 1, heads, PAIR, width), lambda i, w: (0, 1, 0, 0, 0)),
                pl.BlockSpec((step, width), lambda i, w: (i, 0)),
                narrow,
                pl.BlockSpec((1, width), lambda i, w: (0, 0)),
            ]
            + [pl.BlockSpec((groups, step, PAIR), lambda i, w: (0, i, 0))] * heads,
            out_specs=[narrow] * 2,
            scratch_shapes=[pltpu.VMEM((2, step, width), jnp.float32)],
        ),
        out_shape=[jax.ShapeDtypeStruct((rows, columns), jnp.bfloat16)] * 2,
        compiler_params=room(60),
        cost_estimate=cost(11),
        name="mesh_rows",
    )(where, weight, feat, cot, gain, *parts)


def place_kernel(groups, where_ref, *rest):
    parts, out_ref = rest[:groups], rest[groups]
    rows = parts[0].shape[0]
    for s in range(groups):
        f = lax.rem(where_ref[0] - s + groups, groups)
        here = pl.ds(pl.multiple_of(f * rows, rows), rows)
        out_ref[here, :] = parts[s][...]


def place_rows(where, parts):
    groups = len(parts)
    rows, columns = parts[0].shape
    return pl.pallas_call(
        lambda *refs: place_kernel(groups, *refs),
        in_specs=[SMEM] + [VMEM] * groups,
        out_specs=VMEM,
        out_shape=jax.ShapeDtypeStruct((groups * rows, columns), jnp.bfloat16),
        compiler_params=room(24),
        cost_estimate=cost(2),
        name="place_rows",
    )(where, *parts)


def over_graph(values):
    return lax.all_to_all(values, "graph", split_axis=0, concat_axis=0, tiled=True)


def over_feat(parts):
    groups = len(parts)
    return [parts[0]] + [
        lax.ppermute(parts[s], "feat", [(i, (i + s) % groups) for i in range(groups)])
        for s in range(1, groups)
    ]


def after(values, earlier):
    return lax.optimization_barrier((values, earlier))


def corner(values):
    return values[:1, :16, :]


def by_head(first, second):
    heads = first.shape[0] // HEAD
    parts = [x.reshape(heads, HEAD, -1) for x in (first, second)]
    return jnp.concatenate(parts, axis=1)


def body(
    grid_feat,
    mesh_feat,
    send_rows,
    tile_src,
    edge_mask,
    gain_src,
    gain_dst,
    w_query,
    w_key,
    w_value,
    w_out,
    d_out,
):
    grid_count, width = grid_feat.shape
    columns = w_query.shape[1]
    heads = columns // HEAD
    groups = width // columns
    peers = send_rows.shape[1]
    own_tiles = grid_count // TS
    where = lax.axis_index("feat").astype(jnp.int32).reshape(1)
    gain_src = gain_src.reshape(1, width)
    gain_dst = gain_dst.reshape(1, width)
    rows = send_rows.reshape(peers, 2 * TS)

    wanted = own_tiles + jnp.arange(2 * peers, dtype=jnp.int32)
    need = jnp.any(tile_src.reshape(-1, 1) == wanted[None, :], axis=0).astype(jnp.int32)
    need = over_graph(jnp.broadcast_to(need.reshape(peers, 2, 1), (peers, 2, TS)))
    need = need[:, :, 0].reshape(-1)

    cot = lax.all_gather(d_out, "feat", axis=0)
    back_weights = jnp.stack([by_head(w_key.T, w_value.T), by_head(w_query.T, w_out)])
    back_weights = lax.all_gather(back_weights, "feat", axis=0)

    pairs = source_terms(grid_feat, gain_src, w_key, w_value)
    outgoing = gather_rows(need, rows, pairs)
    normed_src = normed_rows(grid_feat, gain_src)
    normed_dst, *targets = target_terms(mesh_feat, gain_dst, w_query, w_out, cot)

    halo = []
    for h in range(heads):
        sent = outgoing[h]
        if h > 0:
            sent, (_, normed_src) = after(sent, (corner(halo[h - 1]), normed_src))
        halo.append(over_graph(sent))

    own_grads, returned, mixed, weight_grads = [], [], [], []
    for h in range(heads):
        own_grad, halo_grad, weight_grad, mixed_columns = attention(
            h, tile_src, pairs, halo[h], targets[h], edge_mask, normed_dst, cot
        )
        own_grads.append(own_grad)
        weight_grads.append(weight_grad)
        mixed.append(lax.all_gather(mixed_columns, "feat", axis=0))
        if h == 0:
            halo_grad, (halo[heads - 1], back_weights) = after(
                halo_grad, (halo[heads - 1], back_weights)
            )
        else:
            halo_grad, (_, mixed[h - 1]) = after(
                halo_grad, (corner(returned[h - 1]), mixed[h - 1])
            )
        returned.append(over_graph(halo_grad))

    sums = []
    for h in range(heads):
        last = h == heads - 1
        if last:
            returned[h], (sums, weight_grads, mixed) = after(
                returned[h], (sums, weight_grads, mixed)
            )
        weight_grad, *blocks = scatter_rows(
            where,
            need,
            own_grads[h],
            returned[h],
            rows,
            normed_src,
            groups,
            weight_grads if last else (),
            peers,
        )
        weight_grads.append(weight_grad)
        sums.append(over_feat(blocks))

    mixed, payload = after(mixed, weight_grads[-1])
    mesh_out, grad_mesh = mesh_rows(where, back_weights, mesh_feat, d_out, gain_dst, mixed)
    sum_rows = [[sums[h][s] for h in range(heads)] for s in range(groups)]
    grid_parts = grid_rows(where, back_weights, grid_feat, gain_src, sum_rows)
    share = jnp.sum(over_graph(payload), axis=0)
    share, (grid_parts, mesh_out, grad_mesh) = after(share, (grid_parts, mesh_out, grad_mesh))
    shares = over_graph(jnp.broadcast_to(share[None], payload.shape))
    grad_grid = place_rows(where, over_feat(grid_parts))
    grad_wq, grad_wk, grad_wv, grad_wo = finish(shares, width, columns)
    return (mesh_out, grad_grid, grad_mesh, grad_wq, grad_wk, grad_wv, grad_wo)


def solution(mesh):
    in_specs = (
        P("graph", None),
        P("graph", None),
        P("graph", None, None),
        P("graph", None),
        P("graph", None),
        P(),
        P(),
        P(None, "feat"),
        P(None, "feat"),
        P(None, "feat"),
        P("feat", None),
        P("graph", "feat"),
    )
    out_specs = (
        P("graph", "feat"),
        P("graph", "feat"),
        P("graph", "feat"),
        P(None, "feat"),
        P(None, "feat"),
        P(None, "feat"),
        P("feat", None),
    )
    return jax.shard_map(body, mesh=mesh, in_specs=in_specs, out_specs=out_specs, check_vma=False)
```

```python
import jax
import jax.numpy as jnp
from jax import lax
from jax.experimental import pallas as pl
from jax.experimental.pallas import tpu as pltpu
from jax.sharding import PartitionSpec as P

HEAD = 64
PAIR = 2 * HEAD
TS = 128
TM = 512
QUAD = 4
BIG = 1e30

NT = (((1,), (1,)), ((), ()))
NN = (((1,), (0,)), ((), ()))
TN = (((0,), (0,)), ((), ()))


def mm(a, b, dims=NN):
    return lax.dot_general(a, b, dims, preferred_element_type=jnp.float32)


def room(mib):
    return pltpu.CompilerParams(vmem_limit_bytes=mib * 2**20)


VMEM = pl.BlockSpec(memory_space=pltpu.VMEM)
SMEM = pl.BlockSpec(memory_space=pltpu.SMEM)
ANY = pl.BlockSpec(memory_space=pl.ANY)


def cost(microseconds):
    return pl.CostEstimate(
        flops=int(microseconds * 1.15e9), bytes_accessed=2**20, transcendentals=0
    )


def hat_of(values):
    centre = values - jnp.mean(values, axis=-1, keepdims=True)
    inverse = lax.rsqrt(jnp.mean(centre * centre, axis=-1, keepdims=True) + 1e-05)
    return centre * inverse, inverse


def norm_back(grad, hat, inverse):
    first = jnp.mean(grad, axis=-1, keepdims=True)
    second = jnp.mean(grad * hat, axis=-1, keepdims=True)
    return (grad - first - hat * second) * inverse


def halves():
    first = lax.broadcasted_iota(jnp.int32, (1, PAIR), 1) < HEAD
    return (
        jnp.where(first, 1.0, 0.0).astype(jnp.bfloat16),
        jnp.where(first, 0.0, 1.0).astype(jnp.bfloat16),
    )


def source_kernel(feat_hbm, gain_ref, key_ref, value_ref, pairs_ref, weight, feat, sems):
    i = pl.program_id(0)
    ahead = 2

    def fetch(n):
        step = feat.shape[1]
        here = pl.ds(pl.multiple_of(n * step, step), step)
        return pltpu.make_async_copy(feat_hbm.at[here, :], feat.at[n], sems.at[n])

    @pl.when(i == 0)
    def _():
        for n in range(ahead):
            fetch(n).start()
        for h in range(key_ref.shape[1] // HEAD):
            here = slice(h * HEAD, (h + 1) * HEAD)
            weight[:, h * PAIR : (h + 1) * PAIR] = jnp.concatenate(
                [key_ref[:, here], value_ref[:, here]], axis=1
            )

    @pl.when(i + ahead < feat.shape[0])
    def _():
        fetch(i + ahead).start()

    fetch(i).wait()
    hat, _ = hat_of(feat[i].astype(jnp.float32))
    normed = (hat * gain_ref[...]).astype(jnp.bfloat16)
    pairs_ref[...] = mm(normed, weight[...]).astype(jnp.bfloat16)


def source_terms(feat, gain, w_key, w_value):
    rows, width = feat.shape
    wide = 2 * w_key.shape[1]
    step = 1024
    steps = rows // step
    whole = pl.BlockSpec(w_key.shape, lambda i: (0, 0))
    return pl.pallas_call(
        source_kernel,
        grid=(steps,),
        in_specs=[ANY, pl.BlockSpec((1, width), lambda i: (0, 0)), whole, whole],
        out_specs=pl.BlockSpec((step, wide), lambda i: (i, 0)),
        out_shape=jax.ShapeDtypeStruct((rows, wide), jnp.bfloat16),
        scratch_shapes=[
            pltpu.VMEM((width, wide), jnp.bfloat16),
            pltpu.VMEM((steps, step, width), jnp.bfloat16),
            pltpu.SemaphoreType.DMA((steps,)),
        ],
        compiler_params=room(60),
        cost_estimate=cost(8),
        name="source_terms",
    )(feat, gain, w_key, w_value)


def list_tiles(need_ref, list_ref):
    def add(t, count):
        used = need_ref[t] > 0

        @pl.when(used)
        def _():
            list_ref[count] = t

        return count + used.astype(jnp.int32)

    return lax.fori_loop(0, list_ref.shape[0], add, jnp.int32(0))


def tile_rows(rows_ref, t):
    both = rows_ref[pl.ds(t // 2, 1), :]
    return jnp.where(t % 2 == 1, both[:, TS:], both[:, :TS])


def gather_kernel(need_ref, rows_ref, table_hbm, *rest):
    out_refs = rest[:-6]
    table_ref, hot, sent, list_ref, sems, table_sem = rest[-6:]
    half = table_ref.shape[1]
    fetch = pltpu.make_async_copy(table_hbm, table_ref, table_sem)
    fetch.start()
    count = list_tiles(need_ref, list_ref)

    def copy(slot, k, h, t):
        return pltpu.make_async_copy(
            sent.at[slot, h, pl.ds(k * TS, TS), :],
            out_refs[h].at[t // 2, pl.ds(pl.multiple_of((t % 2) * TS, TS), TS), :],
            sems.at[slot, k, h],
        )

    def each(step, act):
        for k in range(QUAD):
            place = step * QUAD + k

            @pl.when(jnp.logical_and(place >= 0, place < count))
            def _():
                t = list_ref[jnp.maximum(place, 0)]
                for h in range(len(out_refs)):
                    act(copy(lax.rem(step + 2, 2), k, h, t))

    def quad(step, carry):
        tiles = [list_ref[jnp.minimum(step * QUAD + k, count - 1)] for k in range(QUAD)]
        wanted = jnp.concatenate(
            [jnp.transpose(jnp.broadcast_to(tile_rows(rows_ref, t), (TS, TS))) for t in tiles], axis=0
        )
        upper = wanted >= half
        away = jnp.where(upper, wanted - half, wanted)
        away = away - lax.broadcasted_iota(jnp.int32, (QUAD * TS, TS), 1)
        for c in range(half // TS):
            hot[:, c * TS : (c + 1) * TS] = jnp.where(away == c * TS, 1.0, 0.0).astype(
                jnp.bfloat16
            )
        low = mm(hot[...], table_ref[0])
        high = mm(hot[...], table_ref[1])
        each(step - 2, lambda c: c.wait())
        slot = lax.rem(step, 2)
        for h in range(len(out_refs)):
            here = slice(h * PAIR, (h + 1) * PAIR)
            sent[slot, h] = jnp.where(upper, high[:, here], low[:, here]).astype(jnp.bfloat16)
        each(step, lambda c: c.start())
        return carry

    steps = (count + QUAD - 1) // QUAD
    fetch.wait()
    lax.fori_loop(0, steps, quad, 0)
    each(steps - 2, lambda c: c.wait())
    each(steps - 1, lambda c: c.wait())


def gather_rows(need, rows, pairs):
    count, wide = pairs.shape
    heads = wide // PAIR
    peers = need.shape[0] // 2
    return pl.pallas_call(
        gather_kernel,
        in_specs=[SMEM, VMEM, ANY],
        out_specs=[ANY] * heads,
        out_shape=[jax.ShapeDtypeStruct((peers, 2 * TS, PAIR), jnp.bfloat16)] * heads,
        scratch_shapes=[
            pltpu.VMEM((2, count // 2, wide), jnp.bfloat16),
            pltpu.VMEM((QUAD * TS, count // 2), jnp.bfloat16),
            pltpu.VMEM((2, heads, QUAD * TS, PAIR), jnp.bfloat16),
            pltpu.SMEM((need.shape[0],), jnp.int32),
            pltpu.SemaphoreType.DMA((2, QUAD, heads)),
            pltpu.SemaphoreType.DMA,
        ],
        compiler_params=room(60),
        cost_estimate=cost(10),
        name="gather_rows",
    )(need, rows, pairs.reshape(2, count // 2, wide))


def normed_kernel(feat_ref, gain_ref, normed_ref):
    hat, _ = hat_of(feat_ref[...].astype(jnp.float32))
    normed_ref[...] = (hat * gain_ref[...]).astype(jnp.bfloat16)


def normed_rows(feat, gain):
    rows, width = feat.shape
    step = 512
    return pl.pallas_call(
        normed_kernel,
        grid=(rows // step,),
        in_specs=[
            pl.BlockSpec((step, width), lambda i: (i, 0)),
            pl.BlockSpec((1, width), lambda i: (0, 0)),
        ],
        out_specs=pl.BlockSpec((step, width), lambda i: (i, 0)),
        out_shape=jax.ShapeDtypeStruct((rows, width), jnp.bfloat16),
        compiler_params=room(60),
        cost_estimate=cost(8),
        name="normed_rows",
    )(feat, gain)


def target_kernel(feat_ref, gain_ref, wq_ref, wo_ref, cot_ref, normed_ref, *pairs_refs):
    hat, _ = hat_of(feat_ref[...].astype(jnp.float32))
    normed = (hat * gain_ref[...]).astype(jnp.bfloat16)
    normed_ref[...] = normed
    cot = jnp.concatenate([cot_ref[f] for f in range(cot_ref.shape[0])], axis=1)
    queries = (mm(normed, wq_ref[...]) * 0.125).astype(jnp.bfloat16)
    cots = mm(cot, wo_ref[...], NT).astype(jnp.bfloat16)
    for h, ref in enumerate(pairs_refs):
        here = slice(h * HEAD, (h + 1) * HEAD)
        ref[...] = jnp.concatenate([queries[:, here], cots[:, here]], axis=1)


def target_terms(feat, gain, w_query, w_out, cot):
    rows, width = feat.shape
    groups, _, columns = cot.shape
    heads = columns // HEAD
    step = 512
    return pl.pallas_call(
        target_kernel,
        grid=(rows // step,),
        in_specs=[
            pl.BlockSpec((step, width), lambda i: (i, 0)),
            pl.BlockSpec((1, width), lambda i: (0, 0)),
            pl.BlockSpec(w_query.shape, lambda i: (0, 0)),
            pl.BlockSpec(w_out.shape, lambda i: (0, 0)),
            pl.BlockSpec((groups, step, columns), lambda i: (0, i, 0)),
        ],
        out_specs=[pl.BlockSpec((step, width), lambda i: (i, 0))]
        + [pl.BlockSpec((step, PAIR), lambda i: (i, 0))] * heads,
        out_shape=[jax.ShapeDtypeStruct((rows, width), jnp.bfloat16)]
        + [jax.ShapeDtypeStruct((rows, PAIR), jnp.bfloat16)] * heads,
        compiler_params=room(60),
        cost_estimate=cost(6),
        name="target_terms",
    )(feat, gain, w_query, w_out, cot)


def attention_kernel(
    head,
    tiles_ref,
    own_ref,
    halo_ref,
    pairs_ref,
    valid_ref,
    normed_ref,
    cot_ref,
    own_grad_ref,
    halo_grad_ref,
    weight_grad_ref,
    mixed_ref,
    table,
    bias,
    scores,
    slopes,
    both,
    total,
    sems,
):
    j = pl.program_id(0)
    blocks, tiles = table.shape[0], table.shape[1]
    own_tiles = own_ref.shape[0] // TS

    def fetch(b, k):
        t = tiles_ref[b, k]

        @pl.when(t < own_tiles)
        def _():
            here = pl.ds(pl.multiple_of(t * TS, TS), TS)
            pltpu.make_async_copy(
                own_ref.at[here, pl.ds(head * PAIR, PAIR)], table.at[b, k], sems.at[b, k]
            ).start()

        @pl.when(t >= own_tiles)
        def _():
            o = t - own_tiles
            here = pl.ds(pl.multiple_of((o % 2) * TS, TS), TS)
            pltpu.make_async_copy(
                halo_ref.at[o // 2, here, :], table.at[b, k], sems.at[b, k]
            ).start()

    @pl.when(j == 0)
    def _():
        for b in range(blocks):
            for k in range(tiles):
                fetch(b, k)

        def clear(t, carry):
            total[t] = jnp.zeros(total.shape[1:], jnp.float32)
            return carry

        lax.fori_loop(0, total.shape[0], clear, 0)
        weight_grad_ref[...] = jnp.zeros(weight_grad_ref.shape, jnp.float32)

    for k in range(tiles):
        away = (valid_ref[:, k * TS : (k + 1) * TS] - 1).astype(jnp.float32) * BIG
        bias[k] = jnp.transpose(away)

    for k in range(tiles):
        pltpu.make_async_copy(
            own_ref.at[pl.ds(0, TS), pl.ds(head * PAIR, PAIR)], table.at[j, k], sems.at[j, k]
        ).wait()

    def fold(values, how):
        return how(values.reshape(TS // 8, 8, values.shape[-1]), axis=0)

    keep_first, keep_second = halves()
    pairs = pairs_ref[...]
    queries = pairs * keep_first
    cots = pairs * keep_second
    highest = None
    for k in range(tiles):
        s = mm(table[j, k], queries, NT) + bias[k]
        scores[k] = s
        top = fold(s, jnp.max)
        highest = top if highest is None else jnp.maximum(highest, top)
    highest = jnp.max(highest, axis=0, keepdims=True)
    norm = None
    for k in range(tiles):
        e = jnp.exp(scores[k] - highest)
        scores[k] = e
        part = fold(e, jnp.sum)
        norm = part if norm is None else norm + part
    scale = 1.0 / jnp.sum(norm, axis=0, keepdims=True)
    delta = None
    for k in range(tiles):
        a = scores[k] * scale
        scores[k] = a
        both[k, :, TM:] = a.astype(jnp.bfloat16)
        d = mm(table[j, k], cots, NT)
        slopes[k] = d
        part = fold(a * d, jnp.sum)
        delta = part if delta is None else delta + part
    delta = jnp.sum(delta, axis=0, keepdims=True)
    for k in range(tiles):
        both[k, :, :TM] = (scores[k] * (slopes[k] - delta)).astype(jnp.bfloat16)
    stacked = jnp.concatenate([queries, cots], axis=0)
    for k in range(tiles):
        t = tiles_ref[j, k]
        total[t] = total[t] + mm(both[k], stacked)
    crossed = mm(table[j].reshape(tiles * TS, PAIR), both[...].reshape(tiles * TS, 2 * TM), TN)
    d_query = crossed[:HEAD, :TM]
    attended = crossed[HEAD:, TM:]
    mixed = jnp.concatenate([d_query, attended], axis=0)
    mixed_ref[...] = jnp.transpose(mixed).astype(jnp.bfloat16)
    cot = jnp.concatenate([cot_ref[f] for f in range(cot_ref.shape[0])], axis=1)
    wq_part = mm(d_query.astype(jnp.bfloat16), normed_ref[...])
    wo_part = mm(attended.astype(jnp.bfloat16), cot)
    columns = weight_grad_ref.shape[2]
    for f in range(weight_grad_ref.shape[0]):
        here = slice(f * columns, (f + 1) * columns)
        weight_grad_ref[f, :HEAD] += wq_part[:, here]
        weight_grad_ref[f, HEAD:] += wo_part[:, here]

    @pl.when(j == blocks - 1)
    def _():
        def own(t, carry):
            here = pl.ds(pl.multiple_of(t * TS, TS), TS)
            own_grad_ref[here, :] = total[t].astype(jnp.bfloat16)
            return carry

        lax.fori_loop(0, own_tiles, own, 0)

        def halo(q, carry):
            for half in range(2):
                halo_grad_ref[q, half * TS : (half + 1) * TS, :] = total[
                    own_tiles + 2 * q + half
                ].astype(jnp.bfloat16)
            return carry

        lax.fori_loop(0, halo_grad_ref.shape[0], halo, 0)


def attention(head, tile_src, own, halo, pairs, valid, normed, cot):
    rows, _ = pairs.shape
    blocks, tiles = tile_src.shape
    groups, _, columns = cot.shape
    width = normed.shape[1]
    own_grad = (own.shape[0], PAIR)
    table_tiles = own.shape[0] // TS + 2 * halo.shape[0]
    slots = tiles * TS
    return pl.pallas_call(
        lambda *refs: attention_kernel(head, *refs),
        grid=(blocks,),
        in_specs=[
            SMEM,
            ANY,
            ANY,
            pl.BlockSpec((TM, PAIR), lambda j: (j, 0)),
            pl.BlockSpec((TM, slots), lambda j: (j, 0)),
            pl.BlockSpec((TM, width), lambda j: (j, 0)),
            pl.BlockSpec((groups, TM, columns), lambda j: (0, j, 0)),
        ],
        out_specs=[
            pl.BlockSpec(own_grad, lambda j: (0, 0)),
            pl.BlockSpec(halo.shape, lambda j: (0, 0, 0)),
            pl.BlockSpec((groups, PAIR, columns), lambda j: (0, 0, 0)),
            pl.BlockSpec((TM, PAIR), lambda j: (j, 0)),
        ],
        out_shape=[
            jax.ShapeDtypeStruct(own_grad, jnp.bfloat16),
            jax.ShapeDtypeStruct(halo.shape, jnp.bfloat16),
            jax.ShapeDtypeStruct((groups, PAIR, columns), jnp.float32),
            jax.ShapeDtypeStruct((rows, PAIR), jnp.bfloat16),
        ],
        scratch_shapes=[
            pltpu.VMEM((blocks, tiles, TS, PAIR), jnp.bfloat16),
            pltpu.VMEM((tiles, TS, TM), jnp.float32),
            pltpu.VMEM((tiles, TS, TM), jnp.float32),
            pltpu.VMEM((tiles, TS, TM), jnp.float32),
            pltpu.VMEM((tiles, TS, 2 * TM), jnp.bfloat16),
            pltpu.VMEM((table_tiles, TS, PAIR), jnp.float32),
            pltpu.SemaphoreType.DMA((blocks, tiles)),
        ],
        compiler_params=room(60),
        cost_estimate=cost(18),
        name="attention",
    )(tile_src, own, halo, pairs, valid, normed, cot)


def scatter_kernel(earlier, where_ref, need_ref, own_ref, halo_ref, rows_ref, normed_hbm, *rest):
    *rest, total, normed, grad, list_ref, sem = rest
    done, grad_ref, out_refs = rest[:earlier], rest[earlier], rest[earlier + 1 :]
    table_rows = own_ref.shape[0]
    half = table_rows // 2
    groups = len(out_refs)
    group_rows = table_rows // groups
    chunk = 512
    fetch = pltpu.make_async_copy(normed_hbm, normed, sem)
    fetch.start()
    total[...] = own_ref[...].astype(jnp.float32)
    count = list_tiles(need_ref, list_ref)

    def quad(step, carry):
        spots, parts = [], []
        for k in range(QUAD):
            place = step * QUAD + k
            t = list_ref[jnp.minimum(place, count - 1)]
            spot = jnp.where(place < count, tile_rows(rows_ref, t), -1)
            upper = jnp.transpose(jnp.broadcast_to(spot, (TS, TS))) >= half
            part = halo_ref[t // 2, pl.ds((t % 2) * TS, TS), :]
            keep = jnp.where(upper, 1.0, 0.0).astype(jnp.bfloat16)
            drop = jnp.where(upper, 0.0, 1.0).astype(jnp.bfloat16)
            parts.append(jnp.concatenate([part * drop, part * keep], axis=1))
            spots.append(jnp.where(spot >= half, spot - half, spot))
        spots = jnp.concatenate(spots, axis=1)
        parts = jnp.concatenate(parts, axis=0)
        away = spots - lax.broadcasted_iota(jnp.int32, (chunk, QUAD * TS), 0)
        for c in range(half // chunk):
            hot = jnp.where(away == c * chunk, 1.0, 0.0).astype(jnp.bfloat16)
            added = mm(hot, parts)
            for n in range(2):
                here = slice(n * half + c * chunk, n * half + (c + 1) * chunk)
                total[here, :] = total[here, :] + added[:, n * PAIR : (n + 1) * PAIR]
        return carry

    lax.fori_loop(0, (count + QUAD - 1) // QUAD, quad, 0)
    for s, ref in enumerate(out_refs):
        f = lax.rem(where_ref[0] + s, groups)
        here = pl.ds(pl.multiple_of(f * group_rows, group_rows), group_rows)
        ref[...] = total[here, :].astype(jnp.bfloat16)
    fetch.wait()
    columns = grad.shape[2]
    for n in range(groups):
        here = slice(n * group_rows, (n + 1) * group_rows)
        added = mm(total[here, :].astype(jnp.bfloat16), normed[here, :], TN)
        for f in range(groups):
            part = added[:, f * columns : (f + 1) * columns]
            grad[f] = part if n == 0 else grad[f] + part
    if not earlier:
        grad_ref[...] = grad[...]
        return
    rows = grad_ref.shape[1] // (earlier + 1)
    per_block = grad.shape[1] // rows
    for p in range(grad_ref.shape[0]):
        here = slice(p % per_block * rows, (p % per_block + 1) * rows)
        for m, ref in enumerate(list(done) + [grad]):
            grad_ref[p, m * rows : (m + 1) * rows, :] = ref[p // per_block, here, :]


def scatter_rows(where, need, own, halo, rows, normed, groups, earlier=(), peers=None):
    table_rows = own.shape[0]
    columns = normed.shape[1] // groups
    grad = (groups, PAIR, columns)
    out = grad
    if earlier:
        out = (peers, groups * PAIR // peers * (len(earlier) + 1), columns)
    return pl.pallas_call(
        lambda *refs: scatter_kernel(len(earlier), *refs),
        in_specs=[SMEM, SMEM, VMEM, VMEM, VMEM, ANY] + [VMEM] * len(earlier),
        out_specs=[VMEM] * (1 + groups),
        out_shape=[jax.ShapeDtypeStruct(out, jnp.float32)]
        + [jax.ShapeDtypeStruct((table_rows // groups, PAIR), jnp.bfloat16)] * groups,
        scratch_shapes=[
            pltpu.VMEM((table_rows, PAIR), jnp.float32),
            pltpu.VMEM(normed.shape, jnp.bfloat16),
            pltpu.VMEM(grad, jnp.float32),
            pltpu.SMEM((need.shape[0],), jnp.int32),
            pltpu.SemaphoreType.DMA,
        ],
        compiler_params=room(60),
        cost_estimate=cost(11),
        name="scatter_rows",
    )(where, need, own, halo, rows, normed, *earlier)


def finish_kernel(shares_ref, wq_ref, wk_ref, wv_ref, wo_ref, grads):
    count, total_rows, _ = grads.shape
    heads = count // 2
    rows = shares_ref.shape[1] // count
    for p in range(shares_ref.shape[0]):
        for m in range(count):
            grads[m, p * rows : (p + 1) * rows, :] = shares_ref[p, m * rows : (m + 1) * rows, :]
    for f in range(total_rows // PAIR):
        block = slice(f * PAIR, (f + 1) * PAIR)
        turned = [jnp.transpose(grads[m, block, :]) for m in range(count)]
        for h in range(heads):
            here = slice(h * HEAD, (h + 1) * HEAD)
            wo_ref[here, block] = grads[h, f * PAIR + HEAD : (f + 1) * PAIR, :]
        wq_ref[block, :] = 0.125 * jnp.concatenate([t[:, :HEAD] for t in turned[:heads]], axis=1)
        wk_ref[block, :] = jnp.concatenate([t[:, :HEAD] for t in turned[heads:]], axis=1)
        wv_ref[block, :] = jnp.concatenate([t[:, HEAD:] for t in turned[heads:]], axis=1)


def finish(shares, width, columns):
    tall = jax.ShapeDtypeStruct((width, columns), jnp.float32)
    return pl.pallas_call(
        finish_kernel,
        in_specs=[VMEM],
        out_specs=[VMEM] * 4,
        out_shape=[tall] * 3 + [jax.ShapeDtypeStruct((columns, width), jnp.float32)],
        scratch_shapes=[pltpu.VMEM((2 * columns // HEAD, width, columns), jnp.float32)],
        compiler_params=room(24),
        cost_estimate=cost(2),
        name="finish",
    )(shares)


def grid_kernel(groups, heads, where_ref, weight_ref, feat_ref, gain_ref, *rest):
    parts = rest[: groups * heads]
    out_refs = rest[groups * heads : -1]
    placed = rest[-1]
    me = where_ref[0]
    d_src = None
    for s in range(groups):
        f = lax.rem(me - s + groups, groups)
        for h in range(heads):
            part = mm(parts[s * heads + h][...], weight_ref[f, 0, h])
            d_src = part if d_src is None else d_src + part
    hat, inverse = hat_of(feat_ref[...].astype(jnp.float32))
    result = norm_back(d_src * gain_ref[...], hat, inverse).astype(jnp.bfloat16)
    columns = placed.shape[2]
    for f in range(groups):
        placed[f] = result[:, f * columns : (f + 1) * columns]
    for s, ref in enumerate(out_refs):
        ref[...] = placed[lax.rem(me + s, groups)]


def grid_rows(where, weight, feat, gain, parts):
    groups, heads = len(parts), len(parts[0])
    rows = parts[0][0].shape[0]
    width = feat.shape[1]
    columns = width // groups
    step = 512
    steps = rows // step
    return pl.pallas_call(
        lambda *refs: grid_kernel(groups, heads, *refs),
        grid_spec=pltpu.PrefetchScalarGridSpec(
            num_scalar_prefetch=1,
            grid=(steps,),
            in_specs=[
                pl.BlockSpec((groups, 1, heads, PAIR, width), lambda i, w: (0, 0, 0, 0, 0)),
                pl.BlockSpec((step, width), lambda i, w: (w[0] * steps + i, 0)),
                pl.BlockSpec((1, width), lambda i, w: (0, 0)),
            ]
            + [pl.BlockSpec((step, PAIR), lambda i, w: (i, 0))] * (groups * heads),
            out_specs=[pl.BlockSpec((step, columns), lambda i, w: (i, 0))] * groups,
            scratch_shapes=[pltpu.VMEM((groups, step, columns), jnp.bfloat16)],
        ),
        out_shape=[jax.ShapeDtypeStruct((rows, columns), jnp.bfloat16)] * groups,
        compiler_params=room(60),
        cost_estimate=cost(6),
        name="grid_rows",
    )(where, weight, feat, gain, *[part for row in parts for part in row])


def mesh_kernel(heads, where_ref, weight_ref, feat_ref, cot_ref, gain_ref, *rest):
    parts, (mesh_out_ref, grad_ref, wide) = rest[:heads], rest[heads:]
    groups, columns = weight_ref.shape[0], cot_ref.shape[1]
    mine = pl.ds(pl.multiple_of(where_ref[0] * columns, columns), columns)
    keep_first, keep_second = halves()
    d_dst, added = None, None
    for f in range(groups):
        for h in range(heads):
            part = parts[h][f]
            one = mm(part * keep_first, weight_ref[f, 0, h])
            two = mm(part * keep_second, weight_ref[f, 0, h, :, mine])
            d_dst = one if d_dst is None else d_dst + one
            added = two if added is None else added + two
    feat = feat_ref[...].astype(jnp.float32)
    hat, inverse = hat_of(feat)
    wide[0] = feat
    wide[1] = norm_back(d_dst * 0.125 * gain_ref[...], hat, inverse)
    mesh_out_ref[...] = (wide[0, :, mine] + added).astype(jnp.bfloat16)
    grad_ref[...] = (cot_ref[...].astype(jnp.float32) + wide[1, :, mine]).astype(jnp.bfloat16)


def mesh_rows(where, weight, feat, cot, gain, parts):
    groups, heads = weight.shape[0], len(parts)
    rows, width = feat.shape
    columns = cot.shape[1]
    step = 512
    narrow = pl.BlockSpec((step, columns), lambda i, w: (i, 0))
    return pl.pallas_call(
        lambda *refs: mesh_kernel(heads, *refs),
        grid_spec=pltpu.PrefetchScalarGridSpec(
            num_scalar_prefetch=1,
            grid=(rows // step,),
            in_specs=[
                pl.BlockSpec((groups, 1, heads, PAIR, width), lambda i, w: (0, 1, 0, 0, 0)),
                pl.BlockSpec((step, width), lambda i, w: (i, 0)),
                narrow,
                pl.BlockSpec((1, width), lambda i, w: (0, 0)),
            ]
            + [pl.BlockSpec((groups, step, PAIR), lambda i, w: (0, i, 0))] * heads,
            out_specs=[narrow] * 2,
            scratch_shapes=[pltpu.VMEM((2, step, width), jnp.float32)],
        ),
        out_shape=[jax.ShapeDtypeStruct((rows, columns), jnp.bfloat16)] * 2,
        compiler_params=room(60),
        cost_estimate=cost(11),
        name="mesh_rows",
    )(where, weight, feat, cot, gain, *parts)


def place_kernel(groups, where_ref, *rest):
    parts, out_ref = rest[:groups], rest[groups]
    rows = parts[0].shape[0]
    for s in range(groups):
        f = lax.rem(where_ref[0] - s + groups, groups)
        here = pl.ds(pl.multiple_of(f * rows, rows), rows)
        out_ref[here, :] = parts[s][...]


def place_rows(where, parts):
    groups = len(parts)
    rows, columns = parts[0].shape
    return pl.pallas_call(
        lambda *refs: place_kernel(groups, *refs),
        in_specs=[SMEM] + [VMEM] * groups,
        out_specs=VMEM,
        out_shape=jax.ShapeDtypeStruct((groups * rows, columns), jnp.bfloat16),
        compiler_params=room(24),
        cost_estimate=cost(2),
        name="place_rows",
    )(where, *parts)


def over_graph(values):
    return lax.all_to_all(values, "graph", split_axis=0, concat_axis=0, tiled=True)


def over_feat(parts):
    groups = len(parts)
    return [parts[0]] + [
        lax.ppermute(parts[s], "feat", [(i, (i + s) % groups) for i in range(groups)])
        for s in range(1, groups)
    ]


def after(values, earlier):
    return lax.optimization_barrier((values, earlier))


def corner(values):
    return values[:1, :16, :]


def by_head(first, second):
    heads = first.shape[0] // HEAD
    parts = [x.reshape(heads, HEAD, -1) for x in (first, second)]
    return jnp.concatenate(parts, axis=1)


def body(
    grid_feat,
    mesh_feat,
    send_rows,
    tile_src,
    edge_mask,
    gain_src,
    gain_dst,
    w_query,
    w_key,
    w_value,
    w_out,
    d_out,
):
    grid_count, width = grid_feat.shape
    columns = w_query.shape[1]
    heads = columns // HEAD
    groups = width // columns
    peers = send_rows.shape[1]
    own_tiles = grid_count // TS
    where = lax.axis_index("feat").astype(jnp.int32).reshape(1)
    gain_src = gain_src.reshape(1, width)
    gain_dst = gain_dst.reshape(1, width)
    rows = send_rows.reshape(peers, 2 * TS)

    wanted = own_tiles + jnp.arange(2 * peers, dtype=jnp.int32)
    need = jnp.any(tile_src.reshape(-1, 1) == wanted[None, :], axis=0).astype(jnp.int32)
    need = over_graph(jnp.broadcast_to(need.reshape(peers, 2, 1), (peers, 2, TS)))
    need = need[:, :, 0].reshape(-1)

    cot = lax.all_gather(d_out, "feat", axis=0)
    back_weights = jnp.stack([by_head(w_key.T, w_value.T), by_head(w_query.T, w_out)])
    back_weights = lax.all_gather(back_weights, "feat", axis=0)

    pairs = source_terms(grid_feat, gain_src, w_key, w_value)
    outgoing = gather_rows(need, rows, pairs)
    normed_src = normed_rows(grid_feat, gain_src)
    normed_dst, *targets = target_terms(mesh_feat, gain_dst, w_query, w_out, cot)

    halo = []
    for h in range(heads):
        sent = outgoing[h]
        if h > 0:
            sent, (_, normed_src) = after(sent, (corner(halo[h - 1]), normed_src))
        halo.append(over_graph(sent))

    own_grads, returned, mixed, weight_grads = [], [], [], []
    for h in range(heads):
        own_grad, halo_grad, weight_grad, mixed_columns = attention(
            h, tile_src, pairs, halo[h], targets[h], edge_mask, normed_dst, cot
        )
        own_grads.append(own_grad)
        weight_grads.append(weight_grad)
        mixed.append(lax.all_gather(mixed_columns, "feat", axis=0))
        if h == 0:
            halo_grad, (halo[heads - 1], back_weights) = after(
                halo_grad, (halo[heads - 1], back_weights)
            )
        else:
            halo_grad, (_, mixed[h - 1]) = after(
                halo_grad, (corner(returned[h - 1]), mixed[h - 1])
            )
        returned.append(over_graph(halo_grad))

    sums = []
    for h in range(heads):
        last = h == heads - 1
        if last:
            returned[h], (sums, weight_grads, mixed) = after(
                returned[h], (sums, weight_grads, mixed)
            )
        weight_grad, *blocks = scatter_rows(
            where,
            need,
            own_grads[h],
            returned[h],
            rows,
            normed_src,
            groups,
            weight_grads if last else (),
            peers,
        )
        weight_grads.append(weight_grad)
        sums.append(over_feat(blocks))

    mixed, payload = after(mixed, weight_grads[-1])
    mesh_out, grad_mesh = mesh_rows(where, back_weights, mesh_feat, d_out, gain_dst, mixed)
    sum_rows = [[sums[h][s] for h in range(heads)] for s in range(groups)]
    grid_parts = grid_rows(where, back_weights, grid_feat, gain_src, sum_rows)
    share = jnp.sum(over_graph(payload), axis=0)
    share, (grid_parts, mesh_out, grad_mesh) = after(share, (grid_parts, mesh_out, grad_mesh))
    shares = over_graph(jnp.broadcast_to(share[None], payload.shape))
    grad_grid = place_rows(where, over_feat(grid_parts))
    grad_wq, grad_wk, grad_wv, grad_wo = finish(shares, width, columns)
    return (mesh_out, grad_grid, grad_mesh, grad_wq, grad_wk, grad_wv, grad_wo)


def solution(mesh):
    in_specs = (
        P("graph", None),
        P("graph", None),
        P("graph", None, None),
        P("graph", None),
        P("graph", None),
        P(),
        P(),
        P(None, "feat"),
        P(None, "feat"),
        P(None, "feat"),
        P("feat", None),
        P("graph", "feat"),
    )
    out_specs = (
        P("graph", "feat"),
        P("graph", "feat"),
        P("graph", "feat"),
        P(None, "feat"),
        P(None, "feat"),
        P(None, "feat"),
        P("feat", None),
    )
    return jax.shard_map(body, mesh=mesh, in_specs=in_specs, out_specs=out_specs, check_vma=False)
```
